512 devices in a mesh: freq: 8 (over y, core), pair: 64 (over z, x).
Axes of the slice: x: 4, y: 4, z: 16, core: 2. Of those that a mesh axis runs over, the one named last changes fastest.
Arguments:
- vertex: bfloat16 [1920, 128, 128], P('pair', 'freq'), may hold values from -1.5 to 1.5
- deriv_s: bfloat16 [1920, 128, 128], P('pair', None, 'freq'), may hold values from -1.1953125 to 1.1953125
- deriv_u: bfloat16 [1920, 128, 128], P('pair', None, 'freq'), may hold values from -1.1953125 to 1.1953125
- freq_map_s: int32 [128], replicated, may hold values from 0 to 127, each once
- freq_map_u: int32 [128], replicated, may hold values from 0 to 127, each once
- pair_sym: int32 [1920], P('pair'), may hold values from 0 to 1919, as said below
- propagator: float32 [128], replicated, may hold values from 0.1 to 1
- left_pairs: int32 [1920, 56], P('pair'), may hold values from 0 to 1919, as said below
- right_pairs: int32 [1920, 56], P('pair'), may hold values from 0 to 1919, as said below
- lengths: int32 [1920], P('pair'), may hold values from 1 to 56
Outputs:
- correction: float32 [1920, 128, 128], P('pair', 'freq')
The draws below stay inside these ranges and needn't reach their ends.
Inputs may be any that keep to these rules, and one draw needn't show every extreme that they name: pair_sym is a permutation of each aligned block of 30 pairs onto itself. For pair r in block b = r // 30, left_pairs[r, k] lies in blocks b - 1, b or b + 1 of 30 pairs. For pair r in block b = r // 30, right_pairs[r, k] lies in blocks b - 1, b or b + 1 of 30 pairs, and the 56 entries of one row are distinct.
All inputs are finite; a program needn't handle non-finite values.
Results may differ from the reference program's by a relative error of at most 0.0042.
Values may be sent and summed in bfloat16 or wider, within the bound.
A program may use at most 64 MiB of HBM per device.

```python
import math
import jax
import jax.numpy as jnp
from jax import lax

NF = 128
PAIR_DEV = 30
K_MAX = 56
PAIRS = 1920


def draw_pair_sym(key, part):
    key = jax.random.fold_in(key, 11)
    blocks = PAIRS // PAIR_DEV
    subkeys = jax.random.split(key, blocks)
    shuffles = jax.vmap(lambda sub: jax.random.permutation(sub, PAIR_DEV))(subkeys).astype(jnp.int32)
    offset_rows = jnp.arange(blocks, dtype=jnp.int32)[:, None] * PAIR_DEV
    return (shuffles + offset_rows).reshape(PAIRS).astype(jnp.int32)


def draw_right_pairs(key, part):
    key = jax.random.fold_in(key, 12)
    window_size = 3 * PAIR_DEV
    subkeys = jax.random.split(key, PAIRS)
    rankings = jax.vmap(lambda sub: jax.random.permutation(sub, window_size))(subkeys).astype(jnp.int32)
    owners = jnp.arange(PAIRS, dtype=jnp.int32) // PAIR_DEV
    window_start = (owners - 1) * PAIR_DEV
    candidates = window_start[:, None] + jnp.arange(window_size, dtype=jnp.int32)[None, :]
    inside = (candidates >= 0) & (candidates < PAIRS)
    scores = rankings + jnp.where(inside, 0, window_size).astype(jnp.int32)
    ordering = jnp.argsort(scores, axis=1)
    picked = jnp.take_along_axis(candidates, ordering[:, :K_MAX], axis=1)
    return picked.astype(jnp.int32)


def draw_left_pairs(key, part):
    key = jax.random.fold_in(key, 13)
    owners = jnp.arange(PAIRS, dtype=jnp.int32) // PAIR_DEV
    window_start = (owners - 1) * PAIR_DEV
    lowest = jnp.maximum(window_start, 0)
    highest = jnp.minimum(window_start + 3 * PAIR_DEV, PAIRS)
    drawn = jax.random.randint(key, (PAIRS, K_MAX), lowest[:, None], highest[:, None])
    return drawn.astype(jnp.int32)


def draw_lengths(key, part):
    key = jax.random.fold_in(key, 14)
    key_top, key_len = jax.random.split(key)
    blocks = PAIRS // PAIR_DEV
    ceilings = jax.random.randint(key_top, (blocks,), K_MAX // 2, K_MAX + 1)
    ceiling_row = ceilings[jnp.arange(PAIRS) // PAIR_DEV]
    drawn = jax.random.randint(key_len, (PAIRS,), 1, ceiling_row + 1)
    drawn = drawn.at[0].set(K_MAX)
    return drawn.astype(jnp.int32)


def steps_of(stream_key, dims, cuts, low, largest):
    factor_of, own = 1.0, jax.random.fold_in(stream_key, 6)
    for position, parts in cuts:
        steps = jnp.exp(jax.random.uniform(jax.random.fold_in(own, position), (parts,), jnp.float32, low / len(cuts), largest / len(cuts)))
        factor_of = factor_of * jnp.repeat(steps, dims[position] // parts).reshape([-1 if axis == position else 1 for axis in range(len(dims))])
    return factor_of


def bell_draw(key, shape, spread, most, cuts=(), kind=jnp.bfloat16):
    values = jax.random.normal(key, shape, jnp.float32) * spread
    if len(cuts) > 0:
        values = steps_of(key, shape, cuts, -0.22, 0.18) * values
    return jnp.clip(values, min=-most, max=most).astype(kind)


def setup_inputs(seed: int = 0) -> dict:
    key_list = jax.random.split(jax.random.key(seed), 11)
    vertex = bell_draw(key_list[0], (PAIRS, NF, NF), 0.25, 1.5, ((0, 64), (1, 8)))
    deriv_s = bell_draw(key_list[1], (PAIRS, NF, NF), 0.2, 1.1953125, ((0, 64), (2, 8)))
    deriv_u = bell_draw(key_list[2], (PAIRS, NF, NF), 0.2, 1.1953125, ((0, 64), (2, 8)))
    freq_map_s = jax.random.permutation(key_list[3], NF).astype(jnp.int32)
    freq_map_u = jax.random.permutation(key_list[4], NF).astype(jnp.int32)
    pair_sym = draw_pair_sym(jax.random.fold_in(key_list[10], 71), 0)
    propagator = jnp.clip(jnp.exp(jax.random.uniform(key_list[6], (NF,), jnp.float32, math.log(0.1), math.log(1.0))), 0.1, 1.0)
    left_pairs = draw_left_pairs(jax.random.fold_in(key_list[10], 71), 0)
    right_pairs = draw_right_pairs(jax.random.fold_in(key_list[10], 71), 0)
    lengths = draw_lengths(jax.random.fold_in(key_list[10], 71), 0)
    return dict(vertex=vertex, deriv_s=deriv_s, deriv_u=deriv_u, freq_map_s=freq_map_s, freq_map_u=freq_map_u, pair_sym=pair_sym, propagator=propagator, left_pairs=left_pairs, right_pairs=right_pairs, lengths=lengths)


def reference(vertex, deriv_s, deriv_u, freq_map_s, freq_map_u, pair_sym, propagator, left_pairs, right_pairs, lengths):
    part_s = jnp.take(deriv_s, freq_map_s, axis=2).astype(jnp.float32)
    part_u = jnp.take(jnp.take(deriv_u, pair_sym, axis=0), freq_map_u, axis=2).astype(jnp.float32)
    deriv_t = (part_s + part_u).astype(jnp.bfloat16)
    left_vertex = (vertex.astype(jnp.float32) * propagator).astype(jnp.bfloat16)
    left_deriv = (deriv_t.astype(jnp.float32) * propagator).astype(jnp.bfloat16)
    weights = (jnp.arange(K_MAX)[None, :] < lengths[:, None]).astype(jnp.float32)

    def one_block(pieces):
        left_idx, right_idx, slot_weight = pieces
        left_one = jnp.take(left_vertex, left_idx, axis=0).astype(jnp.float32) * slot_weight[:, :, None, None]
        left_two = jnp.take(left_deriv, left_idx, axis=0).astype(jnp.float32) * slot_weight[:, :, None, None]
        right_one = jnp.take(deriv_t, right_idx, axis=0).astype(jnp.float32)
        right_two = jnp.take(vertex, right_idx, axis=0).astype(jnp.float32)
        summed = jnp.einsum('pkij,pkjl->pil', left_one, right_one)
        return summed + jnp.einsum('pkij,pkjl->pil', left_two, right_two)

    blocks = PAIRS // PAIR_DEV
    result = lax.map(one_block, (left_pairs.reshape(blocks, PAIR_DEV, K_MAX), right_pairs.reshape(blocks, PAIR_DEV, K_MAX), weights.reshape(blocks, PAIR_DEV, K_MAX)))
    return result.reshape(PAIRS, NF, NF)
```

```python
import functools

import jax
import jax.numpy as jnp
from jax import lax
from jax.experimental import pallas as pl
from jax.experimental.pallas import tpu as pltpu
from jax.sharding import PartitionSpec as P

MESH = pl.DeviceIdType.MESH
BF16 = jnp.bfloat16
F32 = jnp.float32

OWN, BEFORE, AFTER = 0, 1, 2
VERTEX, DERIV = 0, 1


def kernel(
    dims,
    v_ref,
    s_ref,
    u_ref,
    map_s_ref,
    map_u_ref,
    prop_ref,
    left_ref,
    right_ref,
    sym_ref,
    len_ref,
    out_ref,
    window,
    left_vertex,
    left_deriv,
    chunks,
    columns,
    table,
    sel_vec,
    sel,
    recv,
    recv_cols,
    send,
    local,
):
    n_freq, n_pair = dims
    pairs, rows, nf = v_ref.shape
    slots = left_ref.shape[1]
    freq, block = lax.axis_index("freq"), lax.axis_index("pair")

    sibling = (freq + 1 - 2 * (freq % 2), block)
    y_up = ((freq + 2) % n_freq, block)
    y_down = ((freq + n_freq - 2) % n_freq, block)
    x_up = (freq, (block + 1) % n_pair)
    x_down = (freq, (block + n_pair - 1) % n_pair)

    barrier = pltpu.get_barrier_semaphore()
    peers = [((freq + o) % n_freq, block) for o in range(1, n_freq)] + [x_up, x_down]
    for peer in peers:
        pl.semaphore_signal(barrier, inc=1, device_id=peer, device_id_type=MESH)
    pl.semaphore_wait(barrier, len(peers))

    sent = []

    def copy_to(src, dst, recv_sem, peer):
        copy = pltpu.make_async_remote_copy(
            src_ref=src,
            dst_ref=dst,
            send_sem=send.at[len(sent)],
            recv_sem=recv_sem,
            device_id=peer,
            device_id_type=MESH,
        )
        copy.start()
        sent.append(copy)

    def push(b, kind, f, peer, as_block=None):
        to = b if as_block is None else as_block
        copy_to(window.at[b, kind, f], window.at[to, kind, f], recv.at[to, kind, f], peer)

    def push_x(kind, f, upward=(True, False)):
        for up in upward:
            if up:
                push(OWN, kind, f, x_up, BEFORE)
            else:
                push(OWN, kind, f, x_down, AFTER)

    def arrive(b, kind, f):
        ref = window.at[b, kind, f]
        pltpu.make_async_remote_copy(
            src_ref=ref,
            dst_ref=ref,
            send_sem=send.at[0],
            recv_sem=recv.at[b, kind, f],
            device_id=sibling,
            device_id_type=MESH,
        ).wait_recv()

    f_up, f_down, f_far = (freq + 2) % n_freq, (freq + 6) % n_freq, (freq + 4) % n_freq

    window[OWN, VERTEX, freq] = v_ref[...]
    push_x(VERTEX, freq)
    push(OWN, VERTEX, freq, sibling)

    group = nf // rows
    n_groups = columns.shape[2]
    lane = lax.broadcasted_iota(jnp.int32, (rows, nf), 1)
    first_pair = block * pairs
    for kind, src in ((0, s_ref), (1, u_ref)):
        for g in range(n_groups):
            parts = []
            for q in range(group):
                p = g * group + q
                if p >= pairs:
                    parts.append(jnp.zeros((rows, nf), F32))
                elif kind == 0:
                    parts.append(src[p].astype(F32))
                else:
                    parts.append(src[lax.rem(sym_ref[p], pairs)].astype(F32))
            step = 1
            while step < group:
                high = (lane // (rows * step)) % 2 == 1
                for q in range(group):
                    if (q // step) % 2 == 0:
                        a, b = parts[q], parts[q + step]
                        parts[q] = jnp.where(high, pltpu.roll(b, rows * step, 1), a)
                        parts[q + step] = jnp.where(high, b, pltpu.roll(a, nf - rows * step, 1))
                step *= 2
            for f in range(n_freq):
                chunks[f, kind, g] = parts[f].astype(BF16)
    columns[freq] = chunks[freq]
    for o in (4, 3, 5, 2, 6, 1, 7):
        f = (freq + o) % n_freq
        copy_to(chunks.at[f], columns.at[freq], recv_cols.at[freq], (f, block))
    push(OWN, VERTEX, freq, y_up)
    push(OWN, VERTEX, freq, y_down)

    wide = lax.broadcasted_iota(jnp.int32, (nf, nf), 0)
    table[0:nf, :] = jnp.where(wide == map_s_ref[...], 1.0, 0.0).astype(BF16)
    table[nf : 2 * nf, :] = jnp.where(wide == map_u_ref[...], 1.0, 0.0).astype(BF16)
    window_first = first_pair - pairs
    row_id = lax.broadcasted_iota(jnp.int32, (pairs, slots), 0)
    slot_id = lax.broadcasted_iota(jnp.int32, (pairs, slots), 1)
    count = jnp.zeros((pairs, slots), jnp.int32)
    for r in range(pairs):
        count = jnp.where(row_id == r, len_ref[r], count)
    target = jnp.where(slot_id < count, right_ref[...] - window_first, -1)
    source = left_ref[...] - (window_first - 1)
    lanes = lax.broadcasted_iota(jnp.int32, (pairs, nf), 1)
    chosen = jnp.zeros((pairs, nf), jnp.int32)
    for k in range(slots):
        chosen = jnp.where(target[:, k : k + 1] == lanes, source[:, k : k + 1], chosen)
    sel_vec[...] = chosen
    to_scalar = pltpu.make_async_copy(sel_vec, sel, local.at[0])
    to_scalar.start()

    prop = prop_ref[...]
    place = {BEFORE: 1, OWN: 1 + pairs, AFTER: 1 + 2 * pairs}

    def fill_left(left, b, kind):
        rows_of = window[b, kind, freq].astype(F32) * prop
        left[place[b] : place[b] + pairs] = rows_of.astype(BF16)

    left_vertex[0] = jnp.zeros((rows, nf), BF16)
    left_deriv[0] = jnp.zeros((rows, nf), BF16)
    fill_left(left_vertex, OWN, VERTEX)

    for o in range(1, n_freq):
        f = (freq + o) % n_freq
        pltpu.make_async_remote_copy(
            src_ref=chunks.at[f],
            dst_ref=columns.at[f],
            send_sem=send.at[0],
            recv_sem=recv_cols.at[f],
            device_id=(f, block),
            device_id_type=MESH,
        ).wait_recv()
    for g in range(n_groups):
        cols = jnp.concatenate(
            [columns[:, kind, g].reshape(nf, nf) for kind in (0, 1)], axis=0
        )
        rows_t = lax.dot_general(
            cols, table[...], (((0,), (0,)), ((), ())), preferred_element_type=F32
        ).astype(BF16)
        n = min(group, pairs - g * group)
        window[OWN, DERIV, freq, g * group : g * group + n] = rows_t.reshape(group, rows, nf)[:n]
    push_x(DERIV, freq)
    push(OWN, DERIV, freq, y_up)
    push(OWN, DERIV, freq, y_down)
    push(OWN, DERIV, freq, sibling)
    fill_left(left_deriv, OWN, DERIV)

    arrive(OWN, VERTEX, f_down)
    push(OWN, VERTEX, f_down, y_up)
    push(OWN, VERTEX, f_down, sibling)
    arrive(OWN, VERTEX, f_up)
    push(OWN, VERTEX, f_up, sibling)

    for b in (BEFORE, AFTER):
        arrive(b, VERTEX, freq)
        push(b, VERTEX, freq, y_up)
        push(b, VERTEX, freq, y_down)
        push(b, VERTEX, freq, sibling)
        fill_left(left_vertex, b, VERTEX)
    arrive(OWN, VERTEX, f_far)
    push(OWN, VERTEX, f_far, sibling)

    arrive(OWN, DERIV, f_up)
    push(OWN, DERIV, f_up, y_down)
    push_x(DERIV, f_up)
    push(OWN, DERIV, f_up, sibling)
    arrive(OWN, DERIV, f_down)
    push_x(DERIV, f_down)
    push(OWN, DERIV, f_down, sibling)
    for b in (BEFORE, AFTER):
        arrive(b, DERIV, freq)
        push(b, DERIV, freq, sibling)
        fill_left(left_deriv, b, DERIV)
    arrive(OWN, DERIV, f_far)
    push_x(DERIV, f_far)
    push(OWN, DERIV, f_far, sibling)

    def from_sibling(b, kind):
        for f in (0, 2, 4, 6):
            arrive(b, kind, (sibling[0] + f) % n_freq)

    to_scalar.wait()

    def add_terms(b, kind, left):
        offset = place[b] - 1

        def two_pairs(t, carry):
            halves, weights = [], []
            for j in (0, 1):
                p = 2 * t + j
                halves.append(
                    jnp.concatenate([left[sel[r, offset + p]] for r in range(pairs)], axis=0)
                )
                weights.append(window[b, kind, :, p].reshape(nf, nf))
            terms = jnp.dot(
                jnp.concatenate(halves, axis=1),
                jnp.concatenate(weights, axis=0),
                preferred_element_type=F32,
            )
            out_ref[...] += terms.reshape(pairs, rows, nf)
            return carry

        lax.fori_loop(0, pairs // 2, two_pairs, 0)

    out_ref[...] = jnp.zeros_like(out_ref)

    arrive(BEFORE, VERTEX, f_down)
    push(BEFORE, VERTEX, f_down, y_up)
    push(BEFORE, VERTEX, f_down, sibling)
    arrive(AFTER, VERTEX, f_up)
    push(AFTER, VERTEX, f_up, y_down)
    push(AFTER, VERTEX, f_up, sibling)
    from_sibling(OWN, VERTEX)
    add_terms(OWN, VERTEX, left_deriv)
    arrive(BEFORE, VERTEX, f_up)
    push(BEFORE, VERTEX, f_up, sibling)
    arrive(AFTER, VERTEX, f_down)
    push(AFTER, VERTEX, f_down, sibling)
    from_sibling(OWN, DERIV)
    add_terms(OWN, DERIV, left_vertex)
    for b in (BEFORE, AFTER):
        for f in (f_up, f_down):
            arrive(b, DERIV, f)
            push(b, DERIV, f, sibling)
    for b in (BEFORE, AFTER):
        arrive(b, VERTEX, f_far)
        push(b, VERTEX, f_far, sibling)
    for b in (BEFORE, AFTER):
        from_sibling(b, VERTEX)
        add_terms(b, VERTEX, left_deriv)
    for b in (BEFORE, AFTER):
        arrive(b, DERIV, f_far)
        push(b, DERIV, f_far, sibling)
    for b in (BEFORE, AFTER):
        from_sibling(b, DERIV)
        add_terms(b, DERIV, left_vertex)

    for copy in sent:
        copy.wait_send()


def per_device(
    dims,
    vertex,
    deriv_s,
    deriv_u,
    freq_map_s,
    freq_map_u,
    pair_sym,
    propagator,
    left_pairs,
    right_pairs,
    lengths,
):
    n_freq, _ = dims
    pairs, rows, nf = vertex.shape
    n_groups = -(-pairs * rows // nf)
    vmem = pl.BlockSpec(memory_space=pltpu.VMEM)
    smem = pl.BlockSpec(memory_space=pltpu.SMEM)
    return pl.pallas_call(
        functools.partial(kernel, dims),
        out_shape=jax.ShapeDtypeStruct((pairs, rows, nf), F32),
        in_specs=[vmem] * 8 + [smem] * 2,
        out_specs=vmem,
        scratch_shapes=[
            pltpu.VMEM((3, 2, n_freq, pairs, rows, nf), BF16),
            pltpu.VMEM((1 + 3 * pairs, rows, nf), BF16),
            pltpu.VMEM((1 + 3 * pairs, rows, nf), BF16),
            pltpu.VMEM((n_freq, 2, n_groups, rows, nf), BF16),
            pltpu.VMEM((n_freq, 2, n_groups, rows, nf), BF16),
            pltpu.VMEM((2 * nf, nf), BF16),
            pltpu.VMEM((pairs, nf), jnp.int32),
            pltpu.SMEM((pairs, nf), jnp.int32),
            pltpu.SemaphoreType.DMA((3, 2, n_freq)),
            pltpu.SemaphoreType.DMA((n_freq,)),
            pltpu.SemaphoreType.DMA((64,)),
            pltpu.SemaphoreType.DMA((1,)),
        ],
        compiler_params=pltpu.CompilerParams(
            collective_id=0, has_side_effects=True, vmem_limit_bytes=40 * 1024 * 1024
        ),
    )(
        vertex,
        jnp.swapaxes(deriv_s, 1, 2),
        jnp.swapaxes(deriv_u, 1, 2),
        freq_map_s.reshape(1, nf),
        freq_map_u.reshape(1, nf),
        propagator.reshape(1, nf),
        left_pairs,
        right_pairs,
        pair_sym,
        lengths,
    )


def solution(mesh):
    dims = (mesh.shape["freq"], mesh.shape["pair"])
    return jax.shard_map(
        functools.partial(per_device, dims),
        mesh=mesh,
        in_specs=(
            P("pair", "freq", None),
            P("pair", None, "freq"),
            P("pair", None, "freq"),
            P(),
            P(),
            P("pair"),
            P(),
            P("pair", None),
            P("pair", None),
            P("pair"),
        ),
        out_specs=P("pair", "freq", None),
        check_vma=False,
    )
```

```python
import functools

import jax
import jax.numpy as jnp
from jax import lax
from jax.experimental import pallas as pl
from jax.experimental.pallas import tpu as pltpu
from jax.sharding import PartitionSpec as P

MESH = pl.DeviceIdType.MESH
BF16 = jnp.bfloat16
F32 = jnp.float32

OWN, BEFORE, AFTER = 0, 1, 2
VERTEX, DERIV = 0, 1

STEP = 10


def kernel(
    dims,
    v_in,
    s_in,
    u_in,
    map_s_in,
    map_u_in,
    prop_in,
    left_in,
    right_in,
    sym_ref,
    len_ref,
    out_ref,
    s_ref,
    u_ref,
    map_s_ref,
    map_u_ref,
    prop_ref,
    left_ref,
    right_ref,
    window,
    left_vertex,
    left_deriv,
    chunks,
    columns,
    table,
    sel_vec,
    sel,
    recv,
    recv_cols,
    send,
    local,
):
    n_freq, n_pair = dims
    pairs, rows, nf = v_in.shape
    slots = left_ref.shape[1]
    freq, block = lax.axis_index("freq"), lax.axis_index("pair")

    loads = [
        pltpu.make_async_copy(src, dst, local.at[i])
        for i, (src, dst) in enumerate(
            (
                (v_in, window.at[OWN, VERTEX, freq]),
                (s_in, s_ref),
                (u_in, u_ref),
                (map_s_in, map_s_ref),
                (map_u_in, map_u_ref),
                (prop_in, prop_ref),
                (left_in, left_ref),
                (right_in, right_ref),
            )
        )
    ]
    for load in loads:
        load.start()

    sibling = (freq + 1 - 2 * (freq % 2), block)
    y_up = ((freq + 2) % n_freq, block)
    y_down = ((freq + n_freq - 2) % n_freq, block)
    x_up = (freq, (block + 1) % n_pair)
    x_down = (freq, (block + n_pair - 1) % n_pair)

    barrier = pltpu.get_barrier_semaphore()
    peers = [((freq + o) % n_freq, block) for o in range(1, n_freq)] + [x_up, x_down]
    for peer in peers:
        pl.semaphore_signal(barrier, inc=1, device_id=peer, device_id_type=MESH)
    pl.semaphore_wait(barrier, len(peers))

    sent = []

    def copy_to(src, dst, recv_sem, peer):
        copy = pltpu.make_async_remote_copy(
            src_ref=src,
            dst_ref=dst,
            send_sem=send.at[len(sent)],
            recv_sem=recv_sem,
            device_id=peer,
            device_id_type=MESH,
        )
        copy.start()
        sent.append(copy)

    def push(b, kind, f, peer, as_block=None):
        to = b if as_block is None else as_block
        copy_to(window.at[b, kind, f], window.at[to, kind, f], recv.at[to, kind, f], peer)

    def push_x(kind, f, upward=(True, False)):
        for up in upward:
            if up:
                push(OWN, kind, f, x_up, BEFORE)
            else:
                push(OWN, kind, f, x_down, AFTER)

    def arrive(b, kind, f):
        ref = window.at[b, kind, f]
        pltpu.make_async_remote_copy(
            src_ref=ref,
            dst_ref=ref,
            send_sem=send.at[0],
            recv_sem=recv.at[b, kind, f],
            device_id=sibling,
            device_id_type=MESH,
        ).wait_recv()

    f_up, f_down, f_far = (freq + 2) % n_freq, (freq + 6) % n_freq, (freq + 4) % n_freq

    for load in loads:
        load.wait()
    push_x(VERTEX, freq)
    push(OWN, VERTEX, freq, sibling)

    group = nf // rows
    n_groups = columns.shape[2]
    lane = lax.broadcasted_iota(jnp.int32, (rows, nf), 1)
    first_pair = block * pairs
    for kind, src in ((0, s_ref), (1, u_ref)):
        for g in range(n_groups):
            parts = []
            for q in range(group):
                p = g * group + q
                if p >= pairs:
                    parts.append(jnp.zeros((rows, nf), F32))
                elif kind == 0:
                    parts.append(src[p].astype(F32))
                else:
                    parts.append(src[lax.rem(sym_ref[p], pairs)].astype(F32))
            step = 1
            while step < group:
                high = (lane // (rows * step)) % 2 == 1
                for q in range(group):
                    if (q // step) % 2 == 0:
                        a, b = parts[q], parts[q + step]
                        parts[q] = jnp.where(high, pltpu.roll(b, rows * step, 1), a)
                        parts[q + step] = jnp.where(high, b, pltpu.roll(a, nf - rows * step, 1))
                step *= 2
            for f in range(n_freq):
                chunks[f, kind, g] = parts[f].astype(BF16)
    columns[freq] = chunks[freq]
    for o in (4, 3, 5, 2, 6, 1, 7):
        f = (freq + o) % n_freq
        copy_to(chunks.at[f], columns.at[freq], recv_cols.at[freq], (f, block))
    push(OWN, VERTEX, freq, y_up)
    push(OWN, VERTEX, freq, y_down)

    wide = lax.broadcasted_iota(jnp.int32, (nf, nf), 0)
    table[0:nf, :] = jnp.where(wide == map_s_ref[...], 1.0, 0.0).astype(BF16)
    table[nf : 2 * nf, :] = jnp.where(wide == map_u_ref[...], 1.0, 0.0).astype(BF16)
    window_first = first_pair - pairs
    row_id = lax.broadcasted_iota(jnp.int32, (pairs, slots), 0)
    slot_id = lax.broadcasted_iota(jnp.int32, (pairs, slots), 1)
    count = jnp.zeros((pairs, slots), jnp.int32)
    for r in range(pairs):
        count = jnp.where(row_id == r, len_ref[r], count)
    target = jnp.where(slot_id < count, right_ref[...] - window_first, -1)
    source = left_ref[...] - (window_first - 1)
    lanes = lax.broadcasted_iota(jnp.int32, (pairs, nf), 1)
    chosen = jnp.zeros((pairs, nf), jnp.int32)
    for k in range(slots):
        chosen = jnp.where(target[:, k : k + 1] == lanes, source[:, k : k + 1], chosen)
    sel_vec[...] = chosen
    to_scalar = pltpu.make_async_copy(sel_vec, sel, local.at[8])
    to_scalar.start()

    prop = prop_ref[...]
    place = {BEFORE: 1, OWN: 1 + pairs, AFTER: 1 + 2 * pairs}

    def fill_left(left, b, kind):
        rows_of = window[b, kind, freq].astype(F32) * prop
        left[place[b] : place[b] + pairs] = rows_of.astype(BF16)

    left_vertex[0] = jnp.zeros((rows, nf), BF16)
    left_deriv[0] = jnp.zeros((rows, nf), BF16)
    fill_left(left_vertex, OWN, VERTEX)

    for o in range(1, n_freq):
        f = (freq + o) % n_freq
        pltpu.make_async_remote_copy(
            src_ref=chunks.at[f],
            dst_ref=columns.at[f],
            send_sem=send.at[0],
            recv_sem=recv_cols.at[f],
            device_id=(f, block),
            device_id_type=MESH,
        ).wait_recv()
    for g in range(n_groups):
        cols = jnp.concatenate(
            [columns[:, kind, g].reshape(nf, nf) for kind in (0, 1)], axis=0
        )
        rows_t = lax.dot_general(
            cols, table[...], (((0,), (0,)), ((), ())), preferred_element_type=F32
        ).astype(BF16)
        n = min(group, pairs - g * group)
        window[OWN, DERIV, freq, g * group : g * group + n] = rows_t.reshape(group, rows, nf)[:n]
    push_x(DERIV, freq)
    push(OWN, DERIV, freq, y_up)
    push(OWN, DERIV, freq, y_down)
    push(OWN, DERIV, freq, sibling)
    fill_left(left_deriv, OWN, DERIV)

    arrive(OWN, VERTEX, f_down)
    push(OWN, VERTEX, f_down, y_up)
    push(OWN, VERTEX, f_down, sibling)
    arrive(OWN, VERTEX, f_up)
    push(OWN, VERTEX, f_up, sibling)

    for b in (BEFORE, AFTER):
        arrive(b, VERTEX, freq)
        push(b, VERTEX, freq, y_up)
        push(b, VERTEX, freq, y_down)
        push(b, VERTEX, freq, sibling)
        fill_left(left_vertex, b, VERTEX)
    arrive(OWN, VERTEX, f_far)
    push(OWN, VERTEX, f_far, sibling)

    arrive(OWN, DERIV, f_up)
    push(OWN, DERIV, f_up, y_down)
    push_x(DERIV, f_up)
    push(OWN, DERIV, f_up, sibling)
    arrive(OWN, DERIV, f_down)
    push_x(DERIV, f_down)
    push(OWN, DERIV, f_down, sibling)
    for b in (BEFORE, AFTER):
        arrive(b, DERIV, freq)
        push(b, DERIV, freq, sibling)
        fill_left(left_deriv, b, DERIV)
    arrive(OWN, DERIV, f_far)
    push_x(DERIV, f_far)
    push(OWN, DERIV, f_far, sibling)

    def from_sibling(b, kind):
        for f in (0, 2, 4, 6):
            arrive(b, kind, (sibling[0] + f) % n_freq)

    to_scalar.wait()

    def add_terms(b, kind, left):
        offset = place[b] - 1

        def some_pairs(t, carry):
            halves, weights = [], []
            for j in range(STEP):
                p = STEP * t + j
                halves.append(
                    jnp.concatenate([left[sel[r, offset + p]] for r in range(pairs)], axis=0)
                )
                weights.append(window[b, kind, :, p].reshape(nf, nf))
            terms = jnp.dot(
                jnp.concatenate(halves, axis=1),
                jnp.concatenate(weights, axis=0),
                preferred_element_type=F32,
            )
            out_ref[...] += terms.reshape(pairs, rows, nf)
            return carry

        lax.fori_loop(0, pairs // STEP, some_pairs, 0)

    out_ref[...] = jnp.zeros_like(out_ref)

    arrive(BEFORE, VERTEX, f_down)
    push(BEFORE, VERTEX, f_down, y_up)
    push(BEFORE, VERTEX, f_down, sibling)
    arrive(AFTER, VERTEX, f_up)
    push(AFTER, VERTEX, f_up, y_down)
    push(AFTER, VERTEX, f_up, sibling)
    from_sibling(OWN, VERTEX)
    add_terms(OWN, VERTEX, left_deriv)
    arrive(BEFORE, VERTEX, f_up)
    push(BEFORE, VERTEX, f_up, sibling)
    arrive(AFTER, VERTEX, f_down)
    push(AFTER, VERTEX, f_down, sibling)
    from_sibling(OWN, DERIV)
    add_terms(OWN, DERIV, left_vertex)
    for b in (BEFORE, AFTER):
        for f in (f_up, f_down):
            arrive(b, DERIV, f)
            push(b, DERIV, f, sibling)
    for b in (BEFORE, AFTER):
        arrive(b, VERTEX, f_far)
        push(b, VERTEX, f_far, sibling)
    for b in (BEFORE, AFTER):
        from_sibling(b, VERTEX)
        add_terms(b, VERTEX, left_deriv)
    for b in (BEFORE, AFTER):
        arrive(b, DERIV, f_far)
        push(b, DERIV, f_far, sibling)
    for b in (BEFORE, AFTER):
        from_sibling(b, DERIV)
        add_terms(b, DERIV, left_vertex)

    for copy in sent:
        copy.wait_send()


def per_device(
    dims,
    vertex,
    deriv_s,
    deriv_u,
    freq_map_s,
    freq_map_u,
    pair_sym,
    propagator,
    left_pairs,
    right_pairs,
    lengths,
):
    n_freq, _ = dims
    pairs, rows, nf = vertex.shape
    n_groups = -(-pairs * rows // nf)
    vmem = pl.BlockSpec(memory_space=pltpu.VMEM)
    smem = pl.BlockSpec(memory_space=pltpu.SMEM)
    return pl.pallas_call(
        functools.partial(kernel, dims),
        out_shape=jax.ShapeDtypeStruct((pairs, rows, nf), F32),
        in_specs=[pl.BlockSpec(memory_space=pltpu.HBM)] * 8 + [smem] * 2,
        out_specs=vmem,
        scratch_shapes=[
            pltpu.VMEM((pairs, rows, nf), BF16),
            pltpu.VMEM((pairs, rows, nf), BF16),
            pltpu.VMEM((1, nf), jnp.int32),
            pltpu.VMEM((1, nf), jnp.int32),
            pltpu.VMEM((1, nf), F32),
            pltpu.VMEM(left_pairs.shape, jnp.int32),
            pltpu.VMEM(right_pairs.shape, jnp.int32),
            pltpu.VMEM((3, 2, n_freq, pairs, rows, nf), BF16),
            pltpu.VMEM((1 + 3 * pairs, rows, nf), BF16),
            pltpu.VMEM((1 + 3 * pairs, rows, nf), BF16),
            pltpu.VMEM((n_freq, 2, n_groups, rows, nf), BF16),
            pltpu.VMEM((n_freq, 2, n_groups, rows, nf), BF16),
            pltpu.VMEM((2 * nf, nf), BF16),
            pltpu.VMEM((pairs, nf), jnp.int32),
            pltpu.SMEM((pairs, nf), jnp.int32),
            pltpu.SemaphoreType.DMA((3, 2, n_freq)),
            pltpu.SemaphoreType.DMA((n_freq,)),
            pltpu.SemaphoreType.DMA((64,)),
            pltpu.SemaphoreType.DMA((9,)),
        ],
        compiler_params=pltpu.CompilerParams(
            collective_id=0, has_side_effects=True, vmem_limit_bytes=63 * 1024 * 1024
        ),
    )(
        vertex,
        jnp.swapaxes(deriv_s, 1, 2),
        jnp.swapaxes(deriv_u, 1, 2),
        freq_map_s.reshape(1, nf),
        freq_map_u.reshape(1, nf),
        propagator.reshape(1, nf),
        left_pairs,
        right_pairs,
        pair_sym,
        lengths,
    )


def solution(mesh):
    dims = (mesh.shape["freq"], mesh.shape["pair"])
    return jax.shard_map(
        functools.partial(per_device, dims),
        mesh=mesh,
        in_specs=(
            P("pair", "freq", None),
            P("pair", None, "freq"),
            P("pair", None, "freq"),
            P(),
            P(),
            P("pair"),
            P(),
            P("pair", None),
            P("pair", None),
            P("pair"),
        ),
        out_specs=P("pair", "freq", None),
        check_vma=False,
    )
```

```python
import functools

import jax
import jax.numpy as jnp
from jax import lax
from jax.experimental import pallas as pl
from jax.experimental.pallas import tpu as pltpu
from jax.sharding import PartitionSpec as P

MESH = pl.DeviceIdType.MESH
BF16 = jnp.bfloat16
F32 = jnp.float32

OWN, BEFORE, AFTER = 0, 1, 2
VERTEX, DERIV = 0, 1

STEP = 10


def kernel(
    dims,
    v_in,
    s_in,
    u_in,
    map_s_in,
    map_u_in,
    prop_in,
    left_in,
    right_in,
    sym_ref,
    len_ref,
    out_ref,
    s_ref,
    u_ref,
    map_s_ref,
    map_u_ref,
    prop_ref,
    left_ref,
    right_ref,
    window,
    left_vertex,
    left_deriv,
    chunks,
    columns,
    table,
    sel_vec,
    sel,
    recv,
    recv_cols,
    send,
    local,
):
    n_freq, n_pair = dims
    pairs, rows, nf = v_in.shape
    slots = left_ref.shape[1]
    freq, block = lax.axis_index("freq"), lax.axis_index("pair")

    loads = [
        pltpu.make_async_copy(src, dst, local.at[i])
        for i, (src, dst) in enumerate(
            (
                (v_in, window.at[OWN, VERTEX, freq]),
                (s_in, s_ref),
                (u_in, u_ref),
                (map_s_in, map_s_ref),
                (map_u_in, map_u_ref),
                (prop_in, prop_ref),
                (left_in, left_ref),
                (right_in, right_ref),
            )
        )
    ]
    for load in loads:
        load.start()

    sibling = (freq + 1 - 2 * (freq % 2), block)
    y_up = ((freq + 2) % n_freq, block)
    y_down = ((freq + n_freq - 2) % n_freq, block)
    x_up = (freq, (block + 1) % n_pair)
    x_down = (freq, (block + n_pair - 1) % n_pair)

    barrier = pltpu.get_barrier_semaphore()
    peers = [((freq + o) % n_freq, block) for o in range(1, n_freq)] + [x_up, x_down]
    for peer in peers:
        pl.semaphore_signal(barrier, inc=1, device_id=peer, device_id_type=MESH)
    pl.semaphore_wait(barrier, len(peers))

    sent = []

    def copy_to(src, dst, recv_sem, peer):
        copy = pltpu.make_async_remote_copy(
            src_ref=src,
            dst_ref=dst,
            send_sem=send.at[len(sent)],
            recv_sem=recv_sem,
            device_id=peer,
            device_id_type=MESH,
        )
        copy.start()
        sent.append(copy)

    def push(b, kind, f, peer, as_block=None):
        to = b if as_block is None else as_block
        copy_to(window.at[b, kind, f], window.at[to, kind, f], recv.at[to, kind, f], peer)

    def push_x(kind, f, upward=(True, False)):
        for up in upward:
            if up:
                push(OWN, kind, f, x_up, BEFORE)
            else:
                push(OWN, kind, f, x_down, AFTER)

    def arrive(b, kind, f):
        ref = window.at[b, kind, f]
        pltpu.make_async_remote_copy(
            src_ref=ref,
            dst_ref=ref,
            send_sem=send.at[0],
            recv_sem=recv.at[b, kind, f],
            device_id=sibling,
            device_id_type=MESH,
        ).wait_recv()

    f_up, f_down, f_far = (freq + 2) % n_freq, (freq + 6) % n_freq, (freq + 4) % n_freq

    for load in loads:
        load.wait()
    push_x(VERTEX, freq)
    push(OWN, VERTEX, freq, sibling)

    group = nf // rows
    n_groups = columns.shape[2]
    lane = lax.broadcasted_iota(jnp.int32, (rows, nf), 1)
    first_pair = block * pairs
    for kind, src in ((0, s_ref), (1, u_ref)):
        for g in range(n_groups):
            parts = []
            for q in range(group):
                p = g * group + q
                if p >= pairs:
                    parts.append(jnp.zeros((rows, nf), F32))
                elif kind == 0:
                    parts.append(src[p].astype(F32))
                else:
                    parts.append(src[lax.rem(sym_ref[p], pairs)].astype(F32))
            step = 1
            while step < group:
                high = (lane // (rows * step)) % 2 == 1
                for q in range(group):
                    if (q // step) % 2 == 0:
                        a, b = parts[q], parts[q + step]
                        parts[q] = jnp.where(high, pltpu.roll(b, rows * step, 1), a)
                        parts[q + step] = jnp.where(high, b, pltpu.roll(a, nf - rows * step, 1))
                step *= 2
            for f in range(n_freq):
                chunks[f, kind, g] = parts[f].astype(BF16)
    columns[freq] = chunks[freq]
    for o in (4, 3, 5, 2, 6, 1, 7):
        f = (freq + o) % n_freq
        copy_to(chunks.at[f], columns.at[freq], recv_cols.at[freq], (f, block))
    push(OWN, VERTEX, freq, y_up)
    push(OWN, VERTEX, freq, y_down)

    wide = lax.broadcasted_iota(jnp.int32, (nf, nf), 0)
    table[0:nf, :] = jnp.where(wide == map_s_ref[...], 1.0, 0.0).astype(BF16)
    table[nf : 2 * nf, :] = jnp.where(wide == map_u_ref[...], 1.0, 0.0).astype(BF16)
    window_first = first_pair - pairs
    row_id = lax.broadcasted_iota(jnp.int32, (pairs, slots), 0)
    slot_id = lax.broadcasted_iota(jnp.int32, (pairs, slots), 1)
    count = jnp.zeros((pairs, slots), jnp.int32)
    for r in range(pairs):
        count = jnp.where(row_id == r, len_ref[r], count)
    target = jnp.where(slot_id < count, right_ref[...] - window_first, -1)
    source = left_ref[...] - (window_first - 1)
    lanes = lax.broadcasted_iota(jnp.int32, (pairs, nf), 1)
    chosen = jnp.zeros((pairs, nf), jnp.int32)
    for k in range(slots):
        chosen = jnp.where(target[:, k : k + 1] == lanes, source[:, k : k + 1], chosen)
    sel_vec[...] = chosen
    to_scalar = pltpu.make_async_copy(sel_vec, sel, local.at[8])
    to_scalar.start()

    prop = prop_ref[...]
    place = {BEFORE: 1, OWN: 1 + pairs, AFTER: 1 + 2 * pairs}

    def fill_left(left, b, kind):
        rows_of = window[b, kind, freq].astype(F32) * prop
        left[place[b] : place[b] + pairs] = rows_of.astype(BF16)

    left_vertex[0] = jnp.zeros((rows, nf), BF16)
    left_deriv[0] = jnp.zeros((rows, nf), BF16)
    fill_left(left_vertex, OWN, VERTEX)

    def fill_neighbours(left, kind):
        for b in (BEFORE, AFTER):
            arrive(b, kind, freq)
            push(b, kind, freq, sibling)
            fill_left(left, b, kind)

    fill_neighbours(left_vertex, VERTEX)

    for o in range(1, n_freq):
        f = (freq + o) % n_freq
        pltpu.make_async_remote_copy(
            src_ref=chunks.at[f],
            dst_ref=columns.at[f],
            send_sem=send.at[0],
            recv_sem=recv_cols.at[f],
            device_id=(f, block),
            device_id_type=MESH,
        ).wait_recv()
    for g in range(n_groups):
        cols = jnp.concatenate(
            [columns[:, kind, g].reshape(nf, nf) for kind in (0, 1)], axis=0
        )
        rows_t = lax.dot_general(
            cols, table[...], (((0,), (0,)), ((), ())), preferred_element_type=F32
        ).astype(BF16)
        n = min(group, pairs - g * group)
        window[OWN, DERIV, freq, g * group : g * group + n] = rows_t.reshape(group, rows, nf)[:n]
    push(OWN, DERIV, freq, y_up)
    push(OWN, DERIV, freq, y_down)
    push_x(DERIV, freq)
    push(OWN, DERIV, freq, sibling)
    fill_left(left_deriv, OWN, DERIV)

    arrive(OWN, VERTEX, f_down)
    push(OWN, VERTEX, f_down, y_up)
    push_x(VERTEX, f_down)
    push(OWN, VERTEX, f_down, sibling)
    arrive(OWN, VERTEX, f_up)
    push(OWN, VERTEX, f_up, sibling)
    arrive(OWN, DERIV, f_up)
    push(OWN, DERIV, f_up, y_down)
    push_x(DERIV, f_up)
    push(OWN, DERIV, f_up, sibling)
    arrive(OWN, DERIV, f_down)
    push_x(DERIV, f_down)
    push(OWN, DERIV, f_down, sibling)
    for b in (BEFORE, AFTER):
        push(b, VERTEX, freq, y_down)
    fill_neighbours(left_deriv, DERIV)
    arrive(OWN, VERTEX, f_far)
    push(OWN, VERTEX, f_far, sibling)

    def from_sibling(b, kind):
        for f in (0, 2, 4, 6):
            arrive(b, kind, (sibling[0] + f) % n_freq)

    to_scalar.wait()

    def add_terms(b, kind, left):
        offset = place[b] - 1

        def some_pairs(t, carry):
            halves, weights = [], []
            for j in range(STEP):
                p = STEP * t + j
                halves.append(
                    jnp.concatenate([left[sel[r, offset + p]] for r in range(pairs)], axis=0)
                )
                weights.append(window[b, kind, :, p].reshape(nf, nf))
            terms = jnp.dot(
                jnp.concatenate(halves, axis=1),
                jnp.concatenate(weights, axis=0),
                preferred_element_type=F32,
            )
            out_ref[...] += terms.reshape(pairs, rows, nf)
            return carry

        lax.fori_loop(0, pairs // STEP, some_pairs, 0)

    out_ref[...] = jnp.zeros_like(out_ref)

    from_sibling(OWN, VERTEX)
    add_terms(OWN, VERTEX, left_deriv)
    for b in (BEFORE, AFTER):
        arrive(b, VERTEX, f_down)
        push(b, VERTEX, f_down, y_up)
        push(b, VERTEX, f_down, sibling)
    arrive(OWN, DERIV, f_far)
    push_x(DERIV, f_far)
    push(OWN, DERIV, f_far, sibling)
    from_sibling(OWN, DERIV)
    add_terms(OWN, DERIV, left_vertex)
    for f in (f_up, f_down):
        for b in (BEFORE, AFTER):
            arrive(b, DERIV, f)
            push(b, DERIV, f, sibling)
    for b in (BEFORE, AFTER):
        for f in (f_up, f_far):
            arrive(b, VERTEX, f)
            push(b, VERTEX, f, sibling)
        from_sibling(b, VERTEX)
        add_terms(b, VERTEX, left_deriv)
    for b in (BEFORE, AFTER):
        arrive(b, DERIV, f_far)
        push(b, DERIV, f_far, sibling)
    for b in (BEFORE, AFTER):
        from_sibling(b, DERIV)
        add_terms(b, DERIV, left_vertex)

    for copy in sent:
        copy.wait_send()


def per_device(
    dims,
    vertex,
    deriv_s,
    deriv_u,
    freq_map_s,
    freq_map_u,
    pair_sym,
    propagator,
    left_pairs,
    right_pairs,
    lengths,
):
    n_freq, _ = dims
    pairs, rows, nf = vertex.shape
    n_groups = -(-pairs * rows // nf)
    vmem = pl.BlockSpec(memory_space=pltpu.VMEM)
    smem = pl.BlockSpec(memory_space=pltpu.SMEM)
    return pl.pallas_call(
        functools.partial(kernel, dims),
        out_shape=jax.ShapeDtypeStruct((pairs, rows, nf), F32),
        in_specs=[pl.BlockSpec(memory_space=pltpu.HBM)] * 8 + [smem] * 2,
        out_specs=vmem,
        scratch_shapes=[
            pltpu.VMEM((pairs, rows, nf), BF16),
            pltpu.VMEM((pairs, rows, nf), BF16),
            pltpu.VMEM((1, nf), jnp.int32),
            pltpu.VMEM((1, nf), jnp.int32),
            pltpu.VMEM((1, nf), F32),
            pltpu.VMEM(left_pairs.shape, jnp.int32),
            pltpu.VMEM(right_pairs.shape, jnp.int32),
            pltpu.VMEM((3, 2, n_freq, pairs, rows, nf), BF16),
            pltpu.VMEM((1 + 3 * pairs, rows, nf), BF16),
            pltpu.VMEM((1 + 3 * pairs, rows, nf), BF16),
            pltpu.VMEM((n_freq, 2, n_groups, rows, nf), BF16),
            pltpu.VMEM((n_freq, 2, n_groups, rows, nf), BF16),
            pltpu.VMEM((2 * nf, nf), BF16),
            pltpu.VMEM((pairs, nf), jnp.int32),
            pltpu.SMEM((pairs, nf), jnp.int32),
            pltpu.SemaphoreType.DMA((3, 2, n_freq)),
            pltpu.SemaphoreType.DMA((n_freq,)),
            pltpu.SemaphoreType.DMA((64,)),
            pltpu.SemaphoreType.DMA((9,)),
        ],
        compiler_params=pltpu.CompilerParams(
            collective_id=0, has_side_effects=True, vmem_limit_bytes=63 * 1024 * 1024
        ),
    )(
        vertex,
        jnp.swapaxes(deriv_s, 1, 2),
        jnp.swapaxes(deriv_u, 1, 2),
        freq_map_s.reshape(1, nf),
        freq_map_u.reshape(1, nf),
        propagator.reshape(1, nf),
        left_pairs,
        right_pairs,
        pair_sym,
        lengths,
    )


def solution(mesh):
    dims = (mesh.shape["freq"], mesh.shape["pair"])
    return jax.shard_map(
        functools.partial(per_device, dims),
        mesh=mesh,
        in_specs=(
            P("pair", "freq", None),
            P("pair", None, "freq"),
            P("pair", None, "freq"),
            P(),
            P(),
            P("pair"),
            P(),
            P("pair", None),
            P("pair", None),
            P("pair"),
        ),
        out_specs=P("pair", "freq", None),
        check_vma=False,
    )
```

```python
import functools

import jax
import jax.numpy as jnp
from jax import lax
from jax.experimental import pallas as pl
from jax.experimental.pallas import tpu as pltpu
from jax.sharding import PartitionSpec as P

MESH = pl.DeviceIdType.MESH
BF16 = jnp.bfloat16
F32 = jnp.float32

OWN, BEFORE, AFTER = 0, 1, 2
VERTEX, DERIV = 0, 1


def kernel(
    dims,
    v_in,
    s_in,
    u_in,
    map_s_in,
    map_u_in,
    prop_in,
    left_in,
    right_in,
    sym_ref,
    len_ref,
    out_ref,
    s_ref,
    u_ref,
    map_s_ref,
    map_u_ref,
    prop_ref,
    left_ref,
    right_ref,
    window,
    left_vertex,
    left_deriv,
    chunks,
    columns,
    table,
    factors,
    sel_vec,
    sel,
    recv,
    recv_cols,
    send,
    local,
):
    n_freq, n_pair = dims
    pairs, rows, nf = v_in.shape
    slots = left_ref.shape[1]
    freq, block = lax.axis_index("freq"), lax.axis_index("pair")

    loads = [
        pltpu.make_async_copy(src, dst, local.at[i])
        for i, (src, dst) in enumerate(
            (
                (v_in, window.at[OWN, VERTEX, freq]),
                (s_in, s_ref),
                (u_in, u_ref),
                (map_s_in, map_s_ref),
                (map_u_in, map_u_ref),
                (prop_in, prop_ref),
                (left_in, left_ref),
                (right_in, right_ref),
            )
        )
    ]
    for load in loads:
        load.start()

    sibling = (freq + 1 - 2 * (freq % 2), block)
    y_up = ((freq + 2) % n_freq, block)
    y_down = ((freq + n_freq - 2) % n_freq, block)
    x_up = (freq, (block + 1) % n_pair)
    x_down = (freq, (block + n_pair - 1) % n_pair)

    barrier = pltpu.get_barrier_semaphore()
    peers = [((freq + o) % n_freq, block) for o in range(1, n_freq)] + [x_up, x_down]
    for peer in peers:
        pl.semaphore_signal(barrier, inc=1, device_id=peer, device_id_type=MESH)
    pl.semaphore_wait(barrier, len(peers))

    sent = []

    def copy_to(src, dst, recv_sem, peer):
        copy = pltpu.make_async_remote_copy(
            src_ref=src,
            dst_ref=dst,
            send_sem=send.at[len(sent)],
            recv_sem=recv_sem,
            device_id=peer,
            device_id_type=MESH,
        )
        copy.start()
        sent.append(copy)

    def push(b, kind, f, peer, as_block=None):
        to = b if as_block is None else as_block
        copy_to(window.at[b, kind, f], window.at[to, kind, f], recv.at[to, kind, f], peer)

    def push_x(kind, f, upward=(True, False)):
        for up in upward:
            if up:
                push(OWN, kind, f, x_up, BEFORE)
            else:
                push(OWN, kind, f, x_down, AFTER)

    def arrive(b, kind, f):
        ref = window.at[b, kind, f]
        pltpu.make_async_remote_copy(
            src_ref=ref,
            dst_ref=ref,
            send_sem=send.at[0],
            recv_sem=recv.at[b, kind, f],
            device_id=sibling,
            device_id_type=MESH,
        ).wait_recv()

    f_up, f_down, f_far = (freq + 2) % n_freq, (freq + 6) % n_freq, (freq + 4) % n_freq

    for load in loads:
        load.wait()
    push_x(VERTEX, freq)
    push(OWN, VERTEX, freq, sibling)

    group = nf // rows
    n_groups = columns.shape[2]
    lane = lax.broadcasted_iota(jnp.int32, (rows, nf), 1)
    first_pair = block * pairs
    for kind, src in ((0, s_ref), (1, u_ref)):
        for g in range(n_groups):
            parts = []
            for q in range(group):
                p = g * group + q
                if p >= pairs:
                    parts.append(jnp.zeros((rows, nf), F32))
                elif kind == 0:
                    parts.append(src[p].astype(F32))
                else:
                    parts.append(src[lax.rem(sym_ref[p], pairs)].astype(F32))
            step = 1
            while step < group:
                high = (lane // (rows * step)) % 2 == 1
                for q in range(group):
                    if (q // step) % 2 == 0:
                        a, b = parts[q], parts[q + step]
                        parts[q] = jnp.where(high, pltpu.roll(b, rows * step, 1), a)
                        parts[q + step] = jnp.where(high, b, pltpu.roll(a, nf - rows * step, 1))
                step *= 2
            for f in range(n_freq):
                chunks[f, kind, g] = parts[f].astype(BF16)
    columns[freq] = chunks[freq]
    for o in (4, 3, 5, 2, 6, 1, 7):
        f = (freq + o) % n_freq
        copy_to(chunks.at[f], columns.at[freq], recv_cols.at[freq], (f, block))
    push(OWN, VERTEX, freq, y_up)
    push(OWN, VERTEX, freq, y_down)

    wide = lax.broadcasted_iota(jnp.int32, (nf, nf), 0)
    table[0:nf, :] = jnp.where(wide == map_s_ref[...], 1.0, 0.0).astype(BF16)
    table[nf : 2 * nf, :] = jnp.where(wide == map_u_ref[...], 1.0, 0.0).astype(BF16)
    window_first = first_pair - pairs
    row_id = lax.broadcasted_iota(jnp.int32, (pairs, slots), 0)
    slot_id = lax.broadcasted_iota(jnp.int32, (pairs, slots), 1)
    count = jnp.zeros((pairs, slots), jnp.int32)
    for r in range(pairs):
        count = jnp.where(row_id == r, len_ref[r], count)
    target = jnp.where(slot_id < count, right_ref[...] - window_first, -1)
    source = left_ref[...] - (window_first - 1)
    lanes = lax.broadcasted_iota(jnp.int32, (pairs, nf), 1)
    chosen = jnp.zeros((pairs, nf), jnp.int32)
    for k in range(slots):
        chosen = jnp.where(target[:, k : k + 1] == lanes, source[:, k : k + 1], chosen)
    sel_vec[...] = chosen
    to_scalar = pltpu.make_async_copy(sel_vec, sel, local.at[8])
    to_scalar.start()

    prop = prop_ref[...]
    place = {BEFORE: 1, OWN: 1 + pairs, AFTER: 1 + 2 * pairs}

    def fill_left(left, b, kind):
        rows_of = window[b, kind, freq].astype(F32) * prop
        left[place[b] : place[b] + pairs] = rows_of.astype(BF16)

    left_vertex[0] = jnp.zeros((rows, nf), BF16)
    left_deriv[0] = jnp.zeros((rows, nf), BF16)
    fill_left(left_vertex, OWN, VERTEX)

    def fill_neighbours(left, kind):
        for b in (BEFORE, AFTER):
            arrive(b, kind, freq)
            push(b, kind, freq, sibling)
            fill_left(left, b, kind)

    fill_neighbours(left_vertex, VERTEX)

    for o in range(1, n_freq):
        f = (freq + o) % n_freq
        pltpu.make_async_remote_copy(
            src_ref=chunks.at[f],
            dst_ref=columns.at[f],
            send_sem=send.at[0],
            recv_sem=recv_cols.at[f],
            device_id=(f, block),
            device_id_type=MESH,
        ).wait_recv()
    for g in range(n_groups):
        cols = jnp.concatenate(
            [columns[:, kind, g].reshape(nf, nf) for kind in (0, 1)], axis=0
        )
        rows_t = lax.dot_general(
            cols, table[...], (((0,), (0,)), ((), ())), preferred_element_type=F32
        ).astype(BF16)
        n = min(group, pairs - g * group)
        window[OWN, DERIV, freq, g * group : g * group + n] = rows_t.reshape(group, rows, nf)[:n]
    push(OWN, DERIV, freq, y_up)
    push(OWN, DERIV, freq, y_down)
    push_x(DERIV, freq)
    push(OWN, DERIV, freq, sibling)
    fill_left(left_deriv, OWN, DERIV)

    def gather(kind, left):
        def one(q, carry):
            for r in range(pairs):
                factors[kind, q, r * rows : (r + 1) * rows, :] = left[sel[r, q]]
            return carry

        lax.fori_loop(0, 3 * pairs, one, 0)

    to_scalar.wait()
    gather(VERTEX, left_vertex)

    arrive(OWN, VERTEX, f_down)
    push(OWN, VERTEX, f_down, y_up)
    push_x(VERTEX, f_down)
    push(OWN, VERTEX, f_down, sibling)
    arrive(OWN, VERTEX, f_up)
    push(OWN, VERTEX, f_up, sibling)
    arrive(OWN, DERIV, f_up)
    push(OWN, DERIV, f_up, y_down)
    push_x(DERIV, f_up)
    push(OWN, DERIV, f_up, sibling)
    arrive(OWN, DERIV, f_down)
    push_x(DERIV, f_down)
    push(OWN, DERIV, f_down, sibling)
    for b in (BEFORE, AFTER):
        push(b, VERTEX, freq, y_down)
    fill_neighbours(left_deriv, DERIV)
    arrive(OWN, VERTEX, f_far)
    push(OWN, VERTEX, f_far, sibling)
    gather(DERIV, left_deriv)

    def from_sibling(b, kind):
        for f in (0, 2, 4, 6):
            arrive(b, kind, (sibling[0] + f) % n_freq)

    def add_terms(b, kind):
        first = place[b] - 1
        lhs = jnp.concatenate([factors[1 - kind, first + p] for p in range(pairs)], axis=1)
        rhs = jnp.concatenate([window[b, kind, :, p].reshape(nf, nf) for p in range(pairs)], axis=0)
        terms = jnp.dot(lhs, rhs, preferred_element_type=F32)
        out_ref[...] += terms.reshape(pairs, rows, nf)

    out_ref[...] = jnp.zeros_like(out_ref)

    from_sibling(OWN, VERTEX)
    add_terms(OWN, VERTEX)
    for b in (BEFORE, AFTER):
        arrive(b, VERTEX, f_down)
        push(b, VERTEX, f_down, y_up)
        push(b, VERTEX, f_down, sibling)
    arrive(OWN, DERIV, f_far)
    push_x(DERIV, f_far)
    push(OWN, DERIV, f_far, sibling)
    from_sibling(OWN, DERIV)
    add_terms(OWN, DERIV)
    for f in (f_up, f_down):
        for b in (BEFORE, AFTER):
            arrive(b, DERIV, f)
            push(b, DERIV, f, sibling)
    for b in (BEFORE, AFTER):
        for f in (f_up, f_far):
            arrive(b, VERTEX, f)
            push(b, VERTEX, f, sibling)
        from_sibling(b, VERTEX)
        add_terms(b, VERTEX)
    for b in (BEFORE, AFTER):
        arrive(b, DERIV, f_far)
        push(b, DERIV, f_far, sibling)
    for b in (BEFORE, AFTER):
        from_sibling(b, DERIV)
        add_terms(b, DERIV)

    for copy in sent:
        copy.wait_send()


def per_device(
    dims,
    vertex,
    deriv_s,
    deriv_u,
    freq_map_s,
    freq_map_u,
    pair_sym,
    propagator,
    left_pairs,
    right_pairs,
    lengths,
):
    n_freq, _ = dims
    pairs, rows, nf = vertex.shape
    n_groups = -(-pairs * rows // nf)
    vmem = pl.BlockSpec(memory_space=pltpu.VMEM)
    smem = pl.BlockSpec(memory_space=pltpu.SMEM)
    return pl.pallas_call(
        functools.partial(kernel, dims),
        out_shape=jax.ShapeDtypeStruct((pairs, rows, nf), F32),
        in_specs=[pl.BlockSpec(memory_space=pltpu.HBM)] * 8 + [smem] * 2,
        out_specs=vmem,
        scratch_shapes=[
            pltpu.VMEM((pairs, rows, nf), BF16),
            pltpu.VMEM((pairs, rows, nf), BF16),
            pltpu.VMEM((1, nf), jnp.int32),
            pltpu.VMEM((1, nf), jnp.int32),
            pltpu.VMEM((1, nf), F32),
            pltpu.VMEM(left_pairs.shape, jnp.int32),
            pltpu.VMEM(right_pairs.shape, jnp.int32),
            pltpu.VMEM((3, 2, n_freq, pairs, rows, nf), BF16),
            pltpu.VMEM((1 + 3 * pairs, rows, nf), BF16),
            pltpu.VMEM((1 + 3 * pairs, rows, nf), BF16),
            pltpu.VMEM((n_freq, 2, n_groups, rows, nf), BF16),
            pltpu.VMEM((n_freq, 2, n_groups, rows, nf), BF16),
            pltpu.VMEM((2 * nf, nf), BF16),
            pltpu.VMEM((2, 3 * pairs, pairs * rows, nf), BF16),
            pltpu.VMEM((pairs, nf), jnp.int32),
            pltpu.SMEM((pairs, nf), jnp.int32),
            pltpu.SemaphoreType.DMA((3, 2, n_freq)),
            pltpu.SemaphoreType.DMA((n_freq,)),
            pltpu.SemaphoreType.DMA((64,)),
            pltpu.SemaphoreType.DMA((9,)),
        ],
        compiler_params=pltpu.CompilerParams(
            collective_id=0, has_side_effects=True, vmem_limit_bytes=63 * 1024 * 1024
        ),
    )(
        vertex,
        jnp.swapaxes(deriv_s, 1, 2),
        jnp.swapaxes(deriv_u, 1, 2),
        freq_map_s.reshape(1, nf),
        freq_map_u.reshape(1, nf),
        propagator.reshape(1, nf),
        left_pairs,
        right_pairs,
        pair_sym,
        lengths,
    )


def solution(mesh):
    dims = (mesh.shape["freq"], mesh.shape["pair"])
    return jax.shard_map(
        functools.partial(per_device, dims),
        mesh=mesh,
        in_specs=(
            P("pair", "freq", None),
            P("pair", None, "freq"),
            P("pair", None, "freq"),
            P(),
            P(),
            P("pair"),
            P(),
            P("pair", None),
            P("pair", None),
            P("pair"),
        ),
        out_specs=P("pair", "freq", None),
        check_vma=False,
    )
```

```python
import functools

import jax
import jax.numpy as jnp
from jax import lax
from jax.experimental import pallas as pl
from jax.experimental.pallas import tpu as pltpu
from jax.sharding import PartitionSpec as P

MESH = pl.DeviceIdType.MESH
BF16 = jnp.bfloat16
F32 = jnp.float32

BEFORE, OWN, AFTER = 0, 1, 2
VERTEX, DERIV = 0, 1
PARTS, COUPLES = 3, 10


def regroup(parts):
    count = len(parts)
    rows, lanes = parts[0].shape
    width = lanes // count
    lane = lax.broadcasted_iota(jnp.int32, (rows, lanes), 1)
    parts = list(parts)
    step = 1
    while step < count:
        high = (lane // (width * step)) % 2 == 1
        for q in range(count):
            if (q // step) % 2 == 0:
                a, b = parts[q], parts[q + step]
                parts[q] = jnp.where(high, pltpu.roll(b, width * step, 1), a)
                parts[q + step] = jnp.where(high, b, pltpu.roll(a, lanes - width * step, 1))
        step *= 2
    return parts


def kernel(
    dims,
    v_in,
    s_in,
    u_in,
    map_s_in,
    map_u_in,
    prop_in,
    left_in,
    right_in,
    sym_ref,
    len_ref,
    out_ref,
    s_ref,
    u_ref,
    map_s_ref,
    map_u_ref,
    prop_ref,
    left_ref,
    right_ref,
    right,
    packed,
    spread,
    lefts,
    chunks,
    columns,
    table,
    sums,
    part_out,
    part_in,
    sel_vec,
    sel,
    recv_right,
    recv_spread,
    recv_beside,
    recv_cols,
    recv_part,
    send,
    local,
):
    n_freq, n_pair = dims
    n_chip = n_freq // 2
    pairs, rows, nf = v_in.shape
    slots = left_ref.shape[1]
    freq, block = lax.axis_index("freq"), lax.axis_index("pair")
    chip, core = freq // 2, freq % 2

    sibling = (freq + 1 - 2 * core, block)
    x_up = (freq, (block + 1) % n_pair)
    x_down = (freq, (block + n_pair - 1) % n_pair)

    def own(kind, slot=OWN, of=core):
        return right.at[kind, of, slot * pairs : (slot + 1) * pairs]

    loads = [
        pltpu.make_async_copy(src, dst, local.at[i])
        for i, (src, dst) in enumerate(
            (
                (v_in, own(VERTEX)),
                (s_in, s_ref),
                (u_in, u_ref),
                (map_s_in, map_s_ref),
                (map_u_in, map_u_ref),
                (prop_in, prop_ref),
                (left_in, left_ref),
                (right_in, right_ref),
            )
        )
    ]
    for load in loads:
        load.start()

    barrier = pltpu.get_barrier_semaphore()
    peers = [((freq + o) % n_freq, block) for o in range(1, n_freq)] + [x_up, x_down]
    for peer in peers:
        pl.semaphore_signal(barrier, inc=1, device_id=peer, device_id_type=MESH)
    pl.semaphore_wait(barrier, len(peers))

    sent = []

    def push(src, dst, recv_sem, peer):
        copy = pltpu.make_async_remote_copy(
            src_ref=src,
            dst_ref=dst,
            send_sem=send.at[len(sent)],
            recv_sem=recv_sem,
            device_id=peer,
            device_id_type=MESH,
        )
        copy.start()
        sent.append(copy)

    def arrive(ref, recv_sem):
        pltpu.make_async_remote_copy(
            src_ref=ref,
            dst_ref=ref,
            send_sem=send.at[0],
            recv_sem=recv_sem,
            device_id=sibling,
            device_id_type=MESH,
        ).wait_recv()

    def push_beside(kind):
        push(own(kind), own(kind, BEFORE), recv_right.at[kind, core, BEFORE], x_up)
        push(own(kind), own(kind, AFTER), recv_right.at[kind, core, AFTER], x_down)

    def push_sibling(kind, slot):
        push(own(kind, slot), own(kind, slot), recv_right.at[kind, core, slot], sibling)

    n_packed = packed.shape[2]
    zero_rows = jnp.zeros((rows, nf), F32)

    def push_left(kind):
        for g in range(n_packed):
            four = [
                right[kind, core, OWN * pairs + p].astype(F32) if p < pairs else zero_rows
                for p in range(n_chip * g, n_chip * (g + 1))
            ]
            for c, tile in enumerate(regroup(four)):
                packed[kind, c, g] = tile.astype(BF16)
        spread[OWN, kind, chip] = packed[kind, chip]
        for o in (2, 1, 3):
            c = (chip + o) % n_chip
            push(
                packed.at[kind, c],
                spread.at[OWN, kind, chip],
                recv_spread.at[kind, chip],
                (2 * c + core, block),
            )

    def pass_left_on(kind):
        for o in (1, 3, 2):
            c = (chip + o) % n_chip
            arrive(spread.at[OWN, kind, c], recv_spread.at[kind, c])
        push(spread.at[OWN, kind], spread.at[BEFORE, kind], recv_beside.at[kind, BEFORE], x_up)
        push(spread.at[OWN, kind], spread.at[AFTER, kind], recv_beside.at[kind, AFTER], x_down)

    loads[0].wait()
    push_beside(VERTEX)
    push_sibling(VERTEX, OWN)
    push_left(VERTEX)

    for load in loads[1:]:
        load.wait()
    group = nf // rows
    n_groups = columns.shape[2]
    for kind in (0, 1):
        for g in range(n_groups):
            eight = []
            for p in range(g * group, (g + 1) * group):
                if p >= pairs:
                    eight.append(zero_rows)
                elif kind == 0:
                    eight.append(s_ref[p].astype(F32))
                else:
                    eight.append(u_ref[lax.rem(sym_ref[p], pairs)].astype(F32))
            for f, tile in enumerate(regroup(eight)):
                chunks[f, kind, g] = tile.astype(BF16)
    columns[freq] = chunks[freq]
    for o in (4, 3, 5, 2, 6, 1, 7):
        f = (freq + o) % n_freq
        push(chunks.at[f], columns.at[freq], recv_cols.at[freq], (f, block))

    wide = lax.broadcasted_iota(jnp.int32, (nf, nf), 0)
    table[0:nf, :] = jnp.where(wide == map_s_ref[...], 1.0, 0.0).astype(BF16)
    table[nf : 2 * nf, :] = jnp.where(wide == map_u_ref[...], 1.0, 0.0).astype(BF16)
    window_first = (block - 1) * pairs
    row_id = lax.broadcasted_iota(jnp.int32, (pairs, slots), 0)
    slot_id = lax.broadcasted_iota(jnp.int32, (pairs, slots), 1)
    count = jnp.zeros((pairs, slots), jnp.int32)
    for r in range(pairs):
        count = jnp.where(row_id == r, len_ref[r], count)
    target = jnp.where(slot_id < count, right_ref[...] - window_first, -1)
    source = left_ref[...] - window_first
    stride = n_chip * n_packed
    gap = stride - pairs
    source = source + 1 + jnp.where(source >= pairs, gap, 0) + jnp.where(source >= 2 * pairs, gap, 0)
    lanes = lax.broadcasted_iota(jnp.int32, (pairs, nf), 1)
    chosen = jnp.zeros((pairs, nf), jnp.int32)
    for k in range(slots):
        chosen = jnp.where(target[:, k : k + 1] == lanes, source[:, k : k + 1], chosen)
    sel_vec[...] = chosen
    to_scalar = pltpu.make_async_copy(sel_vec, sel, local.at[8])
    to_scalar.start()

    width = nf // n_chip
    tile_lane = lax.broadcasted_iota(jnp.int32, (rows, nf), 1)
    wide_prop = jnp.broadcast_to(prop_ref[...], (rows, nf))
    tiles = regroup([wide_prop] * n_chip)
    prop = tiles[0]
    for c in range(1, n_chip):
        prop = jnp.where(chip == c, tiles[c], prop)

    pass_left_on(VERTEX)

    for o in range(1, n_freq):
        f = (freq + o) % n_freq
        arrive(columns.at[f], recv_cols.at[f])
    for g in range(n_groups):
        cols = jnp.concatenate([columns[:, kind, g].reshape(nf, nf) for kind in (0, 1)], axis=0)
        rows_t = lax.dot_general(
            cols, table[...], (((0,), (0,)), ((), ())), preferred_element_type=F32
        ).astype(BF16)
        n = min(group, pairs - g * group)
        start = OWN * pairs + g * group
        right[DERIV, core, start : start + n] = rows_t.reshape(group, rows, nf)[:n]
    push_beside(DERIV)
    push_left(DERIV)
    push_sibling(DERIV, OWN)

    for half in (0, 1):
        lefts[half, 0] = jnp.zeros(lefts.shape[2:], BF16)

    def fill_lefts(slot):
        def one(g, carry):
            for c in range(n_chip):
                turned = []
                for kind in (VERTEX, DERIV):
                    tile = (spread[slot, kind, c, g].astype(F32) * prop).astype(BF16).astype(F32)
                    turned.append(
                        [tile] + [pltpu.roll(tile, width * k, 1) for k in range(1, n_chip)]
                    )
                for q in range(n_chip):
                    for half in (0, 1):
                        lane0 = 2 * half
                        tile = jnp.where(
                            tile_lane // width == lane0,
                            turned[VERTEX][(lane0 - q) % n_chip],
                            jnp.where(
                                tile_lane // width == lane0 + 1,
                                turned[DERIV][(lane0 + 1 - q) % n_chip],
                                0.0,
                            ),
                        )
                        lefts[half, 1 + slot * stride + g * n_chip + q, c] = tile.astype(BF16)
            return carry

        lax.fori_loop(0, n_packed, one, 0)

    for slot in (BEFORE, AFTER):
        arrive(own(VERTEX, slot), recv_right.at[VERTEX, core, slot])
        push_sibling(VERTEX, slot)
    pass_left_on(DERIV)
    fill_lefts(OWN)
    for slot in (BEFORE, AFTER):
        arrive(own(DERIV, slot), recv_right.at[DERIV, core, slot])
        push_sibling(DERIV, slot)
    for slot in (BEFORE, AFTER):
        for kind in (VERTEX, DERIV):
            arrive(spread.at[slot, kind], recv_beside.at[kind, slot])
        fill_lefts(slot)
    other = 1 - core
    for slot in (OWN, BEFORE, AFTER):
        for kind in (VERTEX, DERIV):
            arrive(own(kind, slot, other), recv_right.at[kind, other, slot])

    to_scalar.wait()
    size = pairs // PARTS
    tall = n_chip * rows

    def add_terms(first_row, first_couple, couples):
        lhs, rhs = [], []
        for j in range(couples):
            q = 2 * (first_couple + j)
            lhs.append(
                jnp.concatenate(
                    [
                        (lefts[0, sel[r, q]] + lefts[1, sel[r, q + 1]]).reshape(tall, nf)
                        for r in range(first_row, first_row + size)
                    ],
                    axis=0,
                )
            )
            for p in (q, q + 1):
                rhs += [right[kind, :, p].reshape(2 * rows, nf) for kind in (DERIV, VERTEX)]
        terms = jnp.dot(
            jnp.concatenate(lhs, axis=1),
            jnp.concatenate(rhs, axis=0),
            preferred_element_type=F32,
        )
        return terms.reshape(size, n_chip, rows, nf)

    n_couples = 3 * pairs // 2
    whole = n_couples // COUPLES
    for part in range(PARTS):
        first_row = part * size
        here = sums.at[first_row : first_row + size]
        here[...] = add_terms(first_row, whole * COUPLES, n_couples - whole * COUPLES)

        def step(t, carry, first_row=first_row, here=here):
            here[...] += add_terms(first_row, t * COUPLES, COUPLES)
            return carry

        lax.fori_loop(0, whole, step, 0)
        for o in (2, 1, 3):
            c = (chip + o) % n_chip
            part_out[part, o] = sums[first_row : first_row + size, c].astype(BF16)
            push(
                part_out.at[part, o],
                part_in.at[part, chip],
                recv_part.at[part, chip],
                (2 * c + core, block),
            )
    for part in range(PARTS):
        first_row = part * size
        total = sums[first_row : first_row + size, chip]
        for o in (1, 3, 2):
            c = (chip + o) % n_chip
            arrive(part_in.at[part, c], recv_part.at[part, c])
            total = total + part_in[part, c].astype(F32)
        out_ref[first_row : first_row + size] = total

    for copy in sent:
        copy.wait_send()


def per_device(
    dims,
    vertex,
    deriv_s,
    deriv_u,
    freq_map_s,
    freq_map_u,
    pair_sym,
    propagator,
    left_pairs,
    right_pairs,
    lengths,
):
    n_freq, _ = dims
    n_chip = n_freq // 2
    pairs, rows, nf = vertex.shape
    n_groups = -(-pairs * rows // nf)
    n_packed = -(-pairs // n_chip)
    size = pairs // PARTS
    hbm = pl.BlockSpec(memory_space=pltpu.HBM)
    smem = pl.BlockSpec(memory_space=pltpu.SMEM)
    dma = pltpu.SemaphoreType.DMA
    return pl.pallas_call(
        functools.partial(kernel, dims),
        out_shape=jax.ShapeDtypeStruct((pairs, rows, nf), F32),
        in_specs=[hbm] * 8 + [smem] * 2,
        out_specs=pl.BlockSpec(memory_space=pltpu.VMEM),
        scratch_shapes=[
            pltpu.VMEM((pairs, rows, nf), BF16),
            pltpu.VMEM((pairs, rows, nf), BF16),
            pltpu.VMEM((1, nf), jnp.int32),
            pltpu.VMEM((1, nf), jnp.int32),
            pltpu.VMEM((1, nf), F32),
            pltpu.VMEM(left_pairs.shape, jnp.int32),
            pltpu.VMEM(right_pairs.shape, jnp.int32),
            pltpu.VMEM((2, 2, 3 * pairs, rows, nf), BF16),
            pltpu.VMEM((2, n_chip, n_packed, rows, nf), BF16),
            pltpu.VMEM((3, 2, n_chip, n_packed, rows, nf), BF16),
            pltpu.VMEM((2, 1 + 3 * n_packed * n_chip, n_chip, rows, nf), BF16),
            pltpu.VMEM((n_freq, 2, n_groups, rows, nf), BF16),
            pltpu.VMEM((n_freq, 2, n_groups, rows, nf), BF16),
            pltpu.VMEM((2 * nf, nf), BF16),
            pltpu.VMEM((pairs, n_chip, rows, nf), F32),
            pltpu.VMEM((PARTS, n_chip, size, rows, nf), BF16),
            pltpu.VMEM((PARTS, n_chip, size, rows, nf), BF16),
            pltpu.VMEM((pairs, nf), jnp.int32),
            pltpu.SMEM((pairs, nf), jnp.int32),
            dma((2, 2, 3)),
            dma((2, n_chip)),
            dma((2, 3)),
            dma((n_freq,)),
            dma((PARTS, n_chip)),
            dma((48,)),
            dma((9,)),
        ],
        compiler_params=pltpu.CompilerParams(
            collective_id=0, has_side_effects=True, vmem_limit_bytes=63 * 1024 * 1024
        ),
    )(
        vertex,
        jnp.swapaxes(deriv_s, 1, 2),
        jnp.swapaxes(deriv_u, 1, 2),
        freq_map_s.reshape(1, nf),
        freq_map_u.reshape(1, nf),
        propagator.reshape(1, nf),
        left_pairs,
        right_pairs,
        pair_sym,
        lengths,
    )


def solution(mesh):
    dims = (mesh.shape["freq"], mesh.shape["pair"])
    return jax.shard_map(
        functools.partial(per_device, dims),
        mesh=mesh,
        in_specs=(
            P("pair", "freq", None),
            P("pair", None, "freq"),
            P("pair", None, "freq"),
            P(),
            P(),
            P("pair"),
            P(),
            P("pair", None),
            P("pair", None),
            P("pair"),
        ),
        out_specs=P("pair", "freq", None),
        check_vma=False,
    )
```

```python
import functools

import jax
import jax.numpy as jnp
from jax import lax
from jax.experimental import pallas as pl
from jax.experimental.pallas import tpu as pltpu
from jax.sharding import PartitionSpec as P

MESH = pl.DeviceIdType.MESH
BF16 = jnp.bfloat16
F32 = jnp.float32

BEFORE, OWN, AFTER = 0, 1, 2
VERTEX, DERIV = 0, 1
PARTS = 6


def regroup(parts):
    count = len(parts)
    rows, lanes = parts[0].shape
    width = lanes // count
    lane = lax.broadcasted_iota(jnp.int32, (rows, lanes), 1)
    parts = list(parts)
    step = 1
    while step < count:
        high = (lane // (width * step)) % 2 == 1
        for q in range(count):
            if (q // step) % 2 == 0:
                a, b = parts[q], parts[q + step]
                parts[q] = jnp.where(high, pltpu.roll(b, width * step, 1), a)
                parts[q + step] = jnp.where(high, b, pltpu.roll(a, lanes - width * step, 1))
        step *= 2
    return parts


def kernel(
    dims,
    v_in,
    s_in,
    u_in,
    map_s_in,
    map_u_in,
    prop_in,
    left_in,
    right_in,
    sym_ref,
    len_ref,
    out_ref,
    s_ref,
    u_ref,
    map_s_ref,
    map_u_ref,
    prop_ref,
    left_ref,
    right_ref,
    right,
    packed,
    spread,
    lefts,
    chunks,
    columns,
    table,
    sums,
    part_out,
    part_in,
    sel_vec,
    sel,
    recv_right,
    recv_spread,
    recv_beside,
    recv_cols,
    recv_part,
    send_part,
    send,
    local,
):
    n_freq, n_pair = dims
    n_chip = n_freq // 2
    pairs, rows, nf = v_in.shape
    slots = left_ref.shape[1]
    freq, block = lax.axis_index("freq"), lax.axis_index("pair")
    chip, core = freq // 2, freq % 2

    sibling = (freq + 1 - 2 * core, block)
    x_up = (freq, (block + 1) % n_pair)
    x_down = (freq, (block + n_pair - 1) % n_pair)

    def own(kind, slot=OWN, of=core):
        return right.at[kind, of, slot * pairs : (slot + 1) * pairs]

    loads = [
        pltpu.make_async_copy(src, dst, local.at[i])
        for i, (src, dst) in enumerate(
            (
                (v_in, own(VERTEX)),
                (s_in, s_ref),
                (u_in, u_ref),
                (map_s_in, map_s_ref),
                (map_u_in, map_u_ref),
                (prop_in, prop_ref),
                (left_in, left_ref),
                (right_in, right_ref),
            )
        )
    ]
    for load in loads:
        load.start()

    barrier = pltpu.get_barrier_semaphore()
    peers = [((freq + o) % n_freq, block) for o in range(1, n_freq)] + [x_up, x_down]
    for peer in peers:
        pl.semaphore_signal(barrier, inc=1, device_id=peer, device_id_type=MESH)
    pl.semaphore_wait(barrier, len(peers))

    sent = []

    def push(src, dst, recv_sem, peer):
        copy = pltpu.make_async_remote_copy(
            src_ref=src,
            dst_ref=dst,
            send_sem=send.at[len(sent)],
            recv_sem=recv_sem,
            device_id=peer,
            device_id_type=MESH,
        )
        copy.start()
        sent.append(copy)

    def arrive(ref, recv_sem):
        pltpu.make_async_remote_copy(
            src_ref=ref,
            dst_ref=ref,
            send_sem=send.at[0],
            recv_sem=recv_sem,
            device_id=sibling,
            device_id_type=MESH,
        ).wait_recv()

    def push_beside(kind):
        push(own(kind), own(kind, BEFORE), recv_right.at[kind, core, BEFORE], x_up)
        push(own(kind), own(kind, AFTER), recv_right.at[kind, core, AFTER], x_down)

    def push_sibling(kind, slot):
        push(own(kind, slot), own(kind, slot), recv_right.at[kind, core, slot], sibling)

    n_packed = packed.shape[2]
    zero_rows = jnp.zeros((rows, nf), F32)

    def push_left(kind):
        for g in range(n_packed):
            four = [
                right[kind, core, OWN * pairs + p].astype(F32) if p < pairs else zero_rows
                for p in range(n_chip * g, n_chip * (g + 1))
            ]
            for c, tile in enumerate(regroup(four)):
                packed[kind, c, g] = tile.astype(BF16)
        spread[OWN, kind, chip] = packed[kind, chip]
        for o in (2, 1, 3):
            c = (chip + o) % n_chip
            push(
                packed.at[kind, c],
                spread.at[OWN, kind, chip],
                recv_spread.at[kind, chip],
                (2 * c + core, block),
            )

    def pass_left_on(kind):
        for o in (1, 3, 2):
            c = (chip + o) % n_chip
            arrive(spread.at[OWN, kind, c], recv_spread.at[kind, c])
        push(spread.at[OWN, kind], spread.at[BEFORE, kind], recv_beside.at[kind, BEFORE], x_up)
        push(spread.at[OWN, kind], spread.at[AFTER, kind], recv_beside.at[kind, AFTER], x_down)

    loads[0].wait()
    push_beside(VERTEX)
    push_sibling(VERTEX, OWN)
    push_left(VERTEX)

    for load in loads[1:]:
        load.wait()
    group = nf // rows
    n_groups = columns.shape[2]
    for kind in (0, 1):
        for g in range(n_groups):
            eight = []
            for p in range(g * group, (g + 1) * group):
                if p >= pairs:
                    eight.append(zero_rows)
                elif kind == 0:
                    eight.append(s_ref[p].astype(F32))
                else:
                    eight.append(u_ref[lax.rem(sym_ref[p], pairs)].astype(F32))
            for f, tile in enumerate(regroup(eight)):
                chunks[f, kind, g] = tile.astype(BF16)
    columns[freq] = chunks[freq]
    for o in (4, 3, 5, 2, 6, 1, 7):
        f = (freq + o) % n_freq
        push(chunks.at[f], columns.at[freq], recv_cols.at[freq], (f, block))

    wide = lax.broadcasted_iota(jnp.int32, (nf, nf), 0)
    table[0:nf, :] = jnp.where(wide == map_s_ref[...], 1.0, 0.0).astype(BF16)
    table[nf : 2 * nf, :] = jnp.where(wide == map_u_ref[...], 1.0, 0.0).astype(BF16)
    window_first = (block - 1) * pairs
    row_id = lax.broadcasted_iota(jnp.int32, (pairs, slots), 0)
    slot_id = lax.broadcasted_iota(jnp.int32, (pairs, slots), 1)
    count = jnp.zeros((pairs, slots), jnp.int32)
    for r in range(pairs):
        count = jnp.where(row_id == r, len_ref[r], count)
    target = jnp.where(slot_id < count, right_ref[...] - window_first, -1)
    source = left_ref[...] - window_first
    stride = n_chip * n_packed
    gap = stride - pairs
    source = source + 1 + jnp.where(source >= pairs, gap, 0) + jnp.where(source >= 2 * pairs, gap, 0)
    lanes = lax.broadcasted_iota(jnp.int32, (pairs, nf), 1)
    chosen = jnp.zeros((pairs, nf), jnp.int32)
    for k in range(slots):
        chosen = jnp.where(target[:, k : k + 1] == lanes, source[:, k : k + 1], chosen)
    sel_vec[...] = chosen
    to_scalar = pltpu.make_async_copy(sel_vec, sel, local.at[8])
    to_scalar.start()

    width = nf // n_chip
    tile_lane = lax.broadcasted_iota(jnp.int32, (rows, nf), 1)
    wide_prop = jnp.broadcast_to(prop_ref[...], (rows, nf))
    tiles = regroup([wide_prop] * n_chip)
    prop = tiles[0]
    for c in range(1, n_chip):
        prop = jnp.where(chip == c, tiles[c], prop)

    pass_left_on(VERTEX)

    for o in range(1, n_freq):
        f = (freq + o) % n_freq
        arrive(columns.at[f], recv_cols.at[f])
    for g in range(n_groups):
        cols = jnp.concatenate([columns[:, kind, g].reshape(nf, nf) for kind in (0, 1)], axis=0)
        rows_t = lax.dot_general(
            cols, table[...], (((0,), (0,)), ((), ())), preferred_element_type=F32
        ).astype(BF16)
        n = min(group, pairs - g * group)
        start = OWN * pairs + g * group
        right[DERIV, core, start : start + n] = rows_t.reshape(group, rows, nf)[:n]
    push_beside(DERIV)
    push_left(DERIV)
    push_sibling(DERIV, OWN)

    for half in (0, 1):
        lefts[half, 0] = jnp.zeros(lefts.shape[2:], BF16)

    def fill_lefts(slot):
        def one(g, carry):
            for c in range(n_chip):
                turned = []
                for kind in (VERTEX, DERIV):
                    tile = (spread[slot, kind, c, g].astype(F32) * prop).astype(BF16).astype(F32)
                    turned.append(
                        [tile] + [pltpu.roll(tile, width * k, 1) for k in range(1, n_chip)]
                    )
                for q in range(n_chip):
                    for half in (0, 1):
                        lane0 = 2 * half
                        tile = jnp.where(
                            tile_lane // width == lane0,
                            turned[VERTEX][(lane0 - q) % n_chip],
                            jnp.where(
                                tile_lane // width == lane0 + 1,
                                turned[DERIV][(lane0 + 1 - q) % n_chip],
                                0.0,
                            ),
                        )
                        lefts[half, 1 + slot * stride + g * n_chip + q, c] = tile.astype(BF16)
            return carry

        lax.fori_loop(0, n_packed, one, 0)

    for slot in (BEFORE, AFTER):
        arrive(own(VERTEX, slot), recv_right.at[VERTEX, core, slot])
        push_sibling(VERTEX, slot)
    pass_left_on(DERIV)
    fill_lefts(OWN)
    for slot in (BEFORE, AFTER):
        arrive(own(DERIV, slot), recv_right.at[DERIV, core, slot])
        push_sibling(DERIV, slot)
    for slot in (BEFORE, AFTER):
        for kind in (VERTEX, DERIV):
            arrive(spread.at[slot, kind], recv_beside.at[kind, slot])
        fill_lefts(slot)
    other = 1 - core
    for slot in (OWN, BEFORE, AFTER):
        for kind in (VERTEX, DERIV):
            arrive(own(kind, slot, other), recv_right.at[kind, other, slot])

    to_scalar.wait()
    size = pairs // PARTS
    tall = n_chip * rows

    def part_copy(part, o):
        c = (chip + o) % n_chip
        return pltpu.make_async_remote_copy(
            src_ref=part_out.at[part, o],
            dst_ref=part_in.at[part, chip],
            send_sem=send_part.at[part, o],
            recv_sem=recv_part.at[part, chip],
            device_id=(2 * c + core, block),
            device_id_type=MESH,
        )

    def one_part(part, carry):
        first_row = part * size
        lhs, rhs = [], []
        for q in range(0, 3 * pairs, 2):
            lhs.append(
                jnp.concatenate(
                    [
                        (
                            lefts[0, sel[first_row + r, q]] + lefts[1, sel[first_row + r, q + 1]]
                        ).reshape(tall, nf)
                        for r in range(size)
                    ],
                    axis=0,
                )
            )
            for p in (q, q + 1):
                rhs += [right[kind, :, p].reshape(2 * rows, nf) for kind in (DERIV, VERTEX)]
        terms = jnp.dot(
            jnp.concatenate(lhs, axis=1),
            jnp.concatenate(rhs, axis=0),
            preferred_element_type=F32,
        )
        sums[...] = terms.reshape(size, n_chip, rows, nf)
        out_ref[pl.ds(first_row, size)] = sums[:, chip]
        for o in (2, 1, 3):
            part_out[part, o] = sums[:, (chip + o) % n_chip].astype(BF16)
            part_copy(part, o).start()
        return carry

    lax.fori_loop(0, PARTS, one_part, 0)
    for part in range(PARTS):
        at = slice(part * size, (part + 1) * size)
        total = out_ref[at]
        for o in (1, 3, 2):
            c = (chip + o) % n_chip
            arrive(part_in.at[part, c], recv_part.at[part, c])
            total = total + part_in[part, c].astype(F32)
        out_ref[at] = total
    for part in range(PARTS):
        for o in (2, 1, 3):
            part_copy(part, o).wait_send()
    for copy in sent:
        copy.wait_send()


def per_device(
    dims,
    vertex,
    deriv_s,
    deriv_u,
    freq_map_s,
    freq_map_u,
    pair_sym,
    propagator,
    left_pairs,
    right_pairs,
    lengths,
):
    n_freq, _ = dims
    n_chip = n_freq // 2
    pairs, rows, nf = vertex.shape
    n_groups = -(-pairs * rows // nf)
    n_packed = -(-pairs // n_chip)
    size = pairs // PARTS
    hbm = pl.BlockSpec(memory_space=pltpu.HBM)
    smem = pl.BlockSpec(memory_space=pltpu.SMEM)
    dma = pltpu.SemaphoreType.DMA
    return pl.pallas_call(
        functools.partial(kernel, dims),
        out_shape=jax.ShapeDtypeStruct((pairs, rows, nf), F32),
        in_specs=[hbm] * 8 + [smem] * 2,
        out_specs=pl.BlockSpec(memory_space=pltpu.VMEM),
        scratch_shapes=[
            pltpu.VMEM((pairs, rows, nf), BF16),
            pltpu.VMEM((pairs, rows, nf), BF16),
            pltpu.VMEM((1, nf), jnp.int32),
            pltpu.VMEM((1, nf), jnp.int32),
            pltpu.VMEM((1, nf), F32),
            pltpu.VMEM(left_pairs.shape, jnp.int32),
            pltpu.VMEM(right_pairs.shape, jnp.int32),
            pltpu.VMEM((2, 2, 3 * pairs, rows, nf), BF16),
            pltpu.VMEM((2, n_chip, n_packed, rows, nf), BF16),
            pltpu.VMEM((3, 2, n_chip, n_packed, rows, nf), BF16),
            pltpu.VMEM((2, 1 + 3 * n_packed * n_chip, n_chip, rows, nf), BF16),
            pltpu.VMEM((n_freq, 2, n_groups, rows, nf), BF16),
            pltpu.VMEM((n_freq, 2, n_groups, rows, nf), BF16),
            pltpu.VMEM((2 * nf, nf), BF16),
            pltpu.VMEM((size, n_chip, rows, nf), F32),
            pltpu.VMEM((PARTS, n_chip, size, rows, nf), BF16),
            pltpu.VMEM((PARTS, n_chip, size, rows, nf), BF16),
            pltpu.VMEM((pairs, nf), jnp.int32),
            pltpu.SMEM((pairs, nf), jnp.int32),
            dma((2, 2, 3)),
            dma((2, n_chip)),
            dma((2, 3)),
            dma((n_freq,)),
            dma((PARTS, n_chip)),
            dma((PARTS, n_chip)),
            dma((48,)),
            dma((9,)),
        ],
        compiler_params=pltpu.CompilerParams(
            collective_id=0, has_side_effects=True, vmem_limit_bytes=63 * 1024 * 1024
        ),
    )(
        vertex,
        jnp.swapaxes(deriv_s, 1, 2),
        jnp.swapaxes(deriv_u, 1, 2),
        freq_map_s.reshape(1, nf),
        freq_map_u.reshape(1, nf),
        propagator.reshape(1, nf),
        left_pairs,
        right_pairs,
        pair_sym,
        lengths,
    )


def solution(mesh):
    dims = (mesh.shape["freq"], mesh.shape["pair"])
    return jax.shard_map(
        functools.partial(per_device, dims),
        mesh=mesh,
        in_specs=(
            P("pair", "freq", None),
            P("pair", None, "freq"),
            P("pair", None, "freq"),
            P(),
            P(),
            P("pair"),
            P(),
            P("pair", None),
            P("pair", None),
            P("pair"),
        ),
        out_specs=P("pair", "freq", None),
        check_vma=False,
    )
```

```python
import functools

import jax
import jax.numpy as jnp
from jax import lax
from jax.experimental import pallas as pl
from jax.experimental.pallas import tpu as pltpu
from jax.sharding import PartitionSpec as P

MESH = pl.DeviceIdType.MESH
BF16 = jnp.bfloat16
F32 = jnp.float32

BEFORE, OWN, AFTER = 0, 1, 2
VERTEX, DERIV = 0, 1
PARTS = 6


def regroup(parts):
    count = len(parts)
    rows, lanes = parts[0].shape
    width = lanes // count
    lane = lax.broadcasted_iota(jnp.int32, (rows, lanes), 1)
    parts = list(parts)
    step = 1
    while step < count:
        high = (lane & (width * step)) != 0
        for q in range(count):
            if (q // step) % 2 == 0:
                a, b = parts[q], parts[q + step]
                parts[q] = jnp.where(high, pltpu.roll(b, width * step, 1), a)
                parts[q + step] = jnp.where(high, b, pltpu.roll(a, lanes - width * step, 1))
        step *= 2
    return parts


def kernel(
    dims,
    v_in,
    s_in,
    u_in,
    map_s_in,
    map_u_in,
    prop_in,
    left_in,
    right_in,
    sym_ref,
    len_ref,
    out_ref,
    s_ref,
    u_ref,
    map_s_ref,
    map_u_ref,
    prop_ref,
    left_ref,
    right_ref,
    right,
    packed,
    spread,
    lefts,
    chunks,
    columns,
    table,
    sums,
    part_out,
    part_in,
    sel_vec,
    sel,
    recv_right,
    recv_spread,
    recv_beside,
    recv_cols,
    recv_part,
    send_part,
    send,
    local,
):
    n_freq, n_pair = dims
    n_chip = n_freq // 2
    pairs, rows, nf = v_in.shape
    slots = left_ref.shape[1]
    freq, block = lax.axis_index("freq"), lax.axis_index("pair")
    chip, core = freq // 2, freq % 2

    sibling = (freq + 1 - 2 * core, block)
    x_up = (freq, (block + 1) % n_pair)
    x_down = (freq, (block + n_pair - 1) % n_pair)

    def own(kind, slot=OWN, of=core):
        return right.at[kind, of, slot * pairs : (slot + 1) * pairs]

    loads = [
        pltpu.make_async_copy(src, dst, local.at[i])
        for i, (src, dst) in enumerate(
            (
                (v_in, own(VERTEX)),
                (s_in, s_ref),
                (u_in, u_ref),
                (map_s_in, map_s_ref),
                (map_u_in, map_u_ref),
                (prop_in, prop_ref),
                (left_in, left_ref),
                (right_in, right_ref),
            )
        )
    ]
    for load in loads:
        load.start()

    barrier = pltpu.get_barrier_semaphore()
    peers = [((freq + o) % n_freq, block) for o in range(1, n_freq)] + [x_up, x_down]
    for peer in peers:
        pl.semaphore_signal(barrier, inc=1, device_id=peer, device_id_type=MESH)
    pl.semaphore_wait(barrier, len(peers))

    sent = []

    def push(src, dst, recv_sem, peer):
        copy = pltpu.make_async_remote_copy(
            src_ref=src,
            dst_ref=dst,
            send_sem=send.at[len(sent)],
            recv_sem=recv_sem,
            device_id=peer,
            device_id_type=MESH,
        )
        copy.start()
        sent.append(copy)

    def arrive(ref, recv_sem):
        pltpu.make_async_remote_copy(
            src_ref=ref,
            dst_ref=ref,
            send_sem=send.at[0],
            recv_sem=recv_sem,
            device_id=sibling,
            device_id_type=MESH,
        ).wait_recv()

    def push_beside(kind):
        push(own(kind), own(kind, BEFORE), recv_right.at[kind, core, BEFORE], x_up)
        push(own(kind), own(kind, AFTER), recv_right.at[kind, core, AFTER], x_down)

    def push_sibling(kind, slot):
        push(own(kind, slot), own(kind, slot), recv_right.at[kind, core, slot], sibling)

    n_packed = packed.shape[2]
    zero_rows = jnp.zeros((rows, nf), BF16)

    def push_left(kind):
        for g in range(n_packed):
            four = [
                right[kind, core, OWN * pairs + p] if p < pairs else zero_rows
                for p in range(n_chip * g, n_chip * (g + 1))
            ]
            for c, tile in enumerate(regroup(four)):
                packed[kind, c, g] = tile
        spread[OWN, kind, chip] = packed[kind, chip]
        for o in (2, 1, 3):
            c = (chip + o) % n_chip
            push(
                packed.at[kind, c],
                spread.at[OWN, kind, chip],
                recv_spread.at[kind, chip],
                (2 * c + core, block),
            )

    def pass_left_on(kind):
        for o in (1, 3, 2):
            c = (chip + o) % n_chip
            arrive(spread.at[OWN, kind, c], recv_spread.at[kind, c])
        push(spread.at[OWN, kind], spread.at[BEFORE, kind], recv_beside.at[kind, BEFORE], x_up)
        push(spread.at[OWN, kind], spread.at[AFTER, kind], recv_beside.at[kind, AFTER], x_down)

    loads[0].wait()
    push_beside(VERTEX)
    push_sibling(VERTEX, OWN)
    push_left(VERTEX)

    for load in loads[1:]:
        load.wait()
    group = nf // rows
    n_groups = columns.shape[2]
    for kind in (0, 1):
        for g in range(n_groups):
            eight = []
            for p in range(g * group, (g + 1) * group):
                if p >= pairs:
                    eight.append(zero_rows)
                elif kind == 0:
                    eight.append(s_ref[p])
                else:
                    eight.append(u_ref[lax.rem(sym_ref[p], pairs)])
            for f, tile in enumerate(regroup(eight)):
                chunks[f, kind, g] = tile
    columns[freq] = chunks[freq]
    for o in (4, 3, 5, 2, 6, 1, 7):
        f = (freq + o) % n_freq
        push(chunks.at[f], columns.at[freq], recv_cols.at[freq], (f, block))

    wide = lax.broadcasted_iota(jnp.int32, (nf, nf), 0)
    table[0:nf, :] = jnp.where(wide == map_s_ref[...], 1.0, 0.0).astype(BF16)
    table[nf : 2 * nf, :] = jnp.where(wide == map_u_ref[...], 1.0, 0.0).astype(BF16)
    window_first = (block - 1) * pairs
    row_id = lax.broadcasted_iota(jnp.int32, (pairs, slots), 0)
    slot_id = lax.broadcasted_iota(jnp.int32, (pairs, slots), 1)
    count = jnp.zeros((pairs, slots), jnp.int32)
    for r in range(pairs):
        count = jnp.where(row_id == r, len_ref[r], count)
    target = jnp.where(slot_id < count, right_ref[...] - window_first, -1)
    source = left_ref[...] - window_first
    stride = n_chip * n_packed
    gap = stride - pairs
    source = source + 1 + jnp.where(source >= pairs, gap, 0) + jnp.where(source >= 2 * pairs, gap, 0)
    lanes = lax.broadcasted_iota(jnp.int32, (pairs, nf), 1)
    chosen = jnp.zeros((pairs, nf), jnp.int32)
    for k in range(slots):
        chosen = jnp.where(target[:, k : k + 1] == lanes, source[:, k : k + 1], chosen)
    sel_vec[...] = chosen
    to_scalar = pltpu.make_async_copy(sel_vec, sel, local.at[8])
    to_scalar.start()

    width = nf // n_chip
    tile_lane = lax.broadcasted_iota(jnp.int32, (rows, nf), 1)
    wide_prop = jnp.broadcast_to(prop_ref[...], (rows, nf))
    tiles = regroup([wide_prop] * n_chip)
    prop = tiles[0]
    for c in range(1, n_chip):
        prop = jnp.where(chip == c, tiles[c], prop)

    for half in (0, 1):
        lefts[half, 0] = jnp.zeros(lefts.shape[2:], BF16)
    zones = [
        (tile_lane >= width * z) & (tile_lane < width * (z + 1)) for z in range(n_chip)
    ]

    def fill_lefts(kind, slot):
        def one(g, carry):
            for c in range(n_chip):
                tile = (spread[slot, kind, c, g].astype(F32) * prop).astype(BF16)
                turned = [tile] + [pltpu.roll(tile, width * k, 1) for k in range(1, n_chip)]
                for q in range(n_chip):
                    at = 1 + slot * stride + g * n_chip + q
                    for half in (0, 1):
                        zone = 2 * half + kind
                        rest = jnp.zeros((rows, nf), BF16) if kind == VERTEX else lefts[half, at, c]
                        lefts[half, at, c] = jnp.where(zones[zone], turned[(zone - q) % n_chip], rest)
            return carry

        lax.fori_loop(0, n_packed, one, 0)

    pass_left_on(VERTEX)

    for o in range(1, n_freq):
        f = (freq + o) % n_freq
        arrive(columns.at[f], recv_cols.at[f])
    for g in range(n_groups):
        cols = jnp.concatenate([columns[:, kind, g].reshape(nf, nf) for kind in (0, 1)], axis=0)
        rows_t = lax.dot_general(
            cols, table[...], (((0,), (0,)), ((), ())), preferred_element_type=F32
        ).astype(BF16)
        n = min(group, pairs - g * group)
        start = OWN * pairs + g * group
        right[DERIV, core, start : start + n] = rows_t.reshape(group, rows, nf)[:n]
    push_beside(DERIV)
    push_left(DERIV)
    push_sibling(DERIV, OWN)

    for slot in (BEFORE, AFTER):
        arrive(own(VERTEX, slot), recv_right.at[VERTEX, core, slot])
        push_sibling(VERTEX, slot)
    fill_lefts(VERTEX, OWN)
    for slot in (BEFORE, AFTER):
        arrive(spread.at[slot, VERTEX], recv_beside.at[VERTEX, slot])
        fill_lefts(VERTEX, slot)

    pass_left_on(DERIV)
    fill_lefts(DERIV, OWN)
    for slot in (BEFORE, AFTER):
        arrive(own(DERIV, slot), recv_right.at[DERIV, core, slot])
        push_sibling(DERIV, slot)
    for slot in (BEFORE, AFTER):
        arrive(spread.at[slot, DERIV], recv_beside.at[DERIV, slot])
        fill_lefts(DERIV, slot)
    other = 1 - core
    for slot in (OWN, BEFORE, AFTER):
        for kind in (VERTEX, DERIV):
            arrive(own(kind, slot, other), recv_right.at[kind, other, slot])

    to_scalar.wait()
    size = pairs // PARTS
    tall = n_chip * rows

    def part_copy(part, o):
        c = (chip + o) % n_chip
        return pltpu.make_async_remote_copy(
            src_ref=part_out.at[part, o],
            dst_ref=part_in.at[part, chip],
            send_sem=send_part.at[part, o],
            recv_sem=recv_part.at[part, chip],
            device_id=(2 * c + core, block),
            device_id_type=MESH,
        )

    def one_part(part, carry):
        first_row = part * size
        lhs, rhs = [], []
        for q in range(0, 3 * pairs, 2):
            lhs.append(
                jnp.concatenate(
                    [
                        (
                            lefts[0, sel[first_row + r, q]] + lefts[1, sel[first_row + r, q + 1]]
                        ).reshape(tall, nf)
                        for r in range(size)
                    ],
                    axis=0,
                )
            )
            for p in (q, q + 1):
                rhs += [right[kind, :, p].reshape(2 * rows, nf) for kind in (DERIV, VERTEX)]
        terms = jnp.dot(
            jnp.concatenate(lhs, axis=1),
            jnp.concatenate(rhs, axis=0),
            preferred_element_type=F32,
        )
        sums[...] = terms.reshape(size, n_chip, rows, nf)
        out_ref[pl.ds(first_row, size)] = sums[:, chip]
        for o in (2, 1, 3):
            part_out[part, o] = sums[:, (chip + o) % n_chip].astype(BF16)
            part_copy(part, o).start()
        return carry

    lax.fori_loop(0, PARTS, one_part, 0)
    for part in range(PARTS):
        at = slice(part * size, (part + 1) * size)
        total = out_ref[at]
        for o in (1, 3, 2):
            c = (chip + o) % n_chip
            arrive(part_in.at[part, c], recv_part.at[part, c])
            total = total + part_in[part, c].astype(F32)
        out_ref[at] = total
    for part in range(PARTS):
        for o in (2, 1, 3):
            part_copy(part, o).wait_send()
    for copy in sent:
        copy.wait_send()


def per_device(
    dims,
    vertex,
    deriv_s,
    deriv_u,
    freq_map_s,
    freq_map_u,
    pair_sym,
    propagator,
    left_pairs,
    right_pairs,
    lengths,
):
    n_freq, _ = dims
    n_chip = n_freq // 2
    pairs, rows, nf = vertex.shape
    n_groups = -(-pairs * rows // nf)
    n_packed = -(-pairs // n_chip)
    size = pairs // PARTS
    hbm = pl.BlockSpec(memory_space=pltpu.HBM)
    smem = pl.BlockSpec(memory_space=pltpu.SMEM)
    dma = pltpu.SemaphoreType.DMA
    return pl.pallas_call(
        functools.partial(kernel, dims),
        out_shape=jax.ShapeDtypeStruct((pairs, rows, nf), F32),
        in_specs=[hbm] * 8 + [smem] * 2,
        out_specs=pl.BlockSpec(memory_space=pltpu.VMEM),
        scratch_shapes=[
            pltpu.VMEM((pairs, rows, nf), BF16),
            pltpu.VMEM((pairs, rows, nf), BF16),
            pltpu.VMEM((1, nf), jnp.int32),
            pltpu.VMEM((1, nf), jnp.int32),
            pltpu.VMEM((1, nf), F32),
            pltpu.VMEM(left_pairs.shape, jnp.int32),
            pltpu.VMEM(right_pairs.shape, jnp.int32),
            pltpu.VMEM((2, 2, 3 * pairs, rows, nf), BF16),
            pltpu.VMEM((2, n_chip, n_packed, rows, nf), BF16),
            pltpu.VMEM((3, 2, n_chip, n_packed, rows, nf), BF16),
            pltpu.VMEM((2, 1 + 3 * n_packed * n_chip, n_chip, rows, nf), BF16),
            pltpu.VMEM((n_freq, 2, n_groups, rows, nf), BF16),
            pltpu.VMEM((n_freq, 2, n_groups, rows, nf), BF16),
            pltpu.VMEM((2 * nf, nf), BF16),
            pltpu.VMEM((size, n_chip, rows, nf), F32),
            pltpu.VMEM((PARTS, n_chip, size, rows, nf), BF16),
            pltpu.VMEM((PARTS, n_chip, size, rows, nf), BF16),
            pltpu.VMEM((pairs, nf), jnp.int32),
            pltpu.SMEM((pairs, nf), jnp.int32),
            dma((2, 2, 3)),
            dma((2, n_chip)),
            dma((2, 3)),
            dma((n_freq,)),
            dma((PARTS, n_chip)),
            dma((PARTS, n_chip)),
            dma((48,)),
            dma((9,)),
        ],
        compiler_params=pltpu.CompilerParams(
            collective_id=0, has_side_effects=True, vmem_limit_bytes=63 * 1024 * 1024
        ),
    )(
        vertex,
        jnp.swapaxes(deriv_s, 1, 2),
        jnp.swapaxes(deriv_u, 1, 2),
        freq_map_s.reshape(1, nf),
        freq_map_u.reshape(1, nf),
        propagator.reshape(1, nf),
        left_pairs,
        right_pairs,
        pair_sym,
        lengths,
    )


def solution(mesh):
    dims = (mesh.shape["freq"], mesh.shape["pair"])
    return jax.shard_map(
        functools.partial(per_device, dims),
        mesh=mesh,
        in_specs=(
            P("pair", "freq", None),
            P("pair", None, "freq"),
            P("pair", None, "freq"),
            P(),
            P(),
            P("pair"),
            P(),
            P("pair", None),
            P("pair", None),
            P("pair"),
        ),
        out_specs=P("pair", "freq", None),
        check_vma=False,
    )
```

```python
import functools

import jax
import jax.numpy as jnp
from jax import lax
from jax.experimental import pallas as pl
from jax.experimental.pallas import tpu as pltpu
from jax.sharding import PartitionSpec as P

MESH = pl.DeviceIdType.MESH
BF16 = jnp.bfloat16
F32 = jnp.float32

BEFORE, OWN, AFTER = 0, 1, 2
VERTEX, DERIV = 0, 1
PARTS = 6


def regroup(parts):
    count = len(parts)
    rows, lanes = parts[0].shape
    width = lanes // count
    lane = lax.broadcasted_iota(jnp.int32, (rows, lanes), 1)
    parts = list(parts)
    step = 1
    while step < count:
        high = (lane & (width * step)) != 0
        for q in range(count):
            if (q // step) % 2 == 0:
                a, b = parts[q], parts[q + step]
                parts[q] = jnp.where(high, pltpu.roll(b, width * step, 1), a)
                parts[q + step] = jnp.where(high, b, pltpu.roll(a, lanes - width * step, 1))
        step *= 2
    return parts


def kernel(
    dims,
    v_in,
    s_in,
    u_in,
    map_s_in,
    map_u_in,
    prop_in,
    left_in,
    right_in,
    sym_ref,
    len_ref,
    out_ref,
    s_ref,
    u_ref,
    map_s_ref,
    map_u_ref,
    prop_ref,
    left_ref,
    right_ref,
    right,
    packed,
    spread,
    lefts,
    chunks,
    columns,
    table,
    sums,
    part_out,
    part_in,
    sel_vec,
    sel,
    recv_right,
    recv_spread,
    recv_beside,
    recv_cols,
    recv_part,
    send_part,
    send,
    local,
):
    n_freq, n_pair = dims
    n_chip = n_freq // 2
    pairs, rows, nf = v_in.shape
    slots = left_ref.shape[1]
    freq, block = lax.axis_index("freq"), lax.axis_index("pair")
    chip, core = freq // 2, freq % 2

    sibling = (freq + 1 - 2 * core, block)
    x_up = (freq, (block + 1) % n_pair)
    x_down = (freq, (block + n_pair - 1) % n_pair)

    def own(kind, slot=OWN, of=core):
        return right.at[kind, of, slot * pairs : (slot + 1) * pairs]

    loads = [
        pltpu.make_async_copy(src, dst, local.at[i])
        for i, (src, dst) in enumerate(
            (
                (v_in, own(VERTEX)),
                (s_in, s_ref),
                (u_in, u_ref),
                (map_s_in, map_s_ref),
                (map_u_in, map_u_ref),
                (prop_in, prop_ref),
                (left_in, left_ref),
                (right_in, right_ref),
            )
        )
    ]
    for load in loads:
        load.start()

    barrier = pltpu.get_barrier_semaphore()
    peers = [((freq + o) % n_freq, block) for o in range(1, n_freq)] + [x_up, x_down]
    for peer in peers:
        pl.semaphore_signal(barrier, inc=1, device_id=peer, device_id_type=MESH)
    pl.semaphore_wait(barrier, len(peers))

    sent = []

    def push(src, dst, recv_sem, peer):
        copy = pltpu.make_async_remote_copy(
            src_ref=src,
            dst_ref=dst,
            send_sem=send.at[len(sent)],
            recv_sem=recv_sem,
            device_id=peer,
            device_id_type=MESH,
        )
        copy.start()
        sent.append(copy)

    def arrive(ref, recv_sem):
        pltpu.make_async_remote_copy(
            src_ref=ref,
            dst_ref=ref,
            send_sem=send.at[0],
            recv_sem=recv_sem,
            device_id=sibling,
            device_id_type=MESH,
        ).wait_recv()

    def push_beside(kind):
        push(own(kind), own(kind, BEFORE), recv_right.at[kind, core, BEFORE], x_up)
        push(own(kind), own(kind, AFTER), recv_right.at[kind, core, AFTER], x_down)

    def push_sibling(kind, slot):
        push(own(kind, slot), own(kind, slot), recv_right.at[kind, core, slot], sibling)

    n_packed = packed.shape[2]
    zero_rows = jnp.zeros((rows, nf), BF16)

    def push_left(kind):
        for g in range(n_packed):
            four = [
                right[kind, core, OWN * pairs + p] if p < pairs else zero_rows
                for p in range(n_chip * g, n_chip * (g + 1))
            ]
            for c, tile in enumerate(regroup(four)):
                packed[kind, c, g] = tile
        spread[OWN, kind, chip] = packed[kind, chip]
        for o in (2, 1, 3):
            c = (chip + o) % n_chip
            push(
                packed.at[kind, c],
                spread.at[OWN, kind, chip],
                recv_spread.at[kind, chip],
                (2 * c + core, block),
            )

    def pass_left_on(kind):
        for o in (1, 3, 2):
            c = (chip + o) % n_chip
            arrive(spread.at[OWN, kind, c], recv_spread.at[kind, c])
        push(spread.at[OWN, kind], spread.at[BEFORE, kind], recv_beside.at[kind, BEFORE], x_up)
        push(spread.at[OWN, kind], spread.at[AFTER, kind], recv_beside.at[kind, AFTER], x_down)

    loads[0].wait()
    push_beside(VERTEX)
    push_sibling(VERTEX, OWN)
    push_left(VERTEX)

    for load in loads[1:]:
        load.wait()
    group = nf // rows
    n_groups = columns.shape[2]
    for kind in (0, 1):
        for g in range(n_groups):
            eight = []
            for p in range(g * group, (g + 1) * group):
                if p >= pairs:
                    eight.append(zero_rows)
                elif kind == 0:
                    eight.append(s_ref[p])
                else:
                    eight.append(u_ref[lax.rem(sym_ref[p], pairs)])
            for f, tile in enumerate(regroup(eight)):
                chunks[f, kind, g] = tile
    columns[freq] = chunks[freq]
    for o in (4, 3, 5, 2, 6, 1, 7):
        f = (freq + o) % n_freq
        push(chunks.at[f], columns.at[freq], recv_cols.at[freq], (f, block))

    wide = lax.broadcasted_iota(jnp.int32, (nf, nf), 0)
    table[0:nf, :] = jnp.where(wide == map_s_ref[...], 1.0, 0.0).astype(BF16)
    table[nf : 2 * nf, :] = jnp.where(wide == map_u_ref[...], 1.0, 0.0).astype(BF16)
    window_first = (block - 1) * pairs
    row_id = lax.broadcasted_iota(jnp.int32, (pairs, slots), 0)
    slot_id = lax.broadcasted_iota(jnp.int32, (pairs, slots), 1)
    count = jnp.zeros((pairs, slots), jnp.int32)
    for r in range(pairs):
        count = jnp.where(row_id == r, len_ref[r], count)
    target = jnp.where(slot_id < count, right_ref[...] - window_first, -1)
    source = left_ref[...] - window_first
    gap = n_chip * n_packed - pairs
    source = source + jnp.where(source >= pairs, gap, 0) + jnp.where(source >= 2 * pairs, gap, 0)
    lanes = lax.broadcasted_iota(jnp.int32, (pairs, nf), 1)
    chosen = jnp.full((pairs, nf), -1, jnp.int32)
    for k in range(slots):
        chosen = jnp.where(target[:, k : k + 1] == lanes, source[:, k : k + 1], chosen)
    turn = (lanes - chosen) & (n_chip - 1)
    tile_id = 1 + turn * (3 * n_packed) + (chosen >> (n_chip.bit_length() - 1))
    sel_vec[...] = jnp.where(chosen < 0, 0, tile_id)
    to_scalar = pltpu.make_async_copy(sel_vec, sel, local.at[8])
    to_scalar.start()

    width = nf // n_chip
    tile_lane = lax.broadcasted_iota(jnp.int32, (rows, nf), 1)
    wide_prop = jnp.broadcast_to(prop_ref[...], (rows, nf))
    tiles = regroup([wide_prop] * n_chip)
    prop = tiles[0]
    for c in range(1, n_chip):
        prop = jnp.where(chip == c, tiles[c], prop)

    for kind in (VERTEX, DERIV):
        lefts[kind, 0] = jnp.zeros(lefts.shape[2:], BF16)

    def fill_lefts(kind, slot):
        def one(g, carry):
            for c in range(n_chip):
                tile = (spread[slot, kind, c, g].astype(F32) * prop).astype(BF16)
                at = 1 + slot * n_packed + g
                lefts[kind, at, c] = tile
                for k in range(1, n_chip):
                    lefts[kind, at + k * (3 * n_packed), c] = pltpu.roll(tile, width * k, 1)
            return carry

        lax.fori_loop(0, n_packed, one, 0)

    pass_left_on(VERTEX)

    for o in range(1, n_freq):
        f = (freq + o) % n_freq
        arrive(columns.at[f], recv_cols.at[f])
    for g in range(n_groups):
        cols = jnp.concatenate([columns[:, kind, g].reshape(nf, nf) for kind in (0, 1)], axis=0)
        rows_t = lax.dot_general(
            cols, table[...], (((0,), (0,)), ((), ())), preferred_element_type=F32
        ).astype(BF16)
        n = min(group, pairs - g * group)
        start = OWN * pairs + g * group
        right[DERIV, core, start : start + n] = rows_t.reshape(group, rows, nf)[:n]
    push_beside(DERIV)
    push_left(DERIV)
    push_sibling(DERIV, OWN)

    for slot in (BEFORE, AFTER):
        arrive(own(VERTEX, slot), recv_right.at[VERTEX, core, slot])
        push_sibling(VERTEX, slot)
    fill_lefts(VERTEX, OWN)
    for slot in (BEFORE, AFTER):
        arrive(spread.at[slot, VERTEX], recv_beside.at[VERTEX, slot])
        fill_lefts(VERTEX, slot)

    pass_left_on(DERIV)
    fill_lefts(DERIV, OWN)
    for slot in (BEFORE, AFTER):
        arrive(own(DERIV, slot), recv_right.at[DERIV, core, slot])
        push_sibling(DERIV, slot)
    other = 1 - core
    for slot in (OWN, BEFORE, AFTER):
        for kind in (VERTEX, DERIV):
            arrive(own(kind, slot, other), recv_right.at[kind, other, slot])

    to_scalar.wait()
    size = pairs // PARTS
    tall = n_chip * rows

    def part_copy(part, o):
        c = (chip + o) % n_chip
        return pltpu.make_async_remote_copy(
            src_ref=part_out.at[part, o],
            dst_ref=part_in.at[part, chip],
            send_sem=send_part.at[part, o],
            recv_sem=recv_part.at[part, chip],
            device_id=(2 * c + core, block),
            device_id_type=MESH,
        )

    tile_lanes = lax.broadcasted_iota(jnp.int32, (n_chip, rows, nf), 2)
    upper = tile_lanes >= 2 * width
    odd = (tile_lanes & width) != 0

    def terms_of(kind, first_row):
        def factor(r, q):
            return lefts[kind, sel[first_row + r, q]]

        lhs, rhs = [], []
        for q in range(0, 3 * pairs, n_chip):
            tiles = []
            for r in range(size):
                tile = jnp.where(odd, factor(r, q + 1), factor(r, q))
                if q + 2 < 3 * pairs:
                    high = jnp.where(odd, factor(r, q + 3), factor(r, q + 2))
                else:
                    high = jnp.zeros((n_chip, rows, nf), BF16)
                tiles.append(jnp.where(upper, high, tile).reshape(tall, nf))
            lhs.append(jnp.concatenate(tiles, axis=0))
            for p in range(q, q + n_chip):
                at = p if p < 3 * pairs else p - 2
                rhs.append(right[1 - kind, :, at].reshape(2 * rows, nf))
        terms = jnp.dot(
            jnp.concatenate(lhs, axis=1),
            jnp.concatenate(rhs, axis=0),
            preferred_element_type=F32,
        )
        return terms.reshape(size, n_chip, rows, nf)

    def vertex_part(part, carry):
        sums[pl.ds(part * size, size)] = terms_of(VERTEX, part * size)
        return carry

    def deriv_part(part, carry):
        here = pl.ds(part * size, size)
        sums[here] += terms_of(DERIV, part * size)
        out_ref[here] = sums[here, chip]
        for o in (2, 1, 3):
            part_out[part, o] = sums[here, (chip + o) % n_chip].astype(BF16)
            part_copy(part, o).start()
        return carry

    lax.fori_loop(0, PARTS, vertex_part, 0)
    for slot in (BEFORE, AFTER):
        arrive(spread.at[slot, DERIV], recv_beside.at[DERIV, slot])
        fill_lefts(DERIV, slot)
    lax.fori_loop(0, PARTS, deriv_part, 0)
    for part in range(PARTS):
        at = slice(part * size, (part + 1) * size)
        total = out_ref[at]
        for o in (1, 3, 2):
            c = (chip + o) % n_chip
            arrive(part_in.at[part, c], recv_part.at[part, c])
            total = total + part_in[part, c].astype(F32)
        out_ref[at] = total
    for part in range(PARTS):
        for o in (2, 1, 3):
            part_copy(part, o).wait_send()
    for copy in sent:
        copy.wait_send()


def per_device(
    dims,
    vertex,
    deriv_s,
    deriv_u,
    freq_map_s,
    freq_map_u,
    pair_sym,
    propagator,
    left_pairs,
    right_pairs,
    lengths,
):
    n_freq, _ = dims
    n_chip = n_freq // 2
    pairs, rows, nf = vertex.shape
    n_groups = -(-pairs * rows // nf)
    n_packed = -(-pairs // n_chip)
    size = pairs // PARTS
    hbm = pl.BlockSpec(memory_space=pltpu.HBM)
    smem = pl.BlockSpec(memory_space=pltpu.SMEM)
    dma = pltpu.SemaphoreType.DMA
    return pl.pallas_call(
        functools.partial(kernel, dims),
        out_shape=jax.ShapeDtypeStruct((pairs, rows, nf), F32),
        in_specs=[hbm] * 8 + [smem] * 2,
        out_specs=pl.BlockSpec(memory_space=pltpu.VMEM),
        scratch_shapes=[
            pltpu.VMEM((pairs, rows, nf), BF16),
            pltpu.VMEM((pairs, rows, nf), BF16),
            pltpu.VMEM((1, nf), jnp.int32),
            pltpu.VMEM((1, nf), jnp.int32),
            pltpu.VMEM((1, nf), F32),
            pltpu.VMEM(left_pairs.shape, jnp.int32),
            pltpu.VMEM(right_pairs.shape, jnp.int32),
            pltpu.VMEM((2, 2, 3 * pairs, rows, nf), BF16),
            pltpu.VMEM((2, n_chip, n_packed, rows, nf), BF16),
            pltpu.VMEM((3, 2, n_chip, n_packed, rows, nf), BF16),
            pltpu.VMEM((2, 1 + n_chip * 3 * n_packed, n_chip, rows, nf), BF16),
            pltpu.VMEM((n_freq, 2, n_groups, rows, nf), BF16),
            pltpu.VMEM((n_freq, 2, n_groups, rows, nf), BF16),
            pltpu.VMEM((2 * nf, nf), BF16),
            pltpu.VMEM((pairs, n_chip, rows, nf), F32),
            pltpu.VMEM((PARTS, n_chip, size, rows, nf), BF16),
            pltpu.VMEM((PARTS, n_chip, size, rows, nf), BF16),
            pltpu.VMEM((pairs, nf), jnp.int32),
            pltpu.SMEM((pairs, nf), jnp.int32),
            dma((2, 2, 3)),
            dma((2, n_chip)),
            dma((2, 3)),
            dma((n_freq,)),
            dma((PARTS, n_chip)),
            dma((PARTS, n_chip)),
            dma((48,)),
            dma((9,)),
        ],
        compiler_params=pltpu.CompilerParams(
            collective_id=0, has_side_effects=True, vmem_limit_bytes=63 * 1024 * 1024
        ),
    )(
        vertex,
        jnp.swapaxes(deriv_s, 1, 2),
        jnp.swapaxes(deriv_u, 1, 2),
        freq_map_s.reshape(1, nf),
        freq_map_u.reshape(1, nf),
        propagator.reshape(1, nf),
        left_pairs,
        right_pairs,
        pair_sym,
        lengths,
    )


def solution(mesh):
    dims = (mesh.shape["freq"], mesh.shape["pair"])
    return jax.shard_map(
        functools.partial(per_device, dims),
        mesh=mesh,
        in_specs=(
            P("pair", "freq", None),
            P("pair", None, "freq"),
            P("pair", None, "freq"),
            P(),
            P(),
            P("pair"),
            P(),
            P("pair", None),
            P("pair", None),
            P("pair"),
        ),
        out_specs=P("pair", "freq", None),
        check_vma=False,
    )
```

```python
import functools

import jax
import jax.numpy as jnp
from jax import lax
from jax.experimental import pallas as pl
from jax.experimental.pallas import tpu as pltpu
from jax.sharding import PartitionSpec as P

MESH = pl.DeviceIdType.MESH
BF16 = jnp.bfloat16
F32 = jnp.float32

BEFORE, OWN, AFTER = 0, 1, 2
VERTEX, DERIV = 0, 1
PARTS = 6
CHAIN = 12


def regroup(parts):
    count = len(parts)
    rows, lanes = parts[0].shape
    width = lanes // count
    lane = lax.broadcasted_iota(jnp.int32, (rows, lanes), 1)
    parts = list(parts)
    step = 1
    while step < count:
        high = (lane & (width * step)) != 0
        for q in range(count):
            if (q // step) % 2 == 0:
                a, b = parts[q], parts[q + step]
                parts[q] = jnp.where(high, pltpu.roll(b, width * step, 1), a)
                parts[q + step] = jnp.where(high, b, pltpu.roll(a, lanes - width * step, 1))
        step *= 2
    return parts


def kernel(
    dims,
    v_in,
    s_in,
    u_in,
    map_s_in,
    map_u_in,
    prop_in,
    left_in,
    right_in,
    sym_ref,
    len_ref,
    out_ref,
    s_ref,
    u_ref,
    map_s_ref,
    map_u_ref,
    prop_ref,
    left_ref,
    right_ref,
    right,
    packed,
    spread,
    lefts,
    chunks,
    columns,
    table,
    sums,
    part_out,
    part_in,
    sel_vec,
    sel,
    recv_right,
    recv_spread,
    recv_beside,
    recv_cols,
    recv_part,
    send_part,
    send,
    local,
):
    n_freq, n_pair = dims
    n_chip = n_freq // 2
    pairs, rows, nf = v_in.shape
    slots = left_ref.shape[1]
    freq, block = lax.axis_index("freq"), lax.axis_index("pair")
    chip, core = freq // 2, freq % 2

    sibling = (freq + 1 - 2 * core, block)
    x_up = (freq, (block + 1) % n_pair)
    x_down = (freq, (block + n_pair - 1) % n_pair)

    def own(kind, slot=OWN, of=core):
        return right.at[kind, of, slot * pairs : (slot + 1) * pairs]

    loads = [
        pltpu.make_async_copy(src, dst, local.at[i])
        for i, (src, dst) in enumerate(
            (
                (v_in, own(VERTEX)),
                (s_in, s_ref),
                (u_in, u_ref),
                (map_s_in, map_s_ref),
                (map_u_in, map_u_ref),
                (prop_in, prop_ref),
                (left_in, left_ref),
                (right_in, right_ref),
            )
        )
    ]
    for load in loads:
        load.start()

    barrier = pltpu.get_barrier_semaphore()
    peers = [((freq + o) % n_freq, block) for o in range(1, n_freq)] + [x_up, x_down]
    for peer in peers:
        pl.semaphore_signal(barrier, inc=1, device_id=peer, device_id_type=MESH)
    pl.semaphore_wait(barrier, len(peers))

    sent = []

    def push(src, dst, recv_sem, peer):
        copy = pltpu.make_async_remote_copy(
            src_ref=src,
            dst_ref=dst,
            send_sem=send.at[len(sent)],
            recv_sem=recv_sem,
            device_id=peer,
            device_id_type=MESH,
        )
        copy.start()
        sent.append(copy)

    def arrive(ref, recv_sem):
        pltpu.make_async_remote_copy(
            src_ref=ref,
            dst_ref=ref,
            send_sem=send.at[0],
            recv_sem=recv_sem,
            device_id=sibling,
            device_id_type=MESH,
        ).wait_recv()

    def push_beside(kind):
        push(own(kind), own(kind, BEFORE), recv_right.at[kind, core, BEFORE], x_up)
        push(own(kind), own(kind, AFTER), recv_right.at[kind, core, AFTER], x_down)

    def push_sibling(kind, slot):
        push(own(kind, slot), own(kind, slot), recv_right.at[kind, core, slot], sibling)

    n_packed = packed.shape[2]
    zero_rows = jnp.zeros((rows, nf), BF16)

    def push_left(kind):
        for g in range(n_packed):
            four = [
                right[kind, core, OWN * pairs + p] if p < pairs else zero_rows
                for p in range(n_chip * g, n_chip * (g + 1))
            ]
            for c, tile in enumerate(regroup(four)):
                packed[kind, c, g] = tile
        spread[OWN, kind, chip] = packed[kind, chip]
        for o in (2, 1, 3):
            c = (chip + o) % n_chip
            push(
                packed.at[kind, c],
                spread.at[OWN, kind, chip],
                recv_spread.at[kind, chip],
                (2 * c + core, block),
            )

    def pass_left_on(kind):
        for o in (1, 3, 2):
            c = (chip + o) % n_chip
            arrive(spread.at[OWN, kind, c], recv_spread.at[kind, c])
        push(spread.at[OWN, kind], spread.at[BEFORE, kind], recv_beside.at[kind, BEFORE], x_up)
        push(spread.at[OWN, kind], spread.at[AFTER, kind], recv_beside.at[kind, AFTER], x_down)

    loads[0].wait()
    push_beside(VERTEX)
    push_sibling(VERTEX, OWN)
    push_left(VERTEX)

    for load in loads[1:]:
        load.wait()
    group = nf // rows
    n_groups = columns.shape[2]
    for kind in (0, 1):
        for g in range(n_groups):
            eight = []
            for p in range(g * group, (g + 1) * group):
                if p >= pairs:
                    eight.append(zero_rows)
                elif kind == 0:
                    eight.append(s_ref[p])
                else:
                    eight.append(u_ref[lax.rem(sym_ref[p], pairs)])
            for f, tile in enumerate(regroup(eight)):
                chunks[f, kind, g] = tile
    columns[freq] = chunks[freq]
    for o in (4, 3, 5, 2, 6, 1, 7):
        f = (freq + o) % n_freq
        push(chunks.at[f], columns.at[freq], recv_cols.at[freq], (f, block))

    wide = lax.broadcasted_iota(jnp.int32, (nf, nf), 0)
    table[0:nf, :] = jnp.where(wide == map_s_ref[...], 1.0, 0.0).astype(BF16)
    table[nf : 2 * nf, :] = jnp.where(wide == map_u_ref[...], 1.0, 0.0).astype(BF16)
    window_first = (block - 1) * pairs
    row_id = lax.broadcasted_iota(jnp.int32, (pairs, slots), 0)
    slot_id = lax.broadcasted_iota(jnp.int32, (pairs, slots), 1)
    count = jnp.zeros((pairs, slots), jnp.int32)
    for r in range(pairs):
        count = jnp.where(row_id == r, len_ref[r], count)
    target = jnp.where(slot_id < count, right_ref[...] - window_first, -1)
    source = left_ref[...] - window_first
    stride = n_chip * n_packed
    gap = stride - pairs
    source = source + 1 + jnp.where(source >= pairs, gap, 0) + jnp.where(source >= 2 * pairs, gap, 0)
    lanes = lax.broadcasted_iota(jnp.int32, (pairs, nf), 1)
    chosen = jnp.zeros((pairs, nf), jnp.int32)
    for k in range(slots):
        chosen = jnp.where(target[:, k : k + 1] == lanes, source[:, k : k + 1], chosen)
    sel_vec[...] = chosen
    to_scalar = pltpu.make_async_copy(sel_vec, sel, local.at[8])
    to_scalar.start()

    width = nf // n_chip
    tile_lane = lax.broadcasted_iota(jnp.int32, (rows, nf), 1)
    wide_prop = jnp.broadcast_to(prop_ref[...], (rows, nf))
    tiles = regroup([wide_prop] * n_chip)
    prop = tiles[0]
    for c in range(1, n_chip):
        prop = jnp.where(chip == c, tiles[c], prop)

    for half in (0, 1):
        lefts[half, 0] = jnp.zeros(lefts.shape[2:], BF16)
    zones = [
        (tile_lane >= width * z) & (tile_lane < width * (z + 1)) for z in range(n_chip)
    ]

    def fill_lefts(kind, slot):
        def one(g, carry):
            for c in range(n_chip):
                tile = (spread[slot, kind, c, g].astype(F32) * prop).astype(BF16)
                turned = [tile] + [pltpu.roll(tile, width * k, 1) for k in range(1, n_chip)]
                for q in range(n_chip):
                    at = 1 + slot * stride + g * n_chip + q
                    for half in (0, 1):
                        zone = 2 * half + kind
                        rest = jnp.zeros((rows, nf), BF16) if kind == VERTEX else lefts[half, at, c]
                        lefts[half, at, c] = jnp.where(zones[zone], turned[(zone - q) % n_chip], rest)
            return carry

        lax.fori_loop(0, n_packed, one, 0)

    pass_left_on(VERTEX)

    for o in range(1, n_freq):
        f = (freq + o) % n_freq
        arrive(columns.at[f], recv_cols.at[f])
    for g in range(n_groups):
        cols = jnp.concatenate([columns[:, kind, g].reshape(nf, nf) for kind in (0, 1)], axis=0)
        rows_t = lax.dot_general(
            cols, table[...], (((0,), (0,)), ((), ())), preferred_element_type=F32
        ).astype(BF16)
        n = min(group, pairs - g * group)
        start = OWN * pairs + g * group
        right[DERIV, core, start : start + n] = rows_t.reshape(group, rows, nf)[:n]
    push_beside(DERIV)
    push_left(DERIV)
    push_sibling(DERIV, OWN)

    for slot in (BEFORE, AFTER):
        arrive(own(VERTEX, slot), recv_right.at[VERTEX, core, slot])
        push_sibling(VERTEX, slot)
    fill_lefts(VERTEX, OWN)
    for slot in (BEFORE, AFTER):
        arrive(spread.at[slot, VERTEX], recv_beside.at[VERTEX, slot])
        fill_lefts(VERTEX, slot)

    pass_left_on(DERIV)
    fill_lefts(DERIV, OWN)
    for slot in (BEFORE, AFTER):
        arrive(own(DERIV, slot), recv_right.at[DERIV, core, slot])
        push_sibling(DERIV, slot)
    for slot in (BEFORE, AFTER):
        arrive(spread.at[slot, DERIV], recv_beside.at[DERIV, slot])
        fill_lefts(DERIV, slot)
    other = 1 - core
    for slot in (OWN, BEFORE, AFTER):
        for kind in (VERTEX, DERIV):
            arrive(own(kind, slot, other), recv_right.at[kind, other, slot])

    to_scalar.wait()
    size = pairs // PARTS
    tall = n_chip * rows

    def part_copy(part, o):
        c = (chip + o) % n_chip
        return pltpu.make_async_remote_copy(
            src_ref=part_out.at[part, o],
            dst_ref=part_in.at[part, chip],
            send_sem=send_part.at[part, o],
            recv_sem=recv_part.at[part, chip],
            device_id=(2 * c + core, block),
            device_id_type=MESH,
        )

    def one_part(part, carry):
        first_row = part * size
        lhs, rhs = [], []
        for q in range(0, 3 * pairs, 2):
            lhs.append(
                jnp.concatenate(
                    [
                        (
                            lefts[0, sel[first_row + r, q]] + lefts[1, sel[first_row + r, q + 1]]
                        ).reshape(tall, nf)
                        for r in range(size)
                    ],
                    axis=0,
                )
            )
            for p in (q, q + 1):
                rhs += [right[kind, :, p].reshape(2 * rows, nf) for kind in (DERIV, VERTEX)]
        terms = None
        for first in range(0, len(lhs), CHAIN):
            some = jnp.dot(
                jnp.concatenate(lhs[first : first + CHAIN], axis=1),
                jnp.concatenate(rhs[4 * first : 4 * (first + CHAIN)], axis=0),
                preferred_element_type=F32,
            )
            terms = some if terms is None else terms + some
        sums[...] = terms.reshape(size, n_chip, rows, nf)
        out_ref[pl.ds(first_row, size)] = sums[:, chip]
        for o in (2, 1, 3):
            part_out[part, o] = sums[:, (chip + o) % n_chip].astype(BF16)
            part_copy(part, o).start()
        return carry

    lax.fori_loop(0, PARTS, one_part, 0)
    for part in range(PARTS):
        at = slice(part * size, (part + 1) * size)
        total = out_ref[at]
        for o in (1, 3, 2):
            c = (chip + o) % n_chip
            arrive(part_in.at[part, c], recv_part.at[part, c])
            total = total + part_in[part, c].astype(F32)
        out_ref[at] = total
    for part in range(PARTS):
        for o in (2, 1, 3):
            part_copy(part, o).wait_send()
    for copy in sent:
        copy.wait_send()


def per_device(
    dims,
    vertex,
    deriv_s,
    deriv_u,
    freq_map_s,
    freq_map_u,
    pair_sym,
    propagator,
    left_pairs,
    right_pairs,
    lengths,
):
    n_freq, _ = dims
    n_chip = n_freq // 2
    pairs, rows, nf = vertex.shape
    n_groups = -(-pairs * rows // nf)
    n_packed = -(-pairs // n_chip)
    size = pairs // PARTS
    hbm = pl.BlockSpec(memory_space=pltpu.HBM)
    smem = pl.BlockSpec(memory_space=pltpu.SMEM)
    dma = pltpu.SemaphoreType.DMA
    return pl.pallas_call(
        functools.partial(kernel, dims),
        out_shape=jax.ShapeDtypeStruct((pairs, rows, nf), F32),
        in_specs=[hbm] * 8 + [smem] * 2,
        out_specs=pl.BlockSpec(memory_space=pltpu.VMEM),
        scratch_shapes=[
            pltpu.VMEM((pairs, rows, nf), BF16),
            pltpu.VMEM((pairs, rows, nf), BF16),
            pltpu.VMEM((1, nf), jnp.int32),
            pltpu.VMEM((1, nf), jnp.int32),
            pltpu.VMEM((1, nf), F32),
            pltpu.VMEM(left_pairs.shape, jnp.int32),
            pltpu.VMEM(right_pairs.shape, jnp.int32),
            pltpu.VMEM((2, 2, 3 * pairs, rows, nf), BF16),
            pltpu.VMEM((2, n_chip, n_packed, rows, nf), BF16),
            pltpu.VMEM((3, 2, n_chip, n_packed, rows, nf), BF16),
            pltpu.VMEM((2, 1 + 3 * n_packed * n_chip, n_chip, rows, nf), BF16),
            pltpu.VMEM((n_freq, 2, n_groups, rows, nf), BF16),
            pltpu.VMEM((n_freq, 2, n_groups, rows, nf), BF16),
            pltpu.VMEM((2 * nf, nf), BF16),
            pltpu.VMEM((size, n_chip, rows, nf), F32),
            pltpu.VMEM((PARTS, n_chip, size, rows, nf), BF16),
            pltpu.VMEM((PARTS, n_chip, size, rows, nf), BF16),
            pltpu.VMEM((pairs, nf), jnp.int32),
            pltpu.SMEM((pairs, nf), jnp.int32),
            dma((2, 2, 3)),
            dma((2, n_chip)),
            dma((2, 3)),
            dma((n_freq,)),
            dma((PARTS, n_chip)),
            dma((PARTS, n_chip)),
            dma((48,)),
            dma((9,)),
        ],
        compiler_params=pltpu.CompilerParams(
            collective_id=0, has_side_effects=True, vmem_limit_bytes=63 * 1024 * 1024
        ),
    )(
        vertex,
        jnp.swapaxes(deriv_s, 1, 2),
        jnp.swapaxes(deriv_u, 1, 2),
        freq_map_s.reshape(1, nf),
        freq_map_u.reshape(1, nf),
        propagator.reshape(1, nf),
        left_pairs,
        right_pairs,
        pair_sym,
        lengths,
    )


def solution(mesh):
    dims = (mesh.shape["freq"], mesh.shape["pair"])
    return jax.shard_map(
        functools.partial(per_device, dims),
        mesh=mesh,
        in_specs=(
            P("pair", "freq", None),
            P("pair", None, "freq"),
            P("pair", None, "freq"),
            P(),
            P(),
            P("pair"),
            P(),
            P("pair", None),
            P("pair", None),
            P("pair"),
        ),
        out_specs=P("pair", "freq", None),
        check_vma=False,
    )
```

```python
import functools

import jax
import jax.numpy as jnp
from jax import lax
from jax.experimental import pallas as pl
from jax.experimental.pallas import tpu as pltpu
from jax.sharding import PartitionSpec as P

MESH = pl.DeviceIdType.MESH
BF16 = jnp.bfloat16
F32 = jnp.float32

BEFORE, OWN, AFTER = 0, 1, 2
PARTS = 6


def regroup(parts):
    count = len(parts)
    rows, lanes = parts[0].shape
    width = lanes // count
    lane = lax.broadcasted_iota(jnp.int32, (rows, lanes), 1)
    parts = list(parts)
    step = 1
    while step < count:
        high = (lane & (width * step)) != 0
        for q in range(count):
            if (q // step) % 2 == 0:
                a, b = parts[q], parts[q + step]
                parts[q] = jnp.where(high, pltpu.roll(b, width * step, 1), a)
                parts[q + step] = jnp.where(high, b, pltpu.roll(a, lanes - width * step, 1))
        step *= 2
    return parts


def kernel(
    dims,
    v_in,
    s_in,
    u_in,
    map_s_in,
    map_u_in,
    prop_in,
    left_in,
    right_in,
    sym_ref,
    len_ref,
    out_ref,
    s_ref,
    u_ref,
    map_s_ref,
    map_u_ref,
    prop_ref,
    left_ref,
    right_ref,
    window,
    right,
    packed,
    spread,
    lefts,
    left_deriv,
    factors,
    chunks,
    columns,
    table,
    sums,
    part_out,
    part_in,
    sel_vec,
    sel,
    tile_vec,
    tile_sel,
    recv_vertex,
    recv_deriv,
    recv_spread,
    recv_beside,
    recv_cols,
    recv_part,
    send_part,
    send,
    local,
):
    n_freq, n_pair = dims
    n_chip = n_freq // 2
    pairs, rows, nf = v_in.shape
    slots = left_ref.shape[1]
    freq, block = lax.axis_index("freq"), lax.axis_index("pair")
    chip, core = freq // 2, freq % 2

    sibling = (freq + 1 - 2 * core, block)
    x_up = (freq, (block + 1) % n_pair)
    x_down = (freq, (block + n_pair - 1) % n_pair)

    y_up, y_down = ((freq + 2) % n_freq, block), ((freq + n_freq - 2) % n_freq, block)
    f_up, f_down, f_far = (freq + 2) % n_freq, (freq + 6) % n_freq, (freq + 4) % n_freq

    def deriv_of(slot=OWN, of=core):
        return right.at[of, slot * pairs : (slot + 1) * pairs]

    loads = [
        pltpu.make_async_copy(src, dst, local.at[i])
        for i, (src, dst) in enumerate(
            (
                (v_in, window.at[OWN, freq]),
                (s_in, s_ref),
                (u_in, u_ref),
                (map_s_in, map_s_ref),
                (map_u_in, map_u_ref),
                (prop_in, prop_ref),
                (left_in, left_ref),
                (right_in, right_ref),
            )
        )
    ]
    for load in loads:
        load.start()

    barrier = pltpu.get_barrier_semaphore()
    peers = [((freq + o) % n_freq, block) for o in range(1, n_freq)] + [x_up, x_down]
    for peer in peers:
        pl.semaphore_signal(barrier, inc=1, device_id=peer, device_id_type=MESH)
    pl.semaphore_wait(barrier, len(peers))

    sent = []

    def push(src, dst, recv_sem, peer):
        copy = pltpu.make_async_remote_copy(
            src_ref=src,
            dst_ref=dst,
            send_sem=send.at[len(sent)],
            recv_sem=recv_sem,
            device_id=peer,
            device_id_type=MESH,
        )
        copy.start()
        sent.append(copy)

    def arrive(ref, recv_sem):
        pltpu.make_async_remote_copy(
            src_ref=ref,
            dst_ref=ref,
            send_sem=send.at[0],
            recv_sem=recv_sem,
            device_id=sibling,
            device_id_type=MESH,
        ).wait_recv()

    def send_vertex(slot, f, peer, to=None):
        to = slot if to is None else to
        push(window.at[slot, f], window.at[to, f], recv_vertex.at[to, f], peer)

    def send_vertex_x(f):
        send_vertex(OWN, f, x_up, BEFORE)
        send_vertex(OWN, f, x_down, AFTER)

    def vertex_arrives(slot, f):
        arrive(window.at[slot, f], recv_vertex.at[slot, f])

    def send_deriv(slot, peer, to=None):
        to = slot if to is None else to
        push(deriv_of(slot), deriv_of(to), recv_deriv.at[core, to], peer)

    n_packed = packed.shape[1]
    zero_rows = jnp.zeros((rows, nf), BF16)

    def send_left():
        for g in range(n_packed):
            four = [
                window[OWN, freq, p] if p < pairs else zero_rows
                for p in range(n_chip * g, n_chip * (g + 1))
            ]
            for c, tile in enumerate(regroup(four)):
                packed[c, g] = tile
        spread[OWN, chip] = packed[chip]
        for o in (2, 1, 3):
            c = (chip + o) % n_chip
            push(
                packed.at[c], spread.at[OWN, chip], recv_spread.at[chip], (2 * c + core, block)
            )

    def pass_left_on():
        for o in (1, 3, 2):
            c = (chip + o) % n_chip
            arrive(spread.at[OWN, c], recv_spread.at[c])
        push(spread.at[OWN], spread.at[BEFORE], recv_beside.at[BEFORE], x_up)
        push(spread.at[OWN], spread.at[AFTER], recv_beside.at[AFTER], x_down)

    loads[0].wait()
    send_vertex_x(freq)
    send_left()
    send_vertex(OWN, freq, sibling)

    for load in loads[1:]:
        load.wait()
    group = nf // rows
    n_groups = columns.shape[2]
    for kind in (0, 1):
        for g in range(n_groups):
            eight = []
            for p in range(g * group, (g + 1) * group):
                if p >= pairs:
                    eight.append(zero_rows)
                elif kind == 0:
                    eight.append(s_ref[p])
                else:
                    eight.append(u_ref[lax.rem(sym_ref[p], pairs)])
            for f, tile in enumerate(regroup(eight)):
                chunks[f, kind, g] = tile
    columns[freq] = chunks[freq]
    for o in (4, 3, 5, 2, 6, 1, 7):
        f = (freq + o) % n_freq
        push(chunks.at[f], columns.at[freq], recv_cols.at[freq], (f, block))
    send_vertex(OWN, freq, y_up)
    send_vertex(OWN, freq, y_down)

    wide = lax.broadcasted_iota(jnp.int32, (nf, nf), 0)
    table[0:nf, :] = jnp.where(wide == map_s_ref[...], 1.0, 0.0).astype(BF16)
    table[nf : 2 * nf, :] = jnp.where(wide == map_u_ref[...], 1.0, 0.0).astype(BF16)
    window_first = (block - 1) * pairs
    row_id = lax.broadcasted_iota(jnp.int32, (pairs, slots), 0)
    slot_id = lax.broadcasted_iota(jnp.int32, (pairs, slots), 1)
    count = jnp.zeros((pairs, slots), jnp.int32)
    for r in range(pairs):
        count = jnp.where(row_id == r, len_ref[r], count)
    target = jnp.where(slot_id < count, right_ref[...] - window_first, -1)
    source = left_ref[...] - window_first
    plain = source + 1
    gap = n_chip * n_packed - pairs
    source = source + jnp.where(source >= pairs, gap, 0) + jnp.where(source >= 2 * pairs, gap, 0)
    lanes = lax.broadcasted_iota(jnp.int32, (pairs, nf), 1)
    chosen = jnp.full((pairs, nf), -1, jnp.int32)
    chosen_plain = jnp.zeros((pairs, nf), jnp.int32)
    for k in range(slots):
        hit = target[:, k : k + 1] == lanes
        chosen = jnp.where(hit, source[:, k : k + 1], chosen)
        chosen_plain = jnp.where(hit, plain[:, k : k + 1], chosen_plain)
    turn = (lanes - chosen) & (n_chip - 1)
    tile_id = 1 + turn * (3 * n_packed) + (chosen >> (n_chip.bit_length() - 1))
    tile_vec[...] = jnp.where(chosen < 0, 0, tile_id)
    sel_vec[...] = chosen_plain
    to_scalar = [
        pltpu.make_async_copy(sel_vec, sel, local.at[8]),
        pltpu.make_async_copy(tile_vec, tile_sel, local.at[9]),
    ]
    for copy in to_scalar:
        copy.start()

    width = nf // n_chip
    tile_lane = lax.broadcasted_iota(jnp.int32, (rows, nf), 1)
    wide_prop = jnp.broadcast_to(prop_ref[...], (rows, nf))
    tiles = regroup([wide_prop] * n_chip)
    prop = tiles[0]
    for c in range(1, n_chip):
        prop = jnp.where(chip == c, tiles[c], prop)

    lefts[0] = jnp.zeros(lefts.shape[1:], BF16)
    left_deriv[0] = zero_rows

    def fill_lefts(slot):
        def one(g, carry):
            for c in range(n_chip):
                tile = (spread[slot, c, g].astype(F32) * prop).astype(BF16)
                at = 1 + slot * n_packed + g
                lefts[at, c] = tile
                for k in range(1, n_chip):
                    lefts[at + k * (3 * n_packed), c] = pltpu.roll(tile, width * k, 1)
            return carry

        lax.fori_loop(0, n_packed, one, 0)

    def fill_deriv(slot):
        tall = right[core, slot * pairs : (slot + 1) * pairs].astype(F32) * prop_ref[...]
        left_deriv[1 + slot * pairs : 1 + (slot + 1) * pairs] = tall.astype(BF16)

    pass_left_on()
    for slot in (BEFORE, AFTER):
        vertex_arrives(slot, freq)
        send_vertex(slot, freq, y_down)
        send_vertex(slot, freq, sibling)
    fill_lefts(OWN)

    for o in range(1, n_freq):
        f = (freq + o) % n_freq
        arrive(columns.at[f], recv_cols.at[f])
    for g in range(n_groups):
        cols = jnp.concatenate([columns[:, kind, g].reshape(nf, nf) for kind in (0, 1)], axis=0)
        rows_t = lax.dot_general(
            cols, table[...], (((0,), (0,)), ((), ())), preferred_element_type=F32
        ).astype(BF16)
        n = min(group, pairs - g * group)
        start = OWN * pairs + g * group
        right[core, start : start + n] = rows_t.reshape(group, rows, nf)[:n]
    send_deriv(OWN, x_up, BEFORE)
    send_deriv(OWN, x_down, AFTER)
    send_deriv(OWN, sibling)

    vertex_arrives(OWN, f_down)
    send_vertex(OWN, f_down, y_up)
    send_vertex_x(f_down)
    send_vertex(OWN, f_down, sibling)
    vertex_arrives(OWN, f_up)
    send_vertex(OWN, f_up, sibling)
    fill_deriv(OWN)
    for slot in (BEFORE, AFTER):
        arrive(spread.at[slot], recv_beside.at[slot])
        fill_lefts(slot)
    for copy in to_scalar:
        copy.wait()

    tile_lanes = lax.broadcasted_iota(jnp.int32, (n_chip, rows, nf), 2)
    upper = tile_lanes >= 2 * width
    odd = (tile_lanes & width) != 0
    n_quads = factors.shape[0]

    def gather(t, carry):
        for r in range(pairs):
            one, two, three, four = (lefts[tile_sel[r, n_chip * t + s]] for s in range(n_chip))
            tile = jnp.where(upper, jnp.where(odd, four, three), jnp.where(odd, two, one))
            factors[t, r] = tile
        return carry

    lax.fori_loop(0, n_quads // 3, gather, 0)
    for slot in (BEFORE, AFTER):
        arrive(deriv_of(slot), recv_deriv.at[core, slot])
        send_deriv(slot, sibling)
        fill_deriv(slot)
    lax.fori_loop(n_quads // 3, 2 * n_quads // 3, gather, 0)
    vertex_arrives(OWN, f_far)
    send_vertex_x(f_far)
    send_vertex(OWN, f_far, sibling)
    lax.fori_loop(2 * n_quads // 3, n_quads, gather, 0)
    for slot in (BEFORE, AFTER):
        vertex_arrives(slot, f_up)
        send_vertex(slot, f_up, sibling)
    other = 1 - core
    for slot in (OWN, BEFORE, AFTER):
        arrive(deriv_of(slot, other), recv_deriv.at[other, slot])

    size = pairs // PARTS
    tall = n_chip * rows

    def part_copy(part, o):
        c = (chip + o) % n_chip
        return pltpu.make_async_remote_copy(
            src_ref=part_out.at[part, o],
            dst_ref=part_in.at[part, chip],
            send_sem=send_part.at[part, o],
            recv_sem=recv_part.at[part, chip],
            device_id=(2 * c + core, block),
            device_id_type=MESH,
        )

    def vertex_part(part, carry):
        here = pl.ds(part * size, size)
        lhs = [factors[t, here].reshape(size * tall, nf) for t in range(n_quads)]
        rhs = []
        for p in range(n_chip * n_quads):
            at = p if p < 3 * pairs else p - n_chip
            rhs.append(right[:, at].reshape(2 * rows, nf))
        terms = jnp.dot(
            jnp.concatenate(lhs, axis=1),
            jnp.concatenate(rhs, axis=0),
            preferred_element_type=F32,
        )
        sums[...] = terms.reshape(size, n_chip, rows, nf)
        out_ref[here] = sums[:, chip]
        for o in (2, 1, 3):
            part_out[part, o] = sums[:, (chip + o) % n_chip].astype(BF16)
            part_copy(part, o).start()
        return carry

    lax.fori_loop(0, PARTS // 2, vertex_part, 0)
    for slot in (BEFORE, AFTER):
        vertex_arrives(slot, f_down)
        send_vertex(slot, f_down, sibling)
    lax.fori_loop(PARTS // 2, PARTS, vertex_part, 0)

    half = pairs // 2

    def add_deriv(slot):
        def one(part, carry):
            first_row = part * half
            lhs, rhs = [], []
            for p in range(pairs):
                q = slot * pairs + p
                lhs.append(
                    jnp.concatenate(
                        [left_deriv[sel[first_row + r, q]] for r in range(half)], axis=0
                    )
                )
                rhs.append(window[slot, :, p].reshape(nf, nf))
            terms = jnp.dot(
                jnp.concatenate(lhs, axis=1),
                jnp.concatenate(rhs, axis=0),
                preferred_element_type=F32,
            )
            out_ref[pl.ds(first_row, half)] += terms.reshape(half, rows, nf)
            return carry

        lax.fori_loop(0, 2, one, 0)

    def from_sibling(slot):
        for f in (0, 2, 4, 6):
            vertex_arrives(slot, (sibling[0] + f) % n_freq)

    from_sibling(OWN)
    add_deriv(OWN)
    for slot in (BEFORE, AFTER):
        vertex_arrives(slot, f_far)
        send_vertex(slot, f_far, sibling)
    for slot in (BEFORE, AFTER):
        from_sibling(slot)
        add_deriv(slot)
    for part in range(PARTS):
        at = slice(part * size, (part + 1) * size)
        total = out_ref[at]
        for o in (1, 3, 2):
            c = (chip + o) % n_chip
            arrive(part_in.at[part, c], recv_part.at[part, c])
            total = total + part_in[part, c].astype(F32)
        out_ref[at] = total
    for part in range(PARTS):
        for o in (2, 1, 3):
            part_copy(part, o).wait_send()
    for copy in sent:
        copy.wait_send()


def per_device(
    dims,
    vertex,
    deriv_s,
    deriv_u,
    freq_map_s,
    freq_map_u,
    pair_sym,
    propagator,
    left_pairs,
    right_pairs,
    lengths,
):
    n_freq, _ = dims
    n_chip = n_freq // 2
    pairs, rows, nf = vertex.shape
    n_groups = -(-pairs * rows // nf)
    n_packed = -(-pairs // n_chip)
    size = pairs // PARTS
    hbm = pl.BlockSpec(memory_space=pltpu.HBM)
    smem = pl.BlockSpec(memory_space=pltpu.SMEM)
    dma = pltpu.SemaphoreType.DMA
    return pl.pallas_call(
        functools.partial(kernel, dims),
        out_shape=jax.ShapeDtypeStruct((pairs, rows, nf), F32),
        in_specs=[hbm] * 8 + [smem] * 2,
        out_specs=pl.BlockSpec(memory_space=pltpu.VMEM),
        scratch_shapes=[
            pltpu.VMEM((pairs, rows, nf), BF16),
            pltpu.VMEM((pairs, rows, nf), BF16),
            pltpu.VMEM((1, nf), jnp.int32),
            pltpu.VMEM((1, nf), jnp.int32),
            pltpu.VMEM((1, nf), F32),
            pltpu.VMEM(left_pairs.shape, jnp.int32),
            pltpu.VMEM(right_pairs.shape, jnp.int32),
            pltpu.VMEM((3, n_freq, pairs, rows, nf), BF16),
            pltpu.VMEM((2, 3 * pairs, rows, nf), BF16),
            pltpu.VMEM((n_chip, n_packed, rows, nf), BF16),
            pltpu.VMEM((3, n_chip, n_packed, rows, nf), BF16),
            pltpu.VMEM((1 + n_chip * 3 * n_packed, n_chip, rows, nf), BF16),
            pltpu.VMEM((1 + 3 * pairs, rows, nf), BF16),
            pltpu.VMEM((-(-3 * pairs // n_chip), pairs, n_chip, rows, nf), BF16),
            pltpu.VMEM((n_freq, 2, n_groups, rows, nf), BF16),
            pltpu.VMEM((n_freq, 2, n_groups, rows, nf), BF16),
            pltpu.VMEM((2 * nf, nf), BF16),
            pltpu.VMEM((size, n_chip, rows, nf), F32),
            pltpu.VMEM((PARTS, n_chip, size, rows, nf), BF16),
            pltpu.VMEM((PARTS, n_chip, size, rows, nf), BF16),
            pltpu.VMEM((pairs, nf), jnp.int32),
            pltpu.SMEM((pairs, nf), jnp.int32),
            pltpu.VMEM((pairs, nf), jnp.int32),
            pltpu.SMEM((pairs, nf), jnp.int32),
            dma((3, n_freq)),
            dma((2, 3)),
            dma((n_chip,)),
            dma((3,)),
            dma((n_freq,)),
            dma((PARTS, n_chip)),
            dma((PARTS, n_chip)),
            dma((48,)),
            dma((10,)),
        ],
        compiler_params=pltpu.CompilerParams(
            collective_id=0, has_side_effects=True, vmem_limit_bytes=63 * 1024 * 1024
        ),
    )(
        vertex,
        jnp.swapaxes(deriv_s, 1, 2),
        jnp.swapaxes(deriv_u, 1, 2),
        freq_map_s.reshape(1, nf),
        freq_map_u.reshape(1, nf),
        propagator.reshape(1, nf),
        left_pairs,
        right_pairs,
        pair_sym,
        lengths,
    )


def solution(mesh):
    dims = (mesh.shape["freq"], mesh.shape["pair"])
    return jax.shard_map(
        functools.partial(per_device, dims),
        mesh=mesh,
        in_specs=(
            P("pair", "freq", None),
            P("pair", None, "freq"),
            P("pair", None, "freq"),
            P(),
            P(),
            P("pair"),
            P(),
            P("pair", None),
            P("pair", None),
            P("pair"),
        ),
        out_specs=P("pair", "freq", None),
        check_vma=False,
    )
```

```python
import functools

import jax
import jax.numpy as jnp
from jax import lax
from jax.experimental import pallas as pl
from jax.experimental.pallas import tpu as pltpu
from jax.sharding import PartitionSpec as P

MESH = pl.DeviceIdType.MESH
BF16 = jnp.bfloat16
F32 = jnp.float32

BEFORE, OWN, AFTER = 0, 1, 2
PARTS = 6


def regroup(parts):
    count = len(parts)
    rows, lanes = parts[0].shape
    width = lanes // count
    lane = lax.broadcasted_iota(jnp.int32, (rows, lanes), 1)
    parts = list(parts)
    step = 1
    while step < count:
        high = (lane & (width * step)) != 0
        for q in range(count):
            if (q // step) % 2 == 0:
                a, b = parts[q], parts[q + step]
                parts[q] = jnp.where(high, pltpu.roll(b, width * step, 1), a)
                parts[q + step] = jnp.where(high, b, pltpu.roll(a, lanes - width * step, 1))
        step *= 2
    return parts


def kernel(
    dims,
    v_in,
    s_in,
    u_in,
    map_s_in,
    map_u_in,
    prop_in,
    left_in,
    right_in,
    sym_in,
    len_in,
    out_ref,
    s_ref,
    u_ref,
    map_s_ref,
    map_u_ref,
    prop_ref,
    left_ref,
    right_ref,
    sym_ref,
    len_ref,
    window,
    right,
    packed,
    spread,
    lefts,
    left_deriv,
    factors,
    chunks,
    columns,
    table,
    sums,
    part_out,
    part_in,
    sel_vec,
    sel,
    tile_vec,
    tile_sel,
    recv_vertex,
    recv_deriv,
    recv_spread,
    recv_beside,
    recv_cols,
    recv_part,
    send_part,
    send,
    local,
):
    n_freq, n_pair = dims
    n_chip = n_freq // 2
    pairs, rows, nf = v_in.shape
    slots = left_ref.shape[1]
    freq, block = lax.axis_index("freq"), lax.axis_index("pair")
    chip, core = freq // 2, freq % 2

    sibling = (freq + 1 - 2 * core, block)
    x_up = (freq, (block + 1) % n_pair)
    x_down = (freq, (block + n_pair - 1) % n_pair)

    y_up, y_down = ((freq + 2) % n_freq, block), ((freq + n_freq - 2) % n_freq, block)
    f_up, f_down, f_far = (freq + 2) % n_freq, (freq + 6) % n_freq, (freq + 4) % n_freq

    def deriv_of(slot=OWN, of=core):
        return right.at[of, slot * pairs : (slot + 1) * pairs]

    barrier = pltpu.get_barrier_semaphore()
    peers = [((freq + o) % n_freq, block) for o in range(1, n_freq)] + [x_up, x_down]
    for peer in peers:
        pl.semaphore_signal(barrier, inc=1, device_id=peer, device_id_type=MESH)
    loads = [
        pltpu.make_async_copy(src, dst, local.at[i])
        for i, (src, dst) in enumerate(
            (
                (v_in, window.at[OWN, freq]),
                (sym_in, sym_ref),
                (s_in, s_ref),
                (u_in, u_ref),
                (map_s_in, map_s_ref),
                (map_u_in, map_u_ref),
                (prop_in, prop_ref),
                (left_in, left_ref),
                (right_in, right_ref),
                (len_in, len_ref),
            )
        )
    ]
    for load in loads:
        load.start()

    sent = []

    def push(src, dst, recv_sem, peer):
        copy = pltpu.make_async_remote_copy(
            src_ref=src,
            dst_ref=dst,
            send_sem=send.at[len(sent)],
            recv_sem=recv_sem,
            device_id=peer,
            device_id_type=MESH,
        )
        copy.start()
        sent.append(copy)

    def arrive(ref, recv_sem):
        pltpu.make_async_remote_copy(
            src_ref=ref,
            dst_ref=ref,
            send_sem=send.at[0],
            recv_sem=recv_sem,
            device_id=sibling,
            device_id_type=MESH,
        ).wait_recv()

    def send_vertex(slot, f, peer, to=None):
        to = slot if to is None else to
        push(window.at[slot, f], window.at[to, f], recv_vertex.at[to, f], peer)

    def send_vertex_x(f):
        send_vertex(OWN, f, x_up, BEFORE)
        send_vertex(OWN, f, x_down, AFTER)

    def vertex_arrives(slot, f):
        arrive(window.at[slot, f], recv_vertex.at[slot, f])

    def send_deriv(slot, peer, to=None):
        to = slot if to is None else to
        push(deriv_of(slot), deriv_of(to), recv_deriv.at[core, to], peer)

    n_packed = packed.shape[1]
    zero_rows = jnp.zeros((rows, nf), BF16)

    def pack_left():
        for g in range(n_packed):
            four = [
                window[OWN, freq, p] if p < pairs else zero_rows
                for p in range(n_chip * g, n_chip * (g + 1))
            ]
            for c, tile in enumerate(regroup(four)):
                packed[c, g] = tile
        spread[OWN, chip] = packed[chip]

    def send_left():
        for o in (2, 1, 3):
            c = (chip + o) % n_chip
            push(
                packed.at[c], spread.at[OWN, chip], recv_spread.at[chip], (2 * c + core, block)
            )

    def pass_left_on():
        for o in (1, 3, 2):
            c = (chip + o) % n_chip
            arrive(spread.at[OWN, c], recv_spread.at[c])
        push(spread.at[OWN], spread.at[BEFORE], recv_beside.at[BEFORE], x_up)
        push(spread.at[OWN], spread.at[AFTER], recv_beside.at[AFTER], x_down)

    loads[0].wait()
    pack_left()
    for load in loads[1:4]:
        load.wait()
    group = nf // rows
    n_groups = columns.shape[2]
    for kind in (0, 1):
        for g in range(n_groups):
            eight = []
            for p in range(g * group, (g + 1) * group):
                if p >= pairs:
                    eight.append(zero_rows)
                elif kind == 0:
                    eight.append(s_ref[p])
                else:
                    eight.append(u_ref[lax.rem(sym_ref[p], pairs)])
            for f, tile in enumerate(regroup(eight)):
                chunks[f, kind, g] = tile
    columns[freq] = chunks[freq]

    pl.semaphore_wait(barrier, len(peers))
    send_vertex_x(freq)
    send_left()
    for o in (4, 3, 5, 2, 6, 1, 7):
        f = (freq + o) % n_freq
        push(chunks.at[f], columns.at[freq], recv_cols.at[freq], (f, block))
    send_vertex(OWN, freq, y_up)
    send_vertex(OWN, freq, y_down)
    send_vertex(OWN, freq, sibling)

    for load in loads[4:]:
        load.wait()
    wide = lax.broadcasted_iota(jnp.int32, (nf, nf), 0)
    table[0:nf, :] = jnp.where(wide == map_s_ref[...], 1.0, 0.0).astype(BF16)
    table[nf : 2 * nf, :] = jnp.where(wide == map_u_ref[...], 1.0, 0.0).astype(BF16)

    width = nf // n_chip
    tile_lane = lax.broadcasted_iota(jnp.int32, (rows, nf), 1)
    wide_prop = jnp.broadcast_to(prop_ref[...], (rows, nf))
    tiles = regroup([wide_prop] * n_chip)
    prop = tiles[0]
    for c in range(1, n_chip):
        prop = jnp.where(chip == c, tiles[c], prop)

    lefts[0] = jnp.zeros(lefts.shape[1:], BF16)
    left_deriv[0] = zero_rows

    def fill_lefts(slot):
        def one(g, carry):
            for c in range(n_chip):
                tile = (spread[slot, c, g].astype(F32) * prop).astype(BF16)
                at = 1 + slot * n_packed + g
                lefts[at, c] = tile
                for k in range(1, n_chip):
                    lefts[at + k * (3 * n_packed), c] = pltpu.roll(tile, width * k, 1)
            return carry

        lax.fori_loop(0, n_packed, one, 0)

    def fill_deriv(slot):
        tall = right[core, slot * pairs : (slot + 1) * pairs].astype(F32) * prop_ref[...]
        left_deriv[1 + slot * pairs : 1 + (slot + 1) * pairs] = tall.astype(BF16)

    pass_left_on()

    window_first = (block - 1) * pairs
    row_id = lax.broadcasted_iota(jnp.int32, (pairs, slots), 0)
    slot_id = lax.broadcasted_iota(jnp.int32, (pairs, slots), 1)
    count = jnp.zeros((pairs, slots), jnp.int32)
    for r in range(pairs):
        count = jnp.where(row_id == r, len_ref[r], count)
    target = jnp.where(slot_id < count, right_ref[...] - window_first, -1)
    source = left_ref[...] - window_first
    plain = source + 1
    gap = n_chip * n_packed - pairs
    source = source + jnp.where(source >= pairs, gap, 0) + jnp.where(source >= 2 * pairs, gap, 0)
    lanes = lax.broadcasted_iota(jnp.int32, (pairs, nf), 1)
    chosen = jnp.full((pairs, nf), -1, jnp.int32)
    chosen_plain = jnp.zeros((pairs, nf), jnp.int32)
    for k in range(slots):
        hit = target[:, k : k + 1] == lanes
        chosen = jnp.where(hit, source[:, k : k + 1], chosen)
        chosen_plain = jnp.where(hit, plain[:, k : k + 1], chosen_plain)
    turn = (lanes - chosen) & (n_chip - 1)
    tile_id = 1 + turn * (3 * n_packed) + (chosen >> (n_chip.bit_length() - 1))
    tile_vec[...] = jnp.where(chosen < 0, 0, tile_id)
    sel_vec[...] = chosen_plain
    to_scalar = [
        pltpu.make_async_copy(sel_vec, sel, local.at[10]),
        pltpu.make_async_copy(tile_vec, tile_sel, local.at[11]),
    ]
    for copy in to_scalar:
        copy.start()

    for slot in (BEFORE, AFTER):
        vertex_arrives(slot, freq)
        send_vertex(slot, freq, y_down)
        send_vertex(slot, freq, sibling)
    fill_lefts(OWN)

    for o in range(1, n_freq):
        f = (freq + o) % n_freq
        arrive(columns.at[f], recv_cols.at[f])
    for g in range(n_groups):
        cols = jnp.concatenate([columns[:, kind, g].reshape(nf, nf) for kind in (0, 1)], axis=0)
        rows_t = lax.dot_general(
            cols, table[...], (((0,), (0,)), ((), ())), preferred_element_type=F32
        ).astype(BF16)
        n = min(group, pairs - g * group)
        start = OWN * pairs + g * group
        right[core, start : start + n] = rows_t.reshape(group, rows, nf)[:n]
    send_deriv(OWN, x_up, BEFORE)
    send_deriv(OWN, x_down, AFTER)
    send_deriv(OWN, sibling)

    vertex_arrives(OWN, f_down)
    send_vertex(OWN, f_down, y_up)
    send_vertex_x(f_down)
    send_vertex(OWN, f_down, sibling)
    vertex_arrives(OWN, f_up)
    send_vertex(OWN, f_up, sibling)
    fill_deriv(OWN)
    for slot in (BEFORE, AFTER):
        arrive(spread.at[slot], recv_beside.at[slot])
        fill_lefts(slot)
    for copy in to_scalar:
        copy.wait()

    tile_lanes = lax.broadcasted_iota(jnp.int32, (n_chip, rows, nf), 2)
    upper = tile_lanes >= 2 * width
    odd = (tile_lanes & width) != 0
    n_quads = factors.shape[0]

    def gather(t, carry):
        for r in range(pairs):
            one, two, three, four = (lefts[tile_sel[r, n_chip * t + s]] for s in range(n_chip))
            tile = jnp.where(upper, jnp.where(odd, four, three), jnp.where(odd, two, one))
            factors[t, r] = tile
        return carry

    lax.fori_loop(0, n_quads // 3, gather, 0)
    for slot in (BEFORE, AFTER):
        arrive(deriv_of(slot), recv_deriv.at[core, slot])
        send_deriv(slot, sibling)
        fill_deriv(slot)
    lax.fori_loop(n_quads // 3, 2 * n_quads // 3, gather, 0)
    vertex_arrives(OWN, f_far)
    send_vertex_x(f_far)
    send_vertex(OWN, f_far, sibling)
    lax.fori_loop(2 * n_quads // 3, n_quads, gather, 0)
    for slot in (BEFORE, AFTER):
        vertex_arrives(slot, f_up)
        send_vertex(slot, f_up, sibling)
    other = 1 - core
    for slot in (OWN, BEFORE, AFTER):
        arrive(deriv_of(slot, other), recv_deriv.at[other, slot])

    size = pairs // PARTS
    tall = n_chip * rows

    def part_copy(part, o):
        c = (chip + o) % n_chip
        return pltpu.make_async_remote_copy(
            src_ref=part_out.at[part, o],
            dst_ref=part_in.at[part, chip],
            send_sem=send_part.at[part, o],
            recv_sem=recv_part.at[part, chip],
            device_id=(2 * c + core, block),
            device_id_type=MESH,
        )

    def vertex_part(part, carry):
        here = pl.ds(part * size, size)
        lhs = [factors[t, here].reshape(size * tall, nf) for t in range(n_quads)]
        rhs = []
        for p in range(n_chip * n_quads):
            at = p if p < 3 * pairs else p - n_chip
            rhs.append(right[:, at].reshape(2 * rows, nf))
        terms = jnp.dot(
            jnp.concatenate(lhs, axis=1),
            jnp.concatenate(rhs, axis=0),
            preferred_element_type=F32,
        )
        sums[...] = terms.reshape(size, n_chip, rows, nf)
        out_ref[here] = sums[:, chip]
        for o in (2, 1, 3):
            part_out[part, o] = sums[:, (chip + o) % n_chip].astype(BF16)
            part_copy(part, o).start()
        return carry

    lax.fori_loop(0, PARTS // 2, vertex_part, 0)
    for slot in (BEFORE, AFTER):
        vertex_arrives(slot, f_down)
        send_vertex(slot, f_down, sibling)
    lax.fori_loop(PARTS // 2, PARTS, vertex_part, 0)

    half = pairs // 2

    def add_deriv(slot):
        def one(part, carry):
            first_row = part * half
            lhs, rhs = [], []
            for p in range(pairs):
                q = slot * pairs + p
                lhs.append(
                    jnp.concatenate(
                        [left_deriv[sel[first_row + r, q]] for r in range(half)], axis=0
                    )
                )
                rhs.append(window[slot, :, p].reshape(nf, nf))
            terms = jnp.dot(
                jnp.concatenate(lhs, axis=1),
                jnp.concatenate(rhs, axis=0),
                preferred_element_type=F32,
            )
            out_ref[pl.ds(first_row, half)] += terms.reshape(half, rows, nf)
            return carry

        lax.fori_loop(0, 2, one, 0)

    def from_sibling(slot):
        for f in (0, 2, 4, 6):
            vertex_arrives(slot, (sibling[0] + f) % n_freq)

    from_sibling(OWN)
    add_deriv(OWN)
    for slot in (BEFORE, AFTER):
        vertex_arrives(slot, f_far)
        send_vertex(slot, f_far, sibling)
    for slot in (BEFORE, AFTER):
        from_sibling(slot)
        add_deriv(slot)
    for part in range(PARTS):
        at = slice(part * size, (part + 1) * size)
        total = out_ref[at]
        for o in (1, 3, 2):
            c = (chip + o) % n_chip
            arrive(part_in.at[part, c], recv_part.at[part, c])
            total = total + part_in[part, c].astype(F32)
        out_ref[at] = total
    for part in range(PARTS):
        for o in (2, 1, 3):
            part_copy(part, o).wait_send()
    for copy in sent:
        copy.wait_send()


def per_device(
    dims,
    vertex,
    deriv_s,
    deriv_u,
    freq_map_s,
    freq_map_u,
    pair_sym,
    propagator,
    left_pairs,
    right_pairs,
    lengths,
):
    n_freq, _ = dims
    n_chip = n_freq // 2
    pairs, rows, nf = vertex.shape
    n_groups = -(-pairs * rows // nf)
    n_packed = -(-pairs // n_chip)
    size = pairs // PARTS
    hbm = pl.BlockSpec(memory_space=pltpu.HBM)
    dma = pltpu.SemaphoreType.DMA
    return pl.pallas_call(
        functools.partial(kernel, dims),
        out_shape=jax.ShapeDtypeStruct((pairs, rows, nf), F32),
        in_specs=[hbm] * 10,
        out_specs=pl.BlockSpec(memory_space=pltpu.VMEM),
        scratch_shapes=[
            pltpu.VMEM((pairs, rows, nf), BF16),
            pltpu.VMEM((pairs, rows, nf), BF16),
            pltpu.VMEM((1, nf), jnp.int32),
            pltpu.VMEM((1, nf), jnp.int32),
            pltpu.VMEM((1, nf), F32),
            pltpu.VMEM(left_pairs.shape, jnp.int32),
            pltpu.VMEM(right_pairs.shape, jnp.int32),
            pltpu.SMEM(pair_sym.shape, jnp.int32),
            pltpu.SMEM(lengths.shape, jnp.int32),
            pltpu.VMEM((3, n_freq, pairs, rows, nf), BF16),
            pltpu.VMEM((2, 3 * pairs, rows, nf), BF16),
            pltpu.VMEM((n_chip, n_packed, rows, nf), BF16),
            pltpu.VMEM((3, n_chip, n_packed, rows, nf), BF16),
            pltpu.VMEM((1 + n_chip * 3 * n_packed, n_chip, rows, nf), BF16),
            pltpu.VMEM((1 + 3 * pairs, rows, nf), BF16),
            pltpu.VMEM((-(-3 * pairs // n_chip), pairs, n_chip, rows, nf), BF16),
            pltpu.VMEM((n_freq, 2, n_groups, rows, nf), BF16),
            pltpu.VMEM((n_freq, 2, n_groups, rows, nf), BF16),
            pltpu.VMEM((2 * nf, nf), BF16),
            pltpu.VMEM((size, n_chip, rows, nf), F32),
            pltpu.VMEM((PARTS, n_chip, size, rows, nf), BF16),
            pltpu.VMEM((PARTS, n_chip, size, rows, nf), BF16),
            pltpu.VMEM((pairs, nf), jnp.int32),
            pltpu.SMEM((pairs, nf), jnp.int32),
            pltpu.VMEM((pairs, nf), jnp.int32),
            pltpu.SMEM((pairs, nf), jnp.int32),
            dma((3, n_freq)),
            dma((2, 3)),
            dma((n_chip,)),
            dma((3,)),
            dma((n_freq,)),
            dma((PARTS, n_chip)),
            dma((PARTS, n_chip)),
            dma((48,)),
            dma((12,)),
        ],
        compiler_params=pltpu.CompilerParams(
            collective_id=0, has_side_effects=True, vmem_limit_bytes=63 * 1024 * 1024
        ),
    )(
        vertex,
        jnp.swapaxes(deriv_s, 1, 2),
        jnp.swapaxes(deriv_u, 1, 2),
        freq_map_s.reshape(1, nf),
        freq_map_u.reshape(1, nf),
        propagator.reshape(1, nf),
        left_pairs,
        right_pairs,
        pair_sym,
        lengths,
    )


def solution(mesh):
    dims = (mesh.shape["freq"], mesh.shape["pair"])
    return jax.shard_map(
        functools.partial(per_device, dims),
        mesh=mesh,
        in_specs=(
            P("pair", "freq", None),
            P("pair", None, "freq"),
            P("pair", None, "freq"),
            P(),
            P(),
            P("pair"),
            P(),
            P("pair", None),
            P("pair", None),
            P("pair"),
        ),
        out_specs=P("pair", "freq", None),
        check_vma=False,
    )
```

```python
import functools

import jax
import jax.numpy as jnp
from jax import lax
from jax.experimental import pallas as pl
from jax.experimental.pallas import tpu as pltpu
from jax.sharding import PartitionSpec as P

MESH = pl.DeviceIdType.MESH
BF16 = jnp.bfloat16
F32 = jnp.float32

BEFORE, OWN, AFTER = 0, 1, 2
PARTS = 6


def regroup(parts):
    count = len(parts)
    rows, lanes = parts[0].shape
    width = lanes // count
    lane = lax.broadcasted_iota(jnp.int32, (rows, lanes), 1)
    parts = list(parts)
    step = 1
    while step < count:
        high = (lane & (width * step)) != 0
        for q in range(count):
            if (q // step) % 2 == 0:
                a, b = parts[q], parts[q + step]
                parts[q] = jnp.where(high, pltpu.roll(b, width * step, 1), a)
                parts[q + step] = jnp.where(high, b, pltpu.roll(a, lanes - width * step, 1))
        step *= 2
    return parts


def product(lhs, rhs, cut):
    total = [None, None]
    for first in range(0, len(lhs), 2):
        right = jnp.concatenate(rhs[first : first + 2], axis=0)
        for part, at in enumerate((slice(0, cut), slice(cut, None))):
            left = jnp.concatenate([piece[at] for piece in lhs[first : first + 2]], axis=1)
            one = jnp.dot(left, right, preferred_element_type=F32)
            total[part] = one if total[part] is None else total[part] + one
    return jnp.concatenate(total, axis=0)


def kernel(
    dims,
    v_in,
    s_in,
    u_in,
    map_s_in,
    map_u_in,
    prop_in,
    left_in,
    right_in,
    sym_in,
    len_in,
    vertex_out,
    deriv_out,
    s_ref,
    u_ref,
    map_s_ref,
    map_u_ref,
    prop_ref,
    left_ref,
    right_ref,
    sym_ref,
    len_ref,
    window,
    right,
    packed,
    spread,
    lefts,
    left_deriv,
    factors,
    chunks,
    columns,
    table,
    sums,
    vertex_sum,
    deriv_sum,
    part_out,
    part_in,
    sel_vec,
    sel,
    tile_vec,
    tile_sel,
    recv_vertex,
    recv_deriv,
    recv_spread,
    recv_beside,
    recv_cols,
    recv_part,
    send_part,
    send,
    local,
):
    n_freq, n_pair = dims
    n_chip = n_freq // 2
    pairs, rows, nf = v_in.shape
    slots = left_ref.shape[1]
    freq, block = lax.axis_index("freq"), lax.axis_index("pair")
    chip, core = freq // 2, freq % 2

    sibling = (freq + 1 - 2 * core, block)
    x_up = (freq, (block + 1) % n_pair)
    x_down = (freq, (block + n_pair - 1) % n_pair)

    y_up, y_down = ((freq + 2) % n_freq, block), ((freq + n_freq - 2) % n_freq, block)
    f_up, f_down, f_far = (freq + 2) % n_freq, (freq + 6) % n_freq, (freq + 4) % n_freq

    def deriv_of(slot=OWN, of=core):
        return right.at[of, slot * pairs : (slot + 1) * pairs]

    barrier = pltpu.get_barrier_semaphore()
    peers = [((freq + o) % n_freq, block) for o in range(1, n_freq)] + [x_up, x_down]
    for peer in peers:
        pl.semaphore_signal(barrier, inc=1, device_id=peer, device_id_type=MESH)
    loads = [
        pltpu.make_async_copy(src, dst, local.at[i])
        for i, (src, dst) in enumerate(
            (
                (v_in, window.at[OWN, freq]),
                (sym_in, sym_ref),
                (s_in, s_ref),
                (u_in, u_ref),
                (map_s_in, map_s_ref),
                (map_u_in, map_u_ref),
                (prop_in, prop_ref),
                (left_in, left_ref),
                (right_in, right_ref),
                (len_in, len_ref),
            )
        )
    ]
    for load in loads:
        load.start()

    sent = []

    def push(src, dst, recv_sem, peer):
        copy = pltpu.make_async_remote_copy(
            src_ref=src,
            dst_ref=dst,
            send_sem=send.at[len(sent)],
            recv_sem=recv_sem,
            device_id=peer,
            device_id_type=MESH,
        )
        copy.start()
        sent.append(copy)

    def arrive(ref, recv_sem):
        pltpu.make_async_remote_copy(
            src_ref=ref,
            dst_ref=ref,
            send_sem=send.at[0],
            recv_sem=recv_sem,
            device_id=sibling,
            device_id_type=MESH,
        ).wait_recv()

    def send_vertex(slot, f, peer, to=None):
        to = slot if to is None else to
        push(window.at[slot, f], window.at[to, f], recv_vertex.at[to, f], peer)

    def send_vertex_x(f):
        send_vertex(OWN, f, x_up, BEFORE)
        send_vertex(OWN, f, x_down, AFTER)

    def vertex_arrives(slot, f):
        arrive(window.at[slot, f], recv_vertex.at[slot, f])

    def send_deriv(slot, peer, to=None):
        to = slot if to is None else to
        push(deriv_of(slot), deriv_of(to), recv_deriv.at[core, to], peer)

    n_packed = packed.shape[1]
    zero_rows = jnp.zeros((rows, nf), BF16)

    def pack_left():
        for g in range(n_packed):
            four = [
                window[OWN, freq, p] if p < pairs else zero_rows
                for p in range(n_chip * g, n_chip * (g + 1))
            ]
            for c, tile in enumerate(regroup(four)):
                packed[c, g] = tile
        spread[OWN, chip] = packed[chip]

    def send_left():
        for o in (2, 1, 3):
            c = (chip + o) % n_chip
            push(
                packed.at[c], spread.at[OWN, chip], recv_spread.at[chip], (2 * c + core, block)
            )

    def pass_left_on():
        for o in (1, 3, 2):
            c = (chip + o) % n_chip
            arrive(spread.at[OWN, c], recv_spread.at[c])
        push(spread.at[OWN], spread.at[BEFORE], recv_beside.at[BEFORE], x_up)
        push(spread.at[OWN], spread.at[AFTER], recv_beside.at[AFTER], x_down)

    loads[0].wait()
    pack_left()
    for load in loads[1:4]:
        load.wait()
    group = nf // rows
    n_groups = columns.shape[2]
    for kind in (0, 1):
        for g in range(n_groups):
            eight = []
            for p in range(g * group, (g + 1) * group):
                if p >= pairs:
                    eight.append(zero_rows)
                elif kind == 0:
                    eight.append(s_ref[p])
                else:
                    eight.append(u_ref[lax.rem(sym_ref[p], pairs)])
            for f, tile in enumerate(regroup(eight)):
                chunks[f, kind, g] = tile
    columns[freq] = chunks[freq]

    pl.semaphore_wait(barrier, len(peers))
    send_vertex_x(freq)
    send_left()
    for o in (4, 3, 5, 2, 6, 1, 7):
        f = (freq + o) % n_freq
        push(chunks.at[f], columns.at[freq], recv_cols.at[freq], (f, block))
    send_vertex(OWN, freq, y_up)
    send_vertex(OWN, freq, y_down)
    send_vertex(OWN, freq, sibling)

    for load in loads[4:]:
        load.wait()
    wide = lax.broadcasted_iota(jnp.int32, (nf, nf), 0)
    table[0:nf, :] = jnp.where(wide == map_s_ref[...], 1.0, 0.0).astype(BF16)
    table[nf : 2 * nf, :] = jnp.where(wide == map_u_ref[...], 1.0, 0.0).astype(BF16)

    width = nf // n_chip
    tile_lane = lax.broadcasted_iota(jnp.int32, (rows, nf), 1)
    wide_prop = jnp.broadcast_to(prop_ref[...], (rows, nf))
    tiles = regroup([wide_prop] * n_chip)
    prop = tiles[0]
    for c in range(1, n_chip):
        prop = jnp.where(chip == c, tiles[c], prop)

    lefts[0] = jnp.zeros(lefts.shape[1:], BF16)
    left_deriv[0] = zero_rows

    def fill_lefts(slot):
        def one(g, carry):
            for c in range(n_chip):
                tile = (spread[slot, c, g].astype(F32) * prop).astype(BF16)
                at = 1 + slot * n_packed + g
                lefts[at, c] = tile
                for k in range(1, n_chip):
                    lefts[at + k * (3 * n_packed), c] = pltpu.roll(tile, width * k, 1)
            return carry

        lax.fori_loop(0, n_packed, one, 0)

    def fill_deriv(slot):
        tall = right[core, slot * pairs : (slot + 1) * pairs].astype(F32) * prop_ref[...]
        left_deriv[1 + slot * pairs : 1 + (slot + 1) * pairs] = tall.astype(BF16)

    pass_left_on()

    window_first = (block - 1) * pairs
    row_id = lax.broadcasted_iota(jnp.int32, (pairs, slots), 0)
    slot_id = lax.broadcasted_iota(jnp.int32, (pairs, slots), 1)
    count = jnp.zeros((pairs, slots), jnp.int32)
    for r in range(pairs):
        count = jnp.where(row_id == r, len_ref[r], count)
    target = jnp.where(slot_id < count, right_ref[...] - window_first, -1)
    source = left_ref[...] - window_first
    plain = source + 1
    gap = n_chip * n_packed - pairs
    source = source + jnp.where(source >= pairs, gap, 0) + jnp.where(source >= 2 * pairs, gap, 0)
    lanes = lax.broadcasted_iota(jnp.int32, (pairs, nf), 1)
    chosen = jnp.full((pairs, nf), -1, jnp.int32)
    chosen_plain = jnp.zeros((pairs, nf), jnp.int32)
    for k in range(slots):
        hit = target[:, k : k + 1] == lanes
        chosen = jnp.where(hit, source[:, k : k + 1], chosen)
        chosen_plain = jnp.where(hit, plain[:, k : k + 1], chosen_plain)
    turn = (lanes - chosen) & (n_chip - 1)
    tile_id = 1 + turn * (3 * n_packed) + (chosen >> (n_chip.bit_length() - 1))
    tile_vec[...] = jnp.where(chosen < 0, 0, tile_id)
    sel_vec[...] = chosen_plain
    to_scalar = [
        pltpu.make_async_copy(sel_vec, sel, local.at[10]),
        pltpu.make_async_copy(tile_vec, tile_sel, local.at[11]),
    ]
    for copy in to_scalar:
        copy.start()

    for slot in (BEFORE, AFTER):
        vertex_arrives(slot, freq)
        send_vertex(slot, freq, y_down)
        send_vertex(slot, freq, sibling)
    fill_lefts(OWN)

    for o in range(1, n_freq):
        f = (freq + o) % n_freq
        arrive(columns.at[f], recv_cols.at[f])
    for g in range(n_groups):
        cols = jnp.concatenate([columns[:, kind, g].reshape(nf, nf) for kind in (0, 1)], axis=0)
        rows_t = lax.dot_general(
            cols, table[...], (((0,), (0,)), ((), ())), preferred_element_type=F32
        ).astype(BF16)
        n = min(group, pairs - g * group)
        start = OWN * pairs + g * group
        right[core, start : start + n] = rows_t.reshape(group, rows, nf)[:n]
    send_deriv(OWN, x_up, BEFORE)
    send_deriv(OWN, x_down, AFTER)
    send_deriv(OWN, sibling)

    vertex_arrives(OWN, f_down)
    send_vertex(OWN, f_down, y_up)
    send_vertex_x(f_down)
    send_vertex(OWN, f_down, sibling)
    vertex_arrives(OWN, f_up)
    send_vertex(OWN, f_up, sibling)
    fill_deriv(OWN)
    for slot in (BEFORE, AFTER):
        arrive(spread.at[slot], recv_beside.at[slot])
        fill_lefts(slot)
    for copy in to_scalar:
        copy.wait()

    tile_lanes = lax.broadcasted_iota(jnp.int32, (n_chip, rows, nf), 2)
    upper = tile_lanes >= 2 * width
    odd = (tile_lanes & width) != 0
    n_quads = factors.shape[0]

    def gather(t, carry):
        for r in range(pairs):
            one, two, three, four = (lefts[tile_sel[r, n_chip * t + s]] for s in range(n_chip))
            tile = jnp.where(upper, jnp.where(odd, four, three), jnp.where(odd, two, one))
            factors[t, r] = tile
        return carry

    lax.fori_loop(0, n_quads // 3, gather, 0)
    for slot in (BEFORE, AFTER):
        arrive(deriv_of(slot), recv_deriv.at[core, slot])
        send_deriv(slot, sibling)
        fill_deriv(slot)
    lax.fori_loop(n_quads // 3, 2 * n_quads // 3, gather, 0)
    vertex_arrives(OWN, f_far)
    send_vertex_x(f_far)
    send_vertex(OWN, f_far, sibling)
    lax.fori_loop(2 * n_quads // 3, n_quads, gather, 0)
    for slot in (BEFORE, AFTER):
        vertex_arrives(slot, f_up)
        send_vertex(slot, f_up, sibling)
    other = 1 - core
    for slot in (OWN, BEFORE, AFTER):
        arrive(deriv_of(slot, other), recv_deriv.at[other, slot])

    size = pairs // PARTS
    tall = n_chip * rows

    def part_copy(part, o):
        c = (chip + o) % n_chip
        return pltpu.make_async_remote_copy(
            src_ref=part_out.at[part, o],
            dst_ref=part_in.at[part, chip],
            send_sem=send_part.at[part, o],
            recv_sem=recv_part.at[part, chip],
            device_id=(2 * c + core, block),
            device_id_type=MESH,
        )

    def vertex_part(part, carry):
        here = pl.ds(part * size, size)
        lhs = [factors[t, here].reshape(size * tall, nf) for t in range(n_quads)]
        rhs = []
        for p in range(n_chip * n_quads):
            at = p if p < 3 * pairs else p - n_chip
            rhs.append(right[:, at].reshape(2 * rows, nf))
        rhs = [jnp.concatenate(rhs[n_chip * t : n_chip * (t + 1)], axis=0) for t in range(n_quads)]
        terms = product(lhs, rhs, size * tall // 2)
        sums[...] = terms.reshape(size, n_chip, rows, nf)
        vertex_sum[here] = sums[:, chip]
        for o in (2, 1, 3):
            part_out[part, o] = sums[:, (chip + o) % n_chip].astype(BF16)
            part_copy(part, o).start()
        return carry

    lax.fori_loop(0, PARTS // 2, vertex_part, 0)
    for slot in (BEFORE, AFTER):
        vertex_arrives(slot, f_down)
        send_vertex(slot, f_down, sibling)
    lax.fori_loop(PARTS // 2, PARTS, vertex_part, 0)

    half = pairs // 2

    def store_deriv(part):
        here = pl.ds(part * half, half)
        return pltpu.make_async_copy(deriv_sum.at[here], deriv_out.at[here], local.at[part])

    def add_deriv(slot, first=False, last=False):
        def one(part, carry):
            first_row = part * half
            lhs, rhs = [], []
            for p in range(pairs):
                q = slot * pairs + p
                lhs.append(
                    jnp.concatenate(
                        [left_deriv[sel[first_row + r, q]] for r in range(half)], axis=0
                    )
                )
                rhs.append(window[slot, :, p].reshape(nf, nf))
            terms = product(lhs, rhs, half // 2 * rows).reshape(half, rows, nf)
            here = pl.ds(first_row, half)
            deriv_sum[here] = terms if first else deriv_sum[here] + terms
            if last:
                store_deriv(part).start()
            return carry

        lax.fori_loop(0, 2, one, 0)

    def from_sibling(slot):
        for f in (0, 2, 4, 6):
            vertex_arrives(slot, (sibling[0] + f) % n_freq)

    from_sibling(OWN)
    add_deriv(OWN, first=True)
    for slot in (BEFORE, AFTER):
        vertex_arrives(slot, f_far)
        send_vertex(slot, f_far, sibling)
    from_sibling(BEFORE)
    add_deriv(BEFORE)

    for part in range(PARTS):
        at = slice(part * size, (part + 1) * size)
        total = vertex_sum[at]
        for o in (1, 3, 2):
            c = (chip + o) % n_chip
            arrive(part_in.at[part, c], recv_part.at[part, c])
            total = total + part_in[part, c].astype(F32)
        vertex_sum[at] = total
    store_vertex = pltpu.make_async_copy(vertex_sum, vertex_out, local.at[2])
    store_vertex.start()
    from_sibling(AFTER)
    add_deriv(AFTER, last=True)
    store_vertex.wait()
    for part in (0, 1):
        store_deriv(part).wait()
    for part in range(PARTS):
        for o in (2, 1, 3):
            part_copy(part, o).wait_send()
    for copy in sent:
        copy.wait_send()


def per_device(
    dims,
    vertex,
    deriv_s,
    deriv_u,
    freq_map_s,
    freq_map_u,
    pair_sym,
    propagator,
    left_pairs,
    right_pairs,
    lengths,
):
    n_freq, _ = dims
    n_chip = n_freq // 2
    pairs, rows, nf = vertex.shape
    n_groups = -(-pairs * rows // nf)
    n_packed = -(-pairs // n_chip)
    size = pairs // PARTS
    hbm = pl.BlockSpec(memory_space=pltpu.HBM)
    dma = pltpu.SemaphoreType.DMA
    vertex_sum, deriv_sum = pl.pallas_call(
        functools.partial(kernel, dims),
        out_shape=[jax.ShapeDtypeStruct((pairs, rows, nf), F32)] * 2,
        in_specs=[hbm] * 10,
        out_specs=[hbm] * 2,
        scratch_shapes=[
            pltpu.VMEM((pairs, rows, nf), BF16),
            pltpu.VMEM((pairs, rows, nf), BF16),
            pltpu.VMEM((1, nf), jnp.int32),
            pltpu.VMEM((1, nf), jnp.int32),
            pltpu.VMEM((1, nf), F32),
            pltpu.VMEM(left_pairs.shape, jnp.int32),
            pltpu.VMEM(right_pairs.shape, jnp.int32),
            pltpu.SMEM(pair_sym.shape, jnp.int32),
            pltpu.SMEM(lengths.shape, jnp.int32),
            pltpu.VMEM((3, n_freq, pairs, rows, nf), BF16),
            pltpu.VMEM((2, 3 * pairs, rows, nf), BF16),
            pltpu.VMEM((n_chip, n_packed, rows, nf), BF16),
            pltpu.VMEM((3, n_chip, n_packed, rows, nf), BF16),
            pltpu.VMEM((1 + n_chip * 3 * n_packed, n_chip, rows, nf), BF16),
            pltpu.VMEM((1 + 3 * pairs, rows, nf), BF16),
            pltpu.VMEM((-(-3 * pairs // n_chip), pairs, n_chip, rows, nf), BF16),
            pltpu.VMEM((n_freq, 2, n_groups, rows, nf), BF16),
            pltpu.VMEM((n_freq, 2, n_groups, rows, nf), BF16),
            pltpu.VMEM((2 * nf, nf), BF16),
            pltpu.VMEM((size, n_chip, rows, nf), F32),
            pltpu.VMEM((pairs, rows, nf), F32),
            pltpu.VMEM((pairs, rows, nf), F32),
            pltpu.VMEM((PARTS, n_chip, size, rows, nf), BF16),
            pltpu.VMEM((PARTS, n_chip, size, rows, nf), BF16),
            pltpu.VMEM((pairs, nf), jnp.int32),
            pltpu.SMEM((pairs, nf), jnp.int32),
            pltpu.VMEM((pairs, nf), jnp.int32),
            pltpu.SMEM((pairs, nf), jnp.int32),
            dma((3, n_freq)),
            dma((2, 3)),
            dma((n_chip,)),
            dma((3,)),
            dma((n_freq,)),
            dma((PARTS, n_chip)),
            dma((PARTS, n_chip)),
            dma((48,)),
            dma((12,)),
        ],
        compiler_params=pltpu.CompilerParams(
            collective_id=0, has_side_effects=True, vmem_limit_bytes=63 * 1024 * 1024
        ),
    )(
        vertex,
        jnp.swapaxes(deriv_s, 1, 2),
        jnp.swapaxes(deriv_u, 1, 2),
        freq_map_s.reshape(1, nf),
        freq_map_u.reshape(1, nf),
        propagator.reshape(1, nf),
        left_pairs,
        right_pairs,
        pair_sym,
        lengths,
    )
    return vertex_sum + deriv_sum


def solution(mesh):
    dims = (mesh.shape["freq"], mesh.shape["pair"])
    return jax.shard_map(
        functools.partial(per_device, dims),
        mesh=mesh,
        in_specs=(
            P("pair", "freq", None),
            P("pair", None, "freq"),
            P("pair", None, "freq"),
            P(),
            P(),
            P("pair"),
            P(),
            P("pair", None),
            P("pair", None),
            P("pair"),
        ),
        out_specs=P("pair", "freq", None),
        check_vma=False,
    )
```

```python
import functools

import jax
import jax.numpy as jnp
from jax import lax
from jax.experimental import pallas as pl
from jax.experimental.pallas import tpu as pltpu
from jax.sharding import PartitionSpec as P

MESH = pl.DeviceIdType.MESH
BF16 = jnp.bfloat16
F32 = jnp.float32

BEFORE, OWN, AFTER = 0, 1, 2
PARTS = 6


def regroup(parts):
    count = len(parts)
    rows, lanes = parts[0].shape
    width = lanes // count
    lane = lax.broadcasted_iota(jnp.int32, (rows, lanes), 1)
    parts = list(parts)
    step = 1
    while step < count:
        high = (lane & (width * step)) != 0
        for q in range(count):
            if (q // step) % 2 == 0:
                a, b = parts[q], parts[q + step]
                parts[q] = jnp.where(high, pltpu.roll(b, width * step, 1), a)
                parts[q + step] = jnp.where(high, b, pltpu.roll(a, lanes - width * step, 1))
        step *= 2
    return parts


def kernel(
    dims,
    v_in,
    s_in,
    u_in,
    map_s_in,
    map_u_in,
    prop_in,
    left_in,
    right_in,
    sym_in,
    len_in,
    out_ref,
    s_ref,
    u_ref,
    map_s_ref,
    map_u_ref,
    prop_ref,
    left_ref,
    right_ref,
    sym_ref,
    len_ref,
    window,
    right,
    packed,
    spread,
    lefts,
    left_deriv,
    factors,
    chunks,
    columns,
    table,
    sums,
    part_out,
    part_in,
    sel_vec,
    sel,
    tile_vec,
    tile_sel,
    recv_vertex,
    recv_deriv,
    recv_spread,
    recv_beside,
    recv_cols,
    recv_part,
    send_part,
    send,
    local,
):
    n_freq, n_pair = dims
    n_chip = n_freq // 2
    pairs, rows, nf = v_in.shape
    slots = left_ref.shape[1]
    freq, block = lax.axis_index("freq"), lax.axis_index("pair")
    chip, core = freq // 2, freq % 2

    sibling = (freq + 1 - 2 * core, block)
    x_up = (freq, (block + 1) % n_pair)
    x_down = (freq, (block + n_pair - 1) % n_pair)

    y_up, y_down = ((freq + 2) % n_freq, block), ((freq + n_freq - 2) % n_freq, block)
    f_up, f_down, f_far = (freq + 2) % n_freq, (freq + 6) % n_freq, (freq + 4) % n_freq

    def deriv_of(slot=OWN, of=core):
        return right.at[of, slot * pairs : (slot + 1) * pairs]

    barrier = pltpu.get_barrier_semaphore()
    peers = [((freq + o) % n_freq, block) for o in range(1, n_freq)] + [x_up, x_down]
    for peer in peers:
        pl.semaphore_signal(barrier, inc=1, device_id=peer, device_id_type=MESH)
    loads = [
        pltpu.make_async_copy(src, dst, local.at[i])
        for i, (src, dst) in enumerate(
            (
                (v_in, window.at[OWN, freq]),
                (sym_in, sym_ref),
                (s_in, s_ref),
                (u_in, u_ref),
                (map_s_in, map_s_ref),
                (map_u_in, map_u_ref),
                (prop_in, prop_ref),
                (left_in, left_ref),
                (right_in, right_ref),
                (len_in, len_ref),
            )
        )
    ]
    for load in loads:
        load.start()

    sent = []

    def push(src, dst, recv_sem, peer):
        copy = pltpu.make_async_remote_copy(
            src_ref=src,
            dst_ref=dst,
            send_sem=send.at[len(sent)],
            recv_sem=recv_sem,
            device_id=peer,
            device_id_type=MESH,
        )
        copy.start()
        sent.append(copy)

    def arrive(ref, recv_sem):
        pltpu.make_async_remote_copy(
            src_ref=ref,
            dst_ref=ref,
            send_sem=send.at[0],
            recv_sem=recv_sem,
            device_id=sibling,
            device_id_type=MESH,
        ).wait_recv()

    def send_vertex(slot, f, peer, to=None):
        to = slot if to is None else to
        push(window.at[slot, f], window.at[to, f], recv_vertex.at[to, f], peer)

    def send_vertex_x(f):
        send_vertex(OWN, f, x_up, BEFORE)
        send_vertex(OWN, f, x_down, AFTER)

    def vertex_arrives(slot, f):
        arrive(window.at[slot, f], recv_vertex.at[slot, f])

    def send_deriv(slot, peer, to=None):
        to = slot if to is None else to
        push(deriv_of(slot), deriv_of(to), recv_deriv.at[core, to], peer)

    n_packed = packed.shape[1]
    zero_rows = jnp.zeros((rows, nf), BF16)

    def pack_left():
        for g in range(n_packed):
            four = [
                window[OWN, freq, p] if p < pairs else zero_rows
                for p in range(n_chip * g, n_chip * (g + 1))
            ]
            for c, tile in enumerate(regroup(four)):
                packed[c, g] = tile
        spread[OWN, chip] = packed[chip]

    def send_left():
        for o in (2, 1, 3):
            c = (chip + o) % n_chip
            push(
                packed.at[c], spread.at[OWN, chip], recv_spread.at[chip], (2 * c + core, block)
            )

    def pass_left_on():
        for o in (1, 3, 2):
            c = (chip + o) % n_chip
            arrive(spread.at[OWN, c], recv_spread.at[c])
        push(spread.at[OWN], spread.at[BEFORE], recv_beside.at[BEFORE], x_up)
        push(spread.at[OWN], spread.at[AFTER], recv_beside.at[AFTER], x_down)

    loads[0].wait()
    pack_left()
    for load in loads[1:4]:
        load.wait()
    group = nf // rows
    n_groups = columns.shape[2]
    for kind in (0, 1):
        for g in range(n_groups):
            eight = []
            for p in range(g * group, (g + 1) * group):
                if p >= pairs:
                    eight.append(zero_rows)
                elif kind == 0:
                    eight.append(s_ref[p])
                else:
                    eight.append(u_ref[lax.rem(sym_ref[p], pairs)])
            for f, tile in enumerate(regroup(eight)):
                chunks[f, kind, g] = tile
    columns[freq] = chunks[freq]

    pl.semaphore_wait(barrier, len(peers))
    send_vertex_x(freq)
    send_left()
    for o in (4, 3, 5, 2, 6, 1, 7):
        f = (freq + o) % n_freq
        push(chunks.at[f], columns.at[freq], recv_cols.at[freq], (f, block))
    send_vertex(OWN, freq, y_up)
    send_vertex(OWN, freq, y_down)
    send_vertex(OWN, freq, sibling)

    for load in loads[4:]:
        load.wait()
    wide = lax.broadcasted_iota(jnp.int32, (nf, nf), 0)
    table[0:nf, :] = jnp.where(wide == map_s_ref[...], 1.0, 0.0).astype(BF16)
    table[nf : 2 * nf, :] = jnp.where(wide == map_u_ref[...], 1.0, 0.0).astype(BF16)

    width = nf // n_chip
    tile_lane = lax.broadcasted_iota(jnp.int32, (rows, nf), 1)
    wide_prop = jnp.broadcast_to(prop_ref[...], (rows, nf))
    tiles = regroup([wide_prop] * n_chip)
    prop = tiles[0]
    for c in range(1, n_chip):
        prop = jnp.where(chip == c, tiles[c], prop)

    lefts[0] = jnp.zeros(lefts.shape[1:], BF16)
    left_deriv[0] = zero_rows

    def fill_lefts(slot):
        def one(g, carry):
            for c in range(n_chip):
                tile = (spread[slot, c, g].astype(F32) * prop).astype(BF16)
                at = 1 + slot * n_packed + g
                lefts[at, c] = tile
                for k in range(1, n_chip):
                    lefts[at + k * (3 * n_packed), c] = pltpu.roll(tile, width * k, 1)
            return carry

        lax.fori_loop(0, n_packed, one, 0)

    def fill_deriv(slot):
        tall = right[core, slot * pairs : (slot + 1) * pairs].astype(F32) * prop_ref[...]
        left_deriv[1 + slot * pairs : 1 + (slot + 1) * pairs] = tall.astype(BF16)

    pass_left_on()

    window_first = (block - 1) * pairs
    row_id = lax.broadcasted_iota(jnp.int32, (pairs, slots), 0)
    slot_id = lax.broadcasted_iota(jnp.int32, (pairs, slots), 1)
    count = jnp.zeros((pairs, slots), jnp.int32)
    for r in range(pairs):
        count = jnp.where(row_id == r, len_ref[r], count)
    target = jnp.where(slot_id < count, right_ref[...] - window_first, -1)
    source = left_ref[...] - window_first
    plain = source + 1
    gap = n_chip * n_packed - pairs
    source = source + jnp.where(source >= pairs, gap, 0) + jnp.where(source >= 2 * pairs, gap, 0)
    lanes = lax.broadcasted_iota(jnp.int32, (pairs, nf), 1)
    chosen = jnp.full((pairs, nf), -1, jnp.int32)
    chosen_plain = jnp.zeros((pairs, nf), jnp.int32)
    for k in range(slots):
        hit = target[:, k : k + 1] == lanes
        chosen = jnp.where(hit, source[:, k : k + 1], chosen)
        chosen_plain = jnp.where(hit, plain[:, k : k + 1], chosen_plain)
    turn = (lanes - chosen) & (n_chip - 1)
    tile_id = 1 + turn * (3 * n_packed) + (chosen >> (n_chip.bit_length() - 1))
    tile_vec[...] = jnp.where(chosen < 0, 0, tile_id)
    sel_vec[...] = chosen_plain
    to_scalar = [
        pltpu.make_async_copy(sel_vec, sel, local.at[10]),
        pltpu.make_async_copy(tile_vec, tile_sel, local.at[11]),
    ]
    for copy in to_scalar:
        copy.start()

    for slot in (BEFORE, AFTER):
        vertex_arrives(slot, freq)
        send_vertex(slot, freq, y_down)
        send_vertex(slot, freq, sibling)
    fill_lefts(OWN)

    for o in range(1, n_freq):
        f = (freq + o) % n_freq
        arrive(columns.at[f], recv_cols.at[f])
    for g in range(n_groups):
        cols = jnp.concatenate([columns[:, kind, g].reshape(nf, nf) for kind in (0, 1)], axis=0)
        rows_t = lax.dot_general(
            cols, table[...], (((0,), (0,)), ((), ())), preferred_element_type=F32
        ).astype(BF16)
        n = min(group, pairs - g * group)
        start = OWN * pairs + g * group
        right[core, start : start + n] = rows_t.reshape(group, rows, nf)[:n]
    send_deriv(OWN, x_up, BEFORE)
    send_deriv(OWN, x_down, AFTER)
    send_deriv(OWN, sibling)

    vertex_arrives(OWN, f_down)
    send_vertex(OWN, f_down, y_up)
    send_vertex_x(f_down)
    send_vertex(OWN, f_down, sibling)
    vertex_arrives(OWN, f_up)
    send_vertex(OWN, f_up, sibling)
    fill_deriv(OWN)
    for slot in (BEFORE, AFTER):
        arrive(spread.at[slot], recv_beside.at[slot])
        fill_lefts(slot)
    for copy in to_scalar:
        copy.wait()

    n_quads = factors.shape[0]

    def gather(t, carry):
        for r in range(pairs):
            for s in range(n_chip):
                at = slice(s * width, (s + 1) * width)
                factors[t, r, :, :, at] = lefts[tile_sel[r, n_chip * t + s], :, :, at]
        return carry

    lax.fori_loop(0, n_quads // 3, gather, 0)
    for slot in (BEFORE, AFTER):
        arrive(deriv_of(slot), recv_deriv.at[core, slot])
        send_deriv(slot, sibling)
        fill_deriv(slot)
    lax.fori_loop(n_quads // 3, 2 * n_quads // 3, gather, 0)
    vertex_arrives(OWN, f_far)
    send_vertex_x(f_far)
    send_vertex(OWN, f_far, sibling)
    lax.fori_loop(2 * n_quads // 3, n_quads, gather, 0)
    for slot in (BEFORE, AFTER):
        vertex_arrives(slot, f_up)
        send_vertex(slot, f_up, sibling)
    other = 1 - core
    for slot in (OWN, BEFORE, AFTER):
        arrive(deriv_of(slot, other), recv_deriv.at[other, slot])

    size = pairs // PARTS
    tall = n_chip * rows

    def part_copy(part, o):
        c = (chip + o) % n_chip
        return pltpu.make_async_remote_copy(
            src_ref=part_out.at[part, o],
            dst_ref=part_in.at[part, chip],
            send_sem=send_part.at[part, o],
            recv_sem=recv_part.at[part, chip],
            device_id=(2 * c + core, block),
            device_id_type=MESH,
        )

    def vertex_part(part, carry):
        here = pl.ds(part * size, size)
        lhs = [factors[t, here].reshape(size * tall, nf) for t in range(n_quads)]
        rhs = []
        for p in range(n_chip * n_quads):
            at = p if p < 3 * pairs else p - n_chip
            rhs.append(right[:, at].reshape(2 * rows, nf))
        terms = jnp.dot(
            jnp.concatenate(lhs, axis=1),
            jnp.concatenate(rhs, axis=0),
            preferred_element_type=F32,
        )
        sums[...] = terms.reshape(size, n_chip, rows, nf)
        out_ref[here] = sums[:, chip]
        for o in (2, 1, 3):
            part_out[part, o] = sums[:, (chip + o) % n_chip].astype(BF16)
            part_copy(part, o).start()
        return carry

    lax.fori_loop(0, PARTS // 2, vertex_part, 0)
    for slot in (BEFORE, AFTER):
        vertex_arrives(slot, f_down)
        send_vertex(slot, f_down, sibling)
    lax.fori_loop(PARTS // 2, PARTS, vertex_part, 0)

    half = pairs // 2

    def add_deriv(slot):
        def one(part, carry):
            first_row = part * half
            lhs, rhs = [], []
            for p in range(pairs):
                q = slot * pairs + p
                lhs.append(
                    jnp.concatenate(
                        [left_deriv[sel[first_row + r, q]] for r in range(half)], axis=0
                    )
                )
                rhs.append(window[slot, :, p].reshape(nf, nf))
            terms = jnp.dot(
                jnp.concatenate(lhs, axis=1),
                jnp.concatenate(rhs, axis=0),
                preferred_element_type=F32,
            )
            out_ref[pl.ds(first_row, half)] += terms.reshape(half, rows, nf)
            return carry

        lax.fori_loop(0, 2, one, 0)

    def from_sibling(slot):
        for f in (0, 2, 4, 6):
            vertex_arrives(slot, (sibling[0] + f) % n_freq)

    from_sibling(OWN)
    add_deriv(OWN)
    for slot in (BEFORE, AFTER):
        vertex_arrives(slot, f_far)
        send_vertex(slot, f_far, sibling)
    for slot in (BEFORE, AFTER):
        from_sibling(slot)
        add_deriv(slot)
    for part in range(PARTS):
        at = slice(part * size, (part + 1) * size)
        total = out_ref[at]
        for o in (1, 3, 2):
            c = (chip + o) % n_chip
            arrive(part_in.at[part, c], recv_part.at[part, c])
            total = total + part_in[part, c].astype(F32)
        out_ref[at] = total
    for part in range(PARTS):
        for o in (2, 1, 3):
            part_copy(part, o).wait_send()
    for copy in sent:
        copy.wait_send()


def per_device(
    dims,
    vertex,
    deriv_s,
    deriv_u,
    freq_map_s,
    freq_map_u,
    pair_sym,
    propagator,
    left_pairs,
    right_pairs,
    lengths,
):
    n_freq, _ = dims
    n_chip = n_freq // 2
    pairs, rows, nf = vertex.shape
    n_groups = -(-pairs * rows // nf)
    n_packed = -(-pairs // n_chip)
    size = pairs // PARTS
    hbm = pl.BlockSpec(memory_space=pltpu.HBM)
    dma = pltpu.SemaphoreType.DMA
    return pl.pallas_call(
        functools.partial(kernel, dims),
        out_shape=jax.ShapeDtypeStruct((pairs, rows, nf), F32),
        in_specs=[hbm] * 10,
        out_specs=pl.BlockSpec(memory_space=pltpu.VMEM),
        scratch_shapes=[
            pltpu.VMEM((pairs, rows, nf), BF16),
            pltpu.VMEM((pairs, rows, nf), BF16),
            pltpu.VMEM((1, nf), jnp.int32),
            pltpu.VMEM((1, nf), jnp.int32),
            pltpu.VMEM((1, nf), F32),
            pltpu.VMEM(left_pairs.shape, jnp.int32),
            pltpu.VMEM(right_pairs.shape, jnp.int32),
            pltpu.SMEM(pair_sym.shape, jnp.int32),
            pltpu.SMEM(lengths.shape, jnp.int32),
            pltpu.VMEM((3, n_freq, pairs, rows, nf), BF16),
            pltpu.VMEM((2, 3 * pairs, rows, nf), BF16),
            pltpu.VMEM((n_chip, n_packed, rows, nf), BF16),
            pltpu.VMEM((3, n_chip, n_packed, rows, nf), BF16),
            pltpu.VMEM((1 + n_chip * 3 * n_packed, n_chip, rows, nf), BF16),
            pltpu.VMEM((1 + 3 * pairs, rows, nf), BF16),
            pltpu.VMEM((-(-3 * pairs // n_chip), pairs, n_chip, rows, nf), BF16),
            pltpu.VMEM((n_freq, 2, n_groups, rows, nf), BF16),
            pltpu.VMEM((n_freq, 2, n_groups, rows, nf), BF16),
            pltpu.VMEM((2 * nf, nf), BF16),
            pltpu.VMEM((size, n_chip, rows, nf), F32),
            pltpu.VMEM((PARTS, n_chip, size, rows, nf), BF16),
            pltpu.VMEM((PARTS, n_chip, size, rows, nf), BF16),
            pltpu.VMEM((pairs, nf), jnp.int32),
            pltpu.SMEM((pairs, nf), jnp.int32),
            pltpu.VMEM((pairs, nf), jnp.int32),
            pltpu.SMEM((pairs, nf), jnp.int32),
            dma((3, n_freq)),
            dma((2, 3)),
            dma((n_chip,)),
            dma((3,)),
            dma((n_freq,)),
            dma((PARTS, n_chip)),
            dma((PARTS, n_chip)),
            dma((48,)),
            dma((12,)),
        ],
        compiler_params=pltpu.CompilerParams(
            collective_id=0, has_side_effects=True, vmem_limit_bytes=63 * 1024 * 1024
        ),
    )(
        vertex,
        jnp.swapaxes(deriv_s, 1, 2),
        jnp.swapaxes(deriv_u, 1, 2),
        freq_map_s.reshape(1, nf),
        freq_map_u.reshape(1, nf),
        propagator.reshape(1, nf),
        left_pairs,
        right_pairs,
        pair_sym,
        lengths,
    )


def solution(mesh):
    dims = (mesh.shape["freq"], mesh.shape["pair"])
    return jax.shard_map(
        functools.partial(per_device, dims),
        mesh=mesh,
        in_specs=(
            P("pair", "freq", None),
            P("pair", None, "freq"),
            P("pair", None, "freq"),
            P(),
            P(),
            P("pair"),
            P(),
            P("pair", None),
            P("pair", None),
            P("pair"),
        ),
        out_specs=P("pair", "freq", None),
        check_vma=False,
    )
```

```python
import functools

import jax
import jax.numpy as jnp
from jax import lax
from jax.experimental import pallas as pl
from jax.experimental.pallas import tpu as pltpu
from jax.sharding import PartitionSpec as P

MESH = pl.DeviceIdType.MESH
BF16 = jnp.bfloat16
F32 = jnp.float32

BEFORE, OWN, AFTER = 0, 1, 2
PARTS = 6


def regroup(parts):
    count = len(parts)
    rows, lanes = parts[0].shape
    width = lanes // count
    lane = lax.broadcasted_iota(jnp.int32, (rows, lanes), 1)
    parts = list(parts)
    step = 1
    while step < count:
        high = (lane & (width * step)) != 0
        for q in range(count):
            if (q // step) % 2 == 0:
                a, b = parts[q], parts[q + step]
                parts[q] = jnp.where(high, pltpu.roll(b, width * step, 1), a)
                parts[q + step] = jnp.where(high, b, pltpu.roll(a, lanes - width * step, 1))
        step *= 2
    return parts


def kernel(
    dims,
    v_in,
    s_in,
    u_in,
    map_s_in,
    map_u_in,
    prop_in,
    left_in,
    right_in,
    sym_in,
    len_in,
    out_ref,
    s_ref,
    u_ref,
    map_s_ref,
    map_u_ref,
    prop_ref,
    left_ref,
    right_ref,
    sym_ref,
    len_ref,
    window,
    right,
    packed,
    spread,
    lefts,
    left_deriv,
    factors,
    chunks,
    columns,
    table,
    sums,
    part_out,
    part_in,
    sel_vec,
    sel,
    tile_vec,
    tile_sel,
    recv_vertex,
    recv_deriv,
    recv_spread,
    recv_beside,
    recv_cols,
    recv_part,
    send_part,
    send,
    local,
):
    n_freq, n_pair = dims
    n_chip = n_freq // 2
    pairs, rows, nf = v_in.shape
    slots = left_ref.shape[1]
    freq, block = lax.axis_index("freq"), lax.axis_index("pair")
    chip, core = freq // 2, freq % 2

    sibling = (freq + 1 - 2 * core, block)
    x_up = (freq, (block + 1) % n_pair)
    x_down = (freq, (block + n_pair - 1) % n_pair)

    y_up, y_down = ((freq + 2) % n_freq, block), ((freq + n_freq - 2) % n_freq, block)
    f_up, f_down, f_far = (freq + 2) % n_freq, (freq + 6) % n_freq, (freq + 4) % n_freq

    def deriv_of(slot=OWN, of=core):
        return right.at[of, slot * pairs : (slot + 1) * pairs]

    barrier = pltpu.get_barrier_semaphore()
    peers = [((freq + o) % n_freq, block) for o in range(1, n_freq)] + [x_up, x_down]
    for peer in peers:
        pl.semaphore_signal(barrier, inc=1, device_id=peer, device_id_type=MESH)
    loads = [
        pltpu.make_async_copy(src, dst, local.at[i])
        for i, (src, dst) in enumerate(
            (
                (v_in, window.at[OWN, freq]),
                (sym_in, sym_ref),
                (s_in, s_ref),
                (u_in, u_ref),
                (map_s_in, map_s_ref),
                (map_u_in, map_u_ref),
                (prop_in, prop_ref),
                (left_in, left_ref),
                (right_in, right_ref),
                (len_in, len_ref),
            )
        )
    ]
    for load in loads:
        load.start()

    sent = []

    def push(src, dst, recv_sem, peer):
        copy = pltpu.make_async_remote_copy(
            src_ref=src,
            dst_ref=dst,
            send_sem=send.at[len(sent)],
            recv_sem=recv_sem,
            device_id=peer,
            device_id_type=MESH,
        )
        copy.start()
        sent.append(copy)

    def arrive(ref, recv_sem):
        pltpu.make_async_remote_copy(
            src_ref=ref,
            dst_ref=ref,
            send_sem=send.at[0],
            recv_sem=recv_sem,
            device_id=sibling,
            device_id_type=MESH,
        ).wait_recv()

    def send_vertex(slot, f, peer, to=None):
        to = slot if to is None else to
        push(window.at[slot, f], window.at[to, f], recv_vertex.at[to, f], peer)

    def send_vertex_x(f):
        send_vertex(OWN, f, x_up, BEFORE)
        send_vertex(OWN, f, x_down, AFTER)

    def vertex_arrives(slot, f):
        arrive(window.at[slot, f], recv_vertex.at[slot, f])

    def send_deriv(slot, peer, to=None):
        to = slot if to is None else to
        push(deriv_of(slot), deriv_of(to), recv_deriv.at[core, to], peer)

    n_packed = packed.shape[1]
    zero_rows = jnp.zeros((rows, nf), BF16)

    def pack_left():
        for g in range(n_packed):
            four = [
                window[OWN, freq, p] if p < pairs else zero_rows
                for p in range(n_chip * g, n_chip * (g + 1))
            ]
            for c, tile in enumerate(regroup(four)):
                packed[c, g] = tile
        spread[OWN, chip] = packed[chip]

    def send_left():
        for o in (2, 1, 3):
            c = (chip + o) % n_chip
            push(
                packed.at[c], spread.at[OWN, chip], recv_spread.at[chip], (2 * c + core, block)
            )

    def pass_left_on(c):
        at = spread.at[OWN, c]
        push(at, spread.at[BEFORE, c], recv_beside.at[BEFORE, c], x_up)
        push(at, spread.at[AFTER, c], recv_beside.at[AFTER, c], x_down)

    loads[0].wait()
    pack_left()
    for load in loads[1:4]:
        load.wait()
    group = nf // rows
    n_groups = columns.shape[2]
    for kind in (0, 1):
        for g in range(n_groups):
            eight = []
            for p in range(g * group, (g + 1) * group):
                if p >= pairs:
                    eight.append(zero_rows)
                elif kind == 0:
                    eight.append(s_ref[p])
                else:
                    eight.append(u_ref[lax.rem(sym_ref[p], pairs)])
            for f, tile in enumerate(regroup(eight)):
                chunks[f, kind, g] = tile
    columns[freq] = chunks[freq]

    pl.semaphore_wait(barrier, len(peers))
    send_left()
    pass_left_on(chip)
    for o in (4, 3, 5, 2, 6, 1, 7):
        f = (freq + o) % n_freq
        push(chunks.at[f], columns.at[freq], recv_cols.at[freq], (f, block))
    send_vertex(OWN, freq, y_up)
    send_vertex(OWN, freq, y_down)
    send_vertex(OWN, freq, sibling)

    for load in loads[4:]:
        load.wait()
    wide = lax.broadcasted_iota(jnp.int32, (nf, nf), 0)
    table[0:nf, :] = jnp.where(wide == map_s_ref[...], 1.0, 0.0).astype(BF16)
    table[nf : 2 * nf, :] = jnp.where(wide == map_u_ref[...], 1.0, 0.0).astype(BF16)

    width = nf // n_chip
    tile_lane = lax.broadcasted_iota(jnp.int32, (rows, nf), 1)
    wide_prop = jnp.broadcast_to(prop_ref[...], (rows, nf))
    tiles = regroup([wide_prop] * n_chip)
    prop = tiles[0]
    for c in range(1, n_chip):
        prop = jnp.where(chip == c, tiles[c], prop)

    lefts[0] = jnp.zeros(lefts.shape[1:], BF16)
    left_deriv[0] = zero_rows

    def fill_lefts(slot):
        def one(g, carry):
            for c in range(n_chip):
                tile = (spread[slot, c, g].astype(F32) * prop).astype(BF16)
                at = 1 + slot * n_packed + g
                lefts[at, c] = tile
                for k in range(1, n_chip):
                    lefts[at + k * (3 * n_packed), c] = pltpu.roll(tile, width * k, 1)
            return carry

        lax.fori_loop(0, n_packed, one, 0)

    def fill_deriv(slot):
        tall = right[core, slot * pairs : (slot + 1) * pairs].astype(F32) * prop_ref[...]
        left_deriv[1 + slot * pairs : 1 + (slot + 1) * pairs] = tall.astype(BF16)

    for o in (1, 3, 2):
        c = (chip + o) % n_chip
        arrive(spread.at[OWN, c], recv_spread.at[c])
        pass_left_on(c)
    send_vertex_x(freq)

    window_first = (block - 1) * pairs
    row_id = lax.broadcasted_iota(jnp.int32, (pairs, slots), 0)
    slot_id = lax.broadcasted_iota(jnp.int32, (pairs, slots), 1)
    count = jnp.zeros((pairs, slots), jnp.int32)
    for r in range(pairs):
        count = jnp.where(row_id == r, len_ref[r], count)
    target = jnp.where(slot_id < count, right_ref[...] - window_first, -1)
    source = left_ref[...] - window_first
    plain = source + 1
    gap = n_chip * n_packed - pairs
    source = source + jnp.where(source >= pairs, gap, 0) + jnp.where(source >= 2 * pairs, gap, 0)
    lanes = lax.broadcasted_iota(jnp.int32, (pairs, nf), 1)
    chosen = jnp.full((pairs, nf), -1, jnp.int32)
    chosen_plain = jnp.zeros((pairs, nf), jnp.int32)
    for k in range(slots):
        hit = target[:, k : k + 1] == lanes
        chosen = jnp.where(hit, source[:, k : k + 1], chosen)
        chosen_plain = jnp.where(hit, plain[:, k : k + 1], chosen_plain)
    turn = (lanes - chosen) & (n_chip - 1)
    tile_id = 1 + turn * (3 * n_packed) + (chosen >> (n_chip.bit_length() - 1))
    tile_vec[...] = jnp.where(chosen < 0, 0, tile_id)
    sel_vec[...] = chosen_plain
    to_scalar = [
        pltpu.make_async_copy(sel_vec, sel, local.at[10]),
        pltpu.make_async_copy(tile_vec, tile_sel, local.at[11]),
    ]
    for copy in to_scalar:
        copy.start()

    fill_lefts(OWN)

    for o in range(1, n_freq):
        f = (freq + o) % n_freq
        arrive(columns.at[f], recv_cols.at[f])
    for g in range(n_groups):
        cols = jnp.concatenate([columns[:, kind, g].reshape(nf, nf) for kind in (0, 1)], axis=0)
        rows_t = lax.dot_general(
            cols, table[...], (((0,), (0,)), ((), ())), preferred_element_type=F32
        ).astype(BF16)
        n = min(group, pairs - g * group)
        start = OWN * pairs + g * group
        right[core, start : start + n] = rows_t.reshape(group, rows, nf)[:n]
    send_deriv(OWN, x_up, BEFORE)
    send_deriv(OWN, x_down, AFTER)
    send_deriv(OWN, sibling)

    fill_deriv(OWN)
    for slot in (BEFORE, AFTER):
        for o in (0, 1, 3, 2):
            c = (chip + o) % n_chip
            arrive(spread.at[slot, c], recv_beside.at[slot, c])
        fill_lefts(slot)
    for copy in to_scalar:
        copy.wait()

    tile_lanes = lax.broadcasted_iota(jnp.int32, (n_chip, rows, nf), 2)
    upper = tile_lanes >= 2 * width
    odd = (tile_lanes & width) != 0
    n_quads = factors.shape[0]

    def gather(t, carry):
        for r in range(pairs):
            one, two, three, four = (lefts[tile_sel[r, n_chip * t + s]] for s in range(n_chip))
            tile = jnp.where(upper, jnp.where(odd, four, three), jnp.where(odd, two, one))
            factors[t, r] = tile
        return carry

    cuts = [n_quads * piece // 23 for piece in (0, 4, 9, 14, 19, 23)]
    lax.fori_loop(cuts[0], cuts[1], gather, 0)
    vertex_arrives(OWN, f_down)
    send_vertex(OWN, f_down, y_up)
    send_vertex_x(f_down)
    send_vertex(OWN, f_down, sibling)
    vertex_arrives(OWN, f_up)
    send_vertex(OWN, f_up, sibling)
    lax.fori_loop(cuts[1], cuts[2], gather, 0)
    for slot in (BEFORE, AFTER):
        arrive(deriv_of(slot), recv_deriv.at[core, slot])
        send_deriv(slot, sibling)
        fill_deriv(slot)
    lax.fori_loop(cuts[2], cuts[3], gather, 0)
    for slot in (BEFORE, AFTER):
        vertex_arrives(slot, freq)
        send_vertex(slot, freq, y_down)
        send_vertex(slot, freq, sibling)
    lax.fori_loop(cuts[3], cuts[4], gather, 0)
    vertex_arrives(OWN, f_far)
    send_vertex_x(f_far)
    send_vertex(OWN, f_far, sibling)
    lax.fori_loop(cuts[4], cuts[5], gather, 0)
    other = 1 - core
    for slot in (OWN, BEFORE, AFTER):
        arrive(deriv_of(slot, other), recv_deriv.at[other, slot])

    size = pairs // PARTS
    tall = n_chip * rows

    def part_copy(part, o):
        c = (chip + o) % n_chip
        return pltpu.make_async_remote_copy(
            src_ref=part_out.at[part, o],
            dst_ref=part_in.at[part, chip],
            send_sem=send_part.at[part, o],
            recv_sem=recv_part.at[part, chip],
            device_id=(2 * c + core, block),
            device_id_type=MESH,
        )

    def vertex_part(part, carry):
        here = pl.ds(part * size, size)
        lhs = [factors[t, here].reshape(size * tall, nf) for t in range(n_quads)]
        rhs = []
        for p in range(n_chip * n_quads):
            at = p if p < 3 * pairs else p - n_chip
            rhs.append(right[:, at].reshape(2 * rows, nf))
        terms = jnp.dot(
            jnp.concatenate(lhs, axis=1),
            jnp.concatenate(rhs, axis=0),
            preferred_element_type=F32,
        )
        sums[...] = terms.reshape(size, n_chip, rows, nf)
        out_ref[here] = sums[:, chip]
        for o in (2, 1, 3):
            part_out[part, o] = sums[:, (chip + o) % n_chip].astype(BF16)
            part_copy(part, o).start()
        return carry

    lax.fori_loop(0, PARTS // 2, vertex_part, 0)
    for slot in (BEFORE, AFTER):
        for f in (f_down, f_up):
            vertex_arrives(slot, f)
            send_vertex(slot, f, sibling)
    lax.fori_loop(PARTS // 2, PARTS, vertex_part, 0)

    half = pairs // 2

    def add_deriv(slot):
        def one(part, carry):
            first_row = part * half
            lhs, rhs = [], []
            for p in range(pairs):
                q = slot * pairs + p
                lhs.append(
                    jnp.concatenate(
                        [left_deriv[sel[first_row + r, q]] for r in range(half)], axis=0
                    )
                )
                rhs.append(window[slot, :, p].reshape(nf, nf))
            terms = jnp.dot(
                jnp.concatenate(lhs, axis=1),
                jnp.concatenate(rhs, axis=0),
                preferred_element_type=F32,
            )
            out_ref[pl.ds(first_row, half)] += terms.reshape(half, rows, nf)
            return carry

        lax.fori_loop(0, 2, one, 0)

    def from_sibling(slot):
        for f in (0, 2, 4, 6):
            vertex_arrives(slot, (sibling[0] + f) % n_freq)

    from_sibling(OWN)
    add_deriv(OWN)
    for slot in (BEFORE, AFTER):
        vertex_arrives(slot, f_far)
        send_vertex(slot, f_far, sibling)
    for slot in (BEFORE, AFTER):
        from_sibling(slot)
        add_deriv(slot)
    for part in range(PARTS):
        at = slice(part * size, (part + 1) * size)
        total = out_ref[at]
        for o in (1, 3, 2):
            c = (chip + o) % n_chip
            arrive(part_in.at[part, c], recv_part.at[part, c])
            total = total + part_in[part, c].astype(F32)
        out_ref[at] = total
    for part in range(PARTS):
        for o in (2, 1, 3):
            part_copy(part, o).wait_send()
    for copy in sent:
        copy.wait_send()


def per_device(
    dims,
    vertex,
    deriv_s,
    deriv_u,
    freq_map_s,
    freq_map_u,
    pair_sym,
    propagator,
    left_pairs,
    right_pairs,
    lengths,
):
    n_freq, _ = dims
    n_chip = n_freq // 2
    pairs, rows, nf = vertex.shape
    n_groups = -(-pairs * rows // nf)
    n_packed = -(-pairs // n_chip)
    size = pairs // PARTS
    hbm = pl.BlockSpec(memory_space=pltpu.HBM)
    dma = pltpu.SemaphoreType.DMA
    return pl.pallas_call(
        functools.partial(kernel, dims),
        out_shape=jax.ShapeDtypeStruct((pairs, rows, nf), F32),
        in_specs=[hbm] * 10,
        out_specs=pl.BlockSpec(memory_space=pltpu.VMEM),
        scratch_shapes=[
            pltpu.VMEM((pairs, rows, nf), BF16),
            pltpu.VMEM((pairs, rows, nf), BF16),
            pltpu.VMEM((1, nf), jnp.int32),
            pltpu.VMEM((1, nf), jnp.int32),
            pltpu.VMEM((1, nf), F32),
            pltpu.VMEM(left_pairs.shape, jnp.int32),
            pltpu.VMEM(right_pairs.shape, jnp.int32),
            pltpu.SMEM(pair_sym.shape, jnp.int32),
            pltpu.SMEM(lengths.shape, jnp.int32),
            pltpu.VMEM((3, n_freq, pairs, rows, nf), BF16),
            pltpu.VMEM((2, 3 * pairs, rows, nf), BF16),
            pltpu.VMEM((n_chip, n_packed, rows, nf), BF16),
            pltpu.VMEM((3, n_chip, n_packed, rows, nf), BF16),
            pltpu.VMEM((1 + n_chip * 3 * n_packed, n_chip, rows, nf), BF16),
            pltpu.VMEM((1 + 3 * pairs, rows, nf), BF16),
            pltpu.VMEM((-(-3 * pairs // n_chip), pairs, n_chip, rows, nf), BF16),
            pltpu.VMEM((n_freq, 2, n_groups, rows, nf), BF16),
            pltpu.VMEM((n_freq, 2, n_groups, rows, nf), BF16),
            pltpu.VMEM((2 * nf, nf), BF16),
            pltpu.VMEM((size, n_chip, rows, nf), F32),
            pltpu.VMEM((PARTS, n_chip, size, rows, nf), BF16),
            pltpu.VMEM((PARTS, n_chip, size, rows, nf), BF16),
            pltpu.VMEM((pairs, nf), jnp.int32),
            pltpu.SMEM((pairs, nf), jnp.int32),
            pltpu.VMEM((pairs, nf), jnp.int32),
            pltpu.SMEM((pairs, nf), jnp.int32),
            dma((3, n_freq)),
            dma((2, 3)),
            dma((n_chip,)),
            dma((3, n_chip)),
            dma((n_freq,)),
            dma((PARTS, n_chip)),
            dma((PARTS, n_chip)),
            dma((48,)),
            dma((12,)),
        ],
        compiler_params=pltpu.CompilerParams(
            collective_id=0, has_side_effects=True, vmem_limit_bytes=63 * 1024 * 1024
        ),
    )(
        vertex,
        jnp.swapaxes(deriv_s, 1, 2),
        jnp.swapaxes(deriv_u, 1, 2),
        freq_map_s.reshape(1, nf),
        freq_map_u.reshape(1, nf),
        propagator.reshape(1, nf),
        left_pairs,
        right_pairs,
        pair_sym,
        lengths,
    )


def solution(mesh):
    dims = (mesh.shape["freq"], mesh.shape["pair"])
    return jax.shard_map(
        functools.partial(per_device, dims),
        mesh=mesh,
        in_specs=(
            P("pair", "freq", None),
            P("pair", None, "freq"),
            P("pair", None, "freq"),
            P(),
            P(),
            P("pair"),
            P(),
            P("pair", None),
            P("pair", None),
            P("pair"),
        ),
        out_specs=P("pair", "freq", None),
        check_vma=False,
    )
```

```python
import functools

import jax
import jax.numpy as jnp
from jax import lax
from jax.experimental import pallas as pl
from jax.experimental.pallas import tpu as pltpu
from jax.sharding import PartitionSpec as P

MESH = pl.DeviceIdType.MESH
BF16 = jnp.bfloat16
F32 = jnp.float32

BEFORE, OWN, AFTER = 0, 1, 2
VERTEX, DERIV = 0, 1
PARTS = 6


def regroup(parts):
    count = len(parts)
    rows, lanes = parts[0].shape
    width = lanes // count
    lane = lax.broadcasted_iota(jnp.int32, (rows, lanes), 1)
    parts = list(parts)
    step = 1
    while step < count:
        high = (lane & (width * step)) != 0
        for q in range(count):
            if (q // step) % 2 == 0:
                a, b = parts[q], parts[q + step]
                parts[q] = jnp.where(high, pltpu.roll(b, width * step, 1), a)
                parts[q + step] = jnp.where(high, b, pltpu.roll(a, lanes - width * step, 1))
        step *= 2
    return parts


def kernel(
    dims,
    v_in,
    s_in,
    u_in,
    map_s_in,
    map_u_in,
    prop_in,
    left_in,
    right_in,
    sym_in,
    len_in,
    out,
    s_ref,
    u_ref,
    map_s_ref,
    map_u_ref,
    prop_ref,
    left_ref,
    right_ref,
    sym_ref,
    len_ref,
    out_ref,
    right,
    packed,
    spread,
    lefts,
    chunks,
    columns,
    table,
    sums,
    part_out,
    part_in,
    sel_vec,
    sel,
    recv_right,
    recv_spread,
    recv_beside,
    recv_cols,
    recv_part,
    send_part,
    send,
    local,
):
    n_freq, n_pair = dims
    n_chip = n_freq // 2
    pairs, rows, nf = v_in.shape
    slots = left_ref.shape[1]
    freq, block = lax.axis_index("freq"), lax.axis_index("pair")
    chip, core = freq // 2, freq % 2

    sibling = (freq + 1 - 2 * core, block)
    x_up = (freq, (block + 1) % n_pair)
    x_down = (freq, (block + n_pair - 1) % n_pair)

    def own(kind, slot=OWN, of=core):
        return right.at[kind, of, slot * pairs : (slot + 1) * pairs]

    barrier = pltpu.get_barrier_semaphore()
    peers = [((freq + o) % n_freq, block) for o in range(1, n_freq)] + [x_up, x_down]
    for peer in peers:
        pl.semaphore_signal(barrier, inc=1, device_id=peer, device_id_type=MESH)
    loads = [
        pltpu.make_async_copy(src, dst, local.at[i])
        for i, (src, dst) in enumerate(
            (
                (v_in, own(VERTEX)),
                (sym_in, sym_ref),
                (s_in, s_ref),
                (u_in, u_ref),
                (map_s_in, map_s_ref),
                (map_u_in, map_u_ref),
                (prop_in, prop_ref),
                (left_in, left_ref),
                (right_in, right_ref),
                (len_in, len_ref),
            )
        )
    ]
    for load in loads:
        load.start()

    sent = []

    def push(src, dst, recv_sem, peer):
        copy = pltpu.make_async_remote_copy(
            src_ref=src,
            dst_ref=dst,
            send_sem=send.at[len(sent)],
            recv_sem=recv_sem,
            device_id=peer,
            device_id_type=MESH,
        )
        copy.start()
        sent.append(copy)

    def arrive(ref, recv_sem):
        pltpu.make_async_remote_copy(
            src_ref=ref,
            dst_ref=ref,
            send_sem=send.at[0],
            recv_sem=recv_sem,
            device_id=sibling,
            device_id_type=MESH,
        ).wait_recv()

    def push_beside(kind):
        push(own(kind), own(kind, BEFORE), recv_right.at[kind, core, BEFORE], x_up)
        push(own(kind), own(kind, AFTER), recv_right.at[kind, core, AFTER], x_down)

    def push_sibling(kind, slot):
        push(own(kind, slot), own(kind, slot), recv_right.at[kind, core, slot], sibling)

    n_packed = packed.shape[2]
    zero_rows = jnp.zeros((rows, nf), BF16)

    def pack_left(kind):
        for g in range(n_packed):
            four = [
                right[kind, core, OWN * pairs + p] if p < pairs else zero_rows
                for p in range(n_chip * g, n_chip * (g + 1))
            ]
            for c, tile in enumerate(regroup(four)):
                packed[kind, c, g] = tile
        spread[OWN, kind, chip] = packed[kind, chip]

    def push_left(kind):
        for o in (2, 1, 3):
            c = (chip + o) % n_chip
            push(
                packed.at[kind, c],
                spread.at[OWN, kind, chip],
                recv_spread.at[kind, chip],
                (2 * c + core, block),
            )

    def pass_chunk_on(kind, c):
        at = spread.at[OWN, kind, c]
        push(at, spread.at[BEFORE, kind, c], recv_beside.at[kind, BEFORE, c], x_up)
        push(at, spread.at[AFTER, kind, c], recv_beside.at[kind, AFTER, c], x_down)

    def pass_left_on(kind):
        for o in (1, 3, 2):
            c = (chip + o) % n_chip
            arrive(spread.at[OWN, kind, c], recv_spread.at[kind, c])
            pass_chunk_on(kind, c)

    def left_arrives(kind, slot):
        for o in (0, 1, 3, 2):
            c = (chip + o) % n_chip
            arrive(spread.at[slot, kind, c], recv_beside.at[kind, slot, c])

    loads[0].wait()
    pack_left(VERTEX)
    for load in loads[1:4]:
        load.wait()
    group = nf // rows
    n_groups = columns.shape[2]
    for kind in (0, 1):
        for g in range(n_groups):
            eight = []
            for p in range(g * group, (g + 1) * group):
                if p >= pairs:
                    eight.append(zero_rows)
                elif kind == 0:
                    eight.append(s_ref[p])
                else:
                    eight.append(u_ref[lax.rem(sym_ref[p], pairs)])
            for f, tile in enumerate(regroup(eight)):
                chunks[f, kind, g] = tile
    columns[freq] = chunks[freq]

    pl.semaphore_wait(barrier, len(peers))
    push_left(VERTEX)
    push_beside(VERTEX)
    pass_chunk_on(VERTEX, chip)
    for o in (4, 3, 5, 2, 6, 1, 7):
        f = (freq + o) % n_freq
        push(chunks.at[f], columns.at[freq], recv_cols.at[freq], (f, block))
    push_sibling(VERTEX, OWN)

    for load in loads[4:]:
        load.wait()
    wide = lax.broadcasted_iota(jnp.int32, (nf, nf), 0)
    table[0:nf, :] = jnp.where(wide == map_s_ref[...], 1.0, 0.0).astype(BF16)
    table[nf : 2 * nf, :] = jnp.where(wide == map_u_ref[...], 1.0, 0.0).astype(BF16)
    window_first = (block - 1) * pairs
    row_id = lax.broadcasted_iota(jnp.int32, (pairs, slots), 0)
    slot_id = lax.broadcasted_iota(jnp.int32, (pairs, slots), 1)
    count = jnp.zeros((pairs, slots), jnp.int32)
    for r in range(pairs):
        count = jnp.where(row_id == r, len_ref[r], count)
    target = jnp.where(slot_id < count, right_ref[...] - window_first, -1)
    source = left_ref[...] - window_first
    stride = n_chip * n_packed
    gap = stride - pairs
    source = source + 1 + jnp.where(source >= pairs, gap, 0) + jnp.where(source >= 2 * pairs, gap, 0)
    lanes = lax.broadcasted_iota(jnp.int32, (pairs, nf), 1)
    chosen = jnp.zeros((pairs, nf), jnp.int32)
    for k in range(slots):
        chosen = jnp.where(target[:, k : k + 1] == lanes, source[:, k : k + 1], chosen)
    sel_vec[...] = chosen
    to_scalar = pltpu.make_async_copy(sel_vec, sel, local.at[10])
    to_scalar.start()

    width = nf // n_chip
    tile_lane = lax.broadcasted_iota(jnp.int32, (rows, nf), 1)
    wide_prop = jnp.broadcast_to(prop_ref[...], (rows, nf))
    tiles = regroup([wide_prop] * n_chip)
    prop = tiles[0]
    for c in range(1, n_chip):
        prop = jnp.where(chip == c, tiles[c], prop)

    for half in (0, 1):
        lefts[half, 0] = jnp.zeros(lefts.shape[2:], BF16)
    zones = [
        (tile_lane >= width * z) & (tile_lane < width * (z + 1)) for z in range(n_chip)
    ]

    def fill_lefts(kind, slot):
        def one(g, carry):
            for c in range(n_chip):
                tile = (spread[slot, kind, c, g].astype(F32) * prop).astype(BF16)
                turned = [tile] + [pltpu.roll(tile, width * k, 1) for k in range(1, n_chip)]
                for q in range(n_chip):
                    at = 1 + slot * stride + g * n_chip + q
                    for half in (0, 1):
                        zone = 2 * half + kind
                        rest = jnp.zeros((rows, nf), BF16) if kind == VERTEX else lefts[half, at, c]
                        lefts[half, at, c] = jnp.where(zones[zone], turned[(zone - q) % n_chip], rest)
            return carry

        lax.fori_loop(0, n_packed, one, 0)

    pass_left_on(VERTEX)

    for o in range(1, n_freq):
        f = (freq + o) % n_freq
        arrive(columns.at[f], recv_cols.at[f])
    for g in range(n_groups):
        cols = jnp.concatenate([columns[:, kind, g].reshape(nf, nf) for kind in (0, 1)], axis=0)
        rows_t = lax.dot_general(
            cols, table[...], (((0,), (0,)), ((), ())), preferred_element_type=F32
        ).astype(BF16)
        n = min(group, pairs - g * group)
        start = OWN * pairs + g * group
        right[DERIV, core, start : start + n] = rows_t.reshape(group, rows, nf)[:n]
    pack_left(DERIV)
    push_left(DERIV)
    pass_chunk_on(DERIV, chip)
    push_beside(DERIV)
    push_sibling(DERIV, OWN)

    for slot in (BEFORE, AFTER):
        arrive(own(VERTEX, slot), recv_right.at[VERTEX, core, slot])
        push_sibling(VERTEX, slot)
    fill_lefts(VERTEX, OWN)
    for slot in (BEFORE, AFTER):
        left_arrives(VERTEX, slot)
        fill_lefts(VERTEX, slot)

    pass_left_on(DERIV)
    fill_lefts(DERIV, OWN)
    for slot in (BEFORE, AFTER):
        arrive(own(DERIV, slot), recv_right.at[DERIV, core, slot])
        push_sibling(DERIV, slot)
    for slot in (BEFORE, AFTER):
        left_arrives(DERIV, slot)
        fill_lefts(DERIV, slot)
    other = 1 - core
    for slot in (OWN, BEFORE, AFTER):
        for kind in (VERTEX, DERIV):
            arrive(own(kind, slot, other), recv_right.at[kind, other, slot])

    to_scalar.wait()
    size = pairs // PARTS
    tall = n_chip * rows

    def part_copy(part, o):
        c = (chip + o) % n_chip
        return pltpu.make_async_remote_copy(
            src_ref=part_out.at[part, o],
            dst_ref=part_in.at[part, chip],
            send_sem=send_part.at[part, o],
            recv_sem=recv_part.at[part, chip],
            device_id=(2 * c + core, block),
            device_id_type=MESH,
        )

    def one_part(part, carry):
        first_row = part * size
        lhs, rhs = [], []
        for q in range(0, 3 * pairs, 2):
            lhs.append(
                jnp.concatenate(
                    [
                        (
                            lefts[0, sel[first_row + r, q]] + lefts[1, sel[first_row + r, q + 1]]
                        ).reshape(tall, nf)
                        for r in range(size)
                    ],
                    axis=0,
                )
            )
            for p in (q, q + 1):
                rhs += [right[kind, :, p].reshape(2 * rows, nf) for kind in (DERIV, VERTEX)]
        terms = jnp.dot(
            jnp.concatenate(lhs, axis=1),
            jnp.concatenate(rhs, axis=0),
            preferred_element_type=F32,
        )
        sums[...] = terms.reshape(size, n_chip, rows, nf)
        out_ref[pl.ds(first_row, size)] = sums[:, chip]
        for o in (2, 1, 3):
            part_out[part, o] = sums[:, (chip + o) % n_chip].astype(BF16)
            part_copy(part, o).start()
        return carry

    lax.fori_loop(0, PARTS, one_part, 0)
    stores = []
    for part in range(PARTS):
        at = slice(part * size, (part + 1) * size)
        total = out_ref[at]
        for o in (1, 3, 2):
            c = (chip + o) % n_chip
            arrive(part_in.at[part, c], recv_part.at[part, c])
            total = total + part_in[part, c].astype(F32)
        out_ref[at] = total
        stores.append(pltpu.make_async_copy(out_ref.at[at], out.at[at], local.at[part]))
        stores[-1].start()
    for part in range(PARTS):
        for o in (2, 1, 3):
            part_copy(part, o).wait_send()
    for store in stores:
        store.wait()
    for copy in sent:
        copy.wait_send()


def per_device(
    dims,
    vertex,
    deriv_s,
    deriv_u,
    freq_map_s,
    freq_map_u,
    pair_sym,
    propagator,
    left_pairs,
    right_pairs,
    lengths,
):
    n_freq, _ = dims
    n_chip = n_freq // 2
    pairs, rows, nf = vertex.shape
    n_groups = -(-pairs * rows // nf)
    n_packed = -(-pairs // n_chip)
    size = pairs // PARTS
    hbm = pl.BlockSpec(memory_space=pltpu.HBM)
    dma = pltpu.SemaphoreType.DMA
    return pl.pallas_call(
        functools.partial(kernel, dims),
        out_shape=jax.ShapeDtypeStruct((pairs, rows, nf), F32),
        in_specs=[hbm] * 10,
        out_specs=hbm,
        scratch_shapes=[
            pltpu.VMEM((pairs, rows, nf), BF16),
            pltpu.VMEM((pairs, rows, nf), BF16),
            pltpu.VMEM((1, nf), jnp.int32),
            pltpu.VMEM((1, nf), jnp.int32),
            pltpu.VMEM((1, nf), F32),
            pltpu.VMEM(left_pairs.shape, jnp.int32),
            pltpu.VMEM(right_pairs.shape, jnp.int32),
            pltpu.SMEM(pair_sym.shape, jnp.int32),
            pltpu.SMEM(lengths.shape, jnp.int32),
            pltpu.VMEM((pairs, rows, nf), F32),
            pltpu.VMEM((2, 2, 3 * pairs, rows, nf), BF16),
            pltpu.VMEM((2, n_chip, n_packed, rows, nf), BF16),
            pltpu.VMEM((3, 2, n_chip, n_packed, rows, nf), BF16),
            pltpu.VMEM((2, 1 + 3 * n_packed * n_chip, n_chip, rows, nf), BF16),
            pltpu.VMEM((n_freq, 2, n_groups, rows, nf), BF16),
            pltpu.VMEM((n_freq, 2, n_groups, rows, nf), BF16),
            pltpu.VMEM((2 * nf, nf), BF16),
            pltpu.VMEM((size, n_chip, rows, nf), F32),
            pltpu.VMEM((PARTS, n_chip, size, rows, nf), BF16),
            pltpu.VMEM((PARTS, n_chip, size, rows, nf), BF16),
            pltpu.VMEM((pairs, nf), jnp.int32),
            pltpu.SMEM((pairs, nf), jnp.int32),
            dma((2, 2, 3)),
            dma((2, n_chip)),
            dma((2, 3, n_chip)),
            dma((n_freq,)),
            dma((PARTS, n_chip)),
            dma((PARTS, n_chip)),
            dma((64,)),
            dma((11,)),
        ],
        compiler_params=pltpu.CompilerParams(
            collective_id=0, has_side_effects=True, vmem_limit_bytes=63 * 1024 * 1024
        ),
    )(
        vertex,
        jnp.swapaxes(deriv_s, 1, 2),
        jnp.swapaxes(deriv_u, 1, 2),
        freq_map_s.reshape(1, nf),
        freq_map_u.reshape(1, nf),
        propagator.reshape(1, nf),
        left_pairs,
        right_pairs,
        pair_sym,
        lengths,
    )


def solution(mesh):
    dims = (mesh.shape["freq"], mesh.shape["pair"])
    return jax.shard_map(
        functools.partial(per_device, dims),
        mesh=mesh,
        in_specs=(
            P("pair", "freq", None),
            P("pair", None, "freq"),
            P("pair", None, "freq"),
            P(),
            P(),
            P("pair"),
            P(),
            P("pair", None),
            P("pair", None),
            P("pair"),
        ),
        out_specs=P("pair", "freq", None),
        check_vma=False,
    )
```

```python
import functools

import jax
import jax.numpy as jnp
from jax import lax
from jax.experimental import pallas as pl
from jax.experimental.pallas import tpu as pltpu
from jax.sharding import PartitionSpec as P

MESH = pl.DeviceIdType.MESH
BF16 = jnp.bfloat16
F32 = jnp.float32

BEFORE, OWN, AFTER = 0, 1, 2
VERTEX, DERIV = 0, 1
PARTS = 6


def regroup(parts):
    count = len(parts)
    rows, lanes = parts[0].shape
    width = lanes // count
    lane = lax.broadcasted_iota(jnp.int32, (rows, lanes), 1)
    parts = list(parts)
    step = 1
    while step < count:
        high = (lane & (width * step)) != 0
        for q in range(count):
            if (q // step) % 2 == 0:
                a, b = parts[q], parts[q + step]
                parts[q] = jnp.where(high, pltpu.roll(b, width * step, 1), a)
                parts[q + step] = jnp.where(high, b, pltpu.roll(a, lanes - width * step, 1))
        step *= 2
    return parts


def kernel(
    dims,
    v_in,
    s_in,
    u_in,
    map_s_in,
    map_u_in,
    prop_in,
    left_in,
    right_in,
    sym_in,
    len_in,
    out,
    s_ref,
    u_ref,
    map_s_ref,
    map_u_ref,
    prop_ref,
    left_ref,
    right_ref,
    sym_ref,
    len_ref,
    out_ref,
    right,
    packed,
    spread,
    lefts,
    chunks,
    columns,
    table,
    sums,
    part_out,
    part_in,
    sel_vec,
    sel,
    recv_right,
    recv_spread,
    recv_beside,
    recv_cols,
    recv_part,
    send_part,
    send,
    local,
):
    n_freq, n_pair = dims
    n_chip = n_freq // 2
    pairs, rows, nf = v_in.shape
    slots = left_ref.shape[1]
    freq, block = lax.axis_index("freq"), lax.axis_index("pair")
    chip, core = freq // 2, freq % 2

    sibling = (freq + 1 - 2 * core, block)
    x_up = (freq, (block + 1) % n_pair)
    x_down = (freq, (block + n_pair - 1) % n_pair)

    def own(kind, slot=OWN, of=core):
        return right.at[kind, of, slot * pairs : (slot + 1) * pairs]

    barrier = pltpu.get_barrier_semaphore()
    peers = [((freq + o) % n_freq, block) for o in range(1, n_freq)] + [x_up, x_down]
    for peer in peers:
        pl.semaphore_signal(barrier, inc=1, device_id=peer, device_id_type=MESH)
    loads = [
        pltpu.make_async_copy(src, dst, local.at[i])
        for i, (src, dst) in enumerate(
            (
                (v_in, own(VERTEX)),
                (sym_in, sym_ref),
                (s_in, s_ref),
                (u_in, u_ref),
                (map_s_in, map_s_ref),
                (map_u_in, map_u_ref),
                (prop_in, prop_ref),
                (left_in, left_ref),
                (right_in, right_ref),
                (len_in, len_ref),
            )
        )
    ]
    for load in loads:
        load.start()

    sent = []

    def push(src, dst, recv_sem, peer):
        copy = pltpu.make_async_remote_copy(
            src_ref=src,
            dst_ref=dst,
            send_sem=send.at[len(sent)],
            recv_sem=recv_sem,
            device_id=peer,
            device_id_type=MESH,
        )
        copy.start()
        sent.append(copy)

    def arrive(ref, recv_sem):
        pltpu.make_async_remote_copy(
            src_ref=ref,
            dst_ref=ref,
            send_sem=send.at[0],
            recv_sem=recv_sem,
            device_id=sibling,
            device_id_type=MESH,
        ).wait_recv()

    def push_beside(kind):
        push(own(kind), own(kind, BEFORE), recv_right.at[kind, core, BEFORE], x_up)
        push(own(kind), own(kind, AFTER), recv_right.at[kind, core, AFTER], x_down)

    def push_sibling(kind, slot):
        push(own(kind, slot), own(kind, slot), recv_right.at[kind, core, slot], sibling)

    n_packed = packed.shape[2]
    zero_rows = jnp.zeros((rows, nf), BF16)

    def pack_left(kind):
        for g in range(n_packed):
            four = [
                right[kind, core, OWN * pairs + p] if p < pairs else zero_rows
                for p in range(n_chip * g, n_chip * (g + 1))
            ]
            for c, tile in enumerate(regroup(four)):
                packed[kind, c, g] = tile
        spread[OWN, kind, chip] = packed[kind, chip]

    def push_left(kind):
        for o in (2, 1, 3):
            c = (chip + o) % n_chip
            push(
                packed.at[kind, c],
                spread.at[OWN, kind, chip],
                recv_spread.at[kind, chip],
                (2 * c + core, block),
            )

    def pass_chunk_on(kind, c):
        at = spread.at[OWN, kind, c]
        push(at, spread.at[BEFORE, kind, c], recv_beside.at[kind, BEFORE, c], x_up)
        push(at, spread.at[AFTER, kind, c], recv_beside.at[kind, AFTER, c], x_down)

    def pass_left_on(kind):
        for o in (1, 3, 2):
            c = (chip + o) % n_chip
            arrive(spread.at[OWN, kind, c], recv_spread.at[kind, c])
            pass_chunk_on(kind, c)

    loads[0].wait()
    pack_left(VERTEX)
    for load in loads[1:4]:
        load.wait()
    group = nf // rows
    n_groups = columns.shape[2]
    for kind in (0, 1):
        for g in range(n_groups):
            eight = []
            for p in range(g * group, (g + 1) * group):
                if p >= pairs:
                    eight.append(zero_rows)
                elif kind == 0:
                    eight.append(s_ref[p])
                else:
                    eight.append(u_ref[lax.rem(sym_ref[p], pairs)])
            for f, tile in enumerate(regroup(eight)):
                chunks[f, kind, g] = tile
    columns[freq] = chunks[freq]

    pl.semaphore_wait(barrier, len(peers))
    push_left(VERTEX)
    push_beside(VERTEX)
    pass_chunk_on(VERTEX, chip)
    for o in (4, 3, 5, 2, 6, 1, 7):
        f = (freq + o) % n_freq
        push(chunks.at[f], columns.at[freq], recv_cols.at[freq], (f, block))
    push_sibling(VERTEX, OWN)

    for load in loads[4:]:
        load.wait()
    wide = lax.broadcasted_iota(jnp.int32, (nf, nf), 0)
    table[0:nf, :] = jnp.where(wide == map_s_ref[...], 1.0, 0.0).astype(BF16)
    table[nf : 2 * nf, :] = jnp.where(wide == map_u_ref[...], 1.0, 0.0).astype(BF16)
    window_first = (block - 1) * pairs
    row_id = lax.broadcasted_iota(jnp.int32, (pairs, slots), 0)
    slot_id = lax.broadcasted_iota(jnp.int32, (pairs, slots), 1)
    count = jnp.zeros((pairs, slots), jnp.int32)
    for r in range(pairs):
        count = jnp.where(row_id == r, len_ref[r], count)
    target = jnp.where(slot_id < count, right_ref[...] - window_first, -1)
    source = left_ref[...] - window_first
    stride = n_chip * n_packed
    gap = stride - pairs
    source = source + 1 + jnp.where(source >= pairs, gap, 0) + jnp.where(source >= 2 * pairs, gap, 0)
    lanes = lax.broadcasted_iota(jnp.int32, (pairs, nf), 1)
    chosen = jnp.zeros((pairs, nf), jnp.int32)
    for k in range(slots):
        chosen = jnp.where(target[:, k : k + 1] == lanes, source[:, k : k + 1], chosen)
    sel_vec[...] = chosen
    to_scalar = pltpu.make_async_copy(sel_vec, sel, local.at[10])
    to_scalar.start()

    width = nf // n_chip
    tile_lane = lax.broadcasted_iota(jnp.int32, (rows, nf), 1)
    wide_prop = jnp.broadcast_to(prop_ref[...], (rows, nf))
    tiles = regroup([wide_prop] * n_chip)
    prop = tiles[0]
    for c in range(1, n_chip):
        prop = jnp.where(chip == c, tiles[c], prop)

    for half in (0, 1):
        lefts[half, 0] = jnp.zeros(lefts.shape[2:], BF16)
    zones = [
        (tile_lane >= width * z) & (tile_lane < width * (z + 1)) for z in range(n_chip)
    ]

    def fill_lefts(kind, slot, c):
        def one(g, carry):
            tile = (spread[slot, kind, c, g].astype(F32) * prop).astype(BF16)
            turned = [tile] + [pltpu.roll(tile, width * k, 1) for k in range(1, n_chip)]
            for q in range(n_chip):
                at = 1 + slot * stride + g * n_chip + q
                for half in (0, 1):
                    zone = 2 * half + kind
                    rest = jnp.zeros((rows, nf), BF16) if kind == VERTEX else lefts[half, at, c]
                    lefts[half, at, c] = jnp.where(zones[zone], turned[(zone - q) % n_chip], rest)
            return carry

        lax.fori_loop(0, n_packed, one, 0)

    def left_arrives(kind, o):
        c = (chip + o) % n_chip
        for slot in (BEFORE, AFTER):
            arrive(spread.at[slot, kind, c], recv_beside.at[kind, slot, c])
            fill_lefts(kind, slot, c)

    pass_left_on(VERTEX)

    for o in range(1, n_freq):
        f = (freq + o) % n_freq
        arrive(columns.at[f], recv_cols.at[f])
    for g in range(n_groups):
        cols = jnp.concatenate([columns[:, kind, g].reshape(nf, nf) for kind in (0, 1)], axis=0)
        rows_t = lax.dot_general(
            cols, table[...], (((0,), (0,)), ((), ())), preferred_element_type=F32
        ).astype(BF16)
        n = min(group, pairs - g * group)
        start = OWN * pairs + g * group
        right[DERIV, core, start : start + n] = rows_t.reshape(group, rows, nf)[:n]
    pack_left(DERIV)
    push_left(DERIV)
    pass_chunk_on(DERIV, chip)
    push_beside(DERIV)
    push_sibling(DERIV, OWN)

    for slot in (BEFORE, AFTER):
        arrive(own(VERTEX, slot), recv_right.at[VERTEX, core, slot])
        push_sibling(VERTEX, slot)
    for c in range(n_chip):
        fill_lefts(VERTEX, OWN, c)
    for o in (0, 1, 3, 2):
        left_arrives(VERTEX, o)

    pass_left_on(DERIV)
    for c in range(n_chip):
        fill_lefts(DERIV, OWN, c)
    left_arrives(DERIV, 0)
    for slot in (BEFORE, AFTER):
        arrive(own(DERIV, slot), recv_right.at[DERIV, core, slot])
        push_sibling(DERIV, slot)
    for o in (1, 3, 2):
        left_arrives(DERIV, o)
    other = 1 - core
    for slot in (OWN, BEFORE, AFTER):
        for kind in (VERTEX, DERIV):
            arrive(own(kind, slot, other), recv_right.at[kind, other, slot])

    to_scalar.wait()
    size = pairs // PARTS
    tall = n_chip * rows

    def part_copy(part, o):
        c = (chip + o) % n_chip
        return pltpu.make_async_remote_copy(
            src_ref=part_out.at[part, o],
            dst_ref=part_in.at[part, chip],
            send_sem=send_part.at[part, o],
            recv_sem=recv_part.at[part, chip],
            device_id=(2 * c + core, block),
            device_id_type=MESH,
        )

    def one_part(part, carry):
        first_row = part * size
        lhs, rhs = [], []
        for q in range(0, 3 * pairs, 2):
            lhs.append(
                jnp.concatenate(
                    [
                        (
                            lefts[0, sel[first_row + r, q]] + lefts[1, sel[first_row + r, q + 1]]
                        ).reshape(tall, nf)
                        for r in range(size)
                    ],
                    axis=0,
                )
            )
            for p in (q, q + 1):
                rhs += [right[kind, :, p].reshape(2 * rows, nf) for kind in (DERIV, VERTEX)]
        terms = jnp.dot(
            jnp.concatenate(lhs, axis=1),
            jnp.concatenate(rhs, axis=0),
            preferred_element_type=F32,
        )
        sums[...] = terms.reshape(size, n_chip, rows, nf)
        out_ref[pl.ds(first_row, size)] = sums[:, chip]
        for o in (2, 1, 3):
            part_out[part, o] = sums[:, (chip + o) % n_chip].astype(BF16)
            part_copy(part, o).start()
        return carry

    lax.fori_loop(0, PARTS, one_part, 0)
    stores = []
    for part in range(PARTS):
        at = slice(part * size, (part + 1) * size)
        total = out_ref[at]
        for o in (1, 3, 2):
            c = (chip + o) % n_chip
            arrive(part_in.at[part, c], recv_part.at[part, c])
            total = total + part_in[part, c].astype(F32)
        out_ref[at] = total
        stores.append(pltpu.make_async_copy(out_ref.at[at], out.at[at], local.at[part]))
        stores[-1].start()
    for part in range(PARTS):
        for o in (2, 1, 3):
            part_copy(part, o).wait_send()
    for store in stores:
        store.wait()
    for copy in sent:
        copy.wait_send()


def per_device(
    dims,
    vertex,
    deriv_s,
    deriv_u,
    freq_map_s,
    freq_map_u,
    pair_sym,
    propagator,
    left_pairs,
    right_pairs,
    lengths,
):
    n_freq, _ = dims
    n_chip = n_freq // 2
    pairs, rows, nf = vertex.shape
    n_groups = -(-pairs * rows // nf)
    n_packed = -(-pairs // n_chip)
    size = pairs // PARTS
    hbm = pl.BlockSpec(memory_space=pltpu.HBM)
    dma = pltpu.SemaphoreType.DMA
    return pl.pallas_call(
        functools.partial(kernel, dims),
        out_shape=jax.ShapeDtypeStruct((pairs, rows, nf), F32),
        in_specs=[hbm] * 10,
        out_specs=hbm,
        scratch_shapes=[
            pltpu.VMEM((pairs, rows, nf), BF16),
            pltpu.VMEM((pairs, rows, nf), BF16),
            pltpu.VMEM((1, nf), jnp.int32),
            pltpu.VMEM((1, nf), jnp.int32),
            pltpu.VMEM((1, nf), F32),
            pltpu.VMEM(left_pairs.shape, jnp.int32),
            pltpu.VMEM(right_pairs.shape, jnp.int32),
            pltpu.SMEM(pair_sym.shape, jnp.int32),
            pltpu.SMEM(lengths.shape, jnp.int32),
            pltpu.VMEM((pairs, rows, nf), F32),
            pltpu.VMEM((2, 2, 3 * pairs, rows, nf), BF16),
            pltpu.VMEM((2, n_chip, n_packed, rows, nf), BF16),
            pltpu.VMEM((3, 2, n_chip, n_packed, rows, nf), BF16),
            pltpu.VMEM((2, 1 + 3 * n_packed * n_chip, n_chip, rows, nf), BF16),
            pltpu.VMEM((n_freq, 2, n_groups, rows, nf), BF16),
            pltpu.VMEM((n_freq, 2, n_groups, rows, nf), BF16),
            pltpu.VMEM((2 * nf, nf), BF16),
            pltpu.VMEM((size, n_chip, rows, nf), F32),
            pltpu.VMEM((PARTS, n_chip, size, rows, nf), BF16),
            pltpu.VMEM((PARTS, n_chip, size, rows, nf), BF16),
            pltpu.VMEM((pairs, nf), jnp.int32),
            pltpu.SMEM((pairs, nf), jnp.int32),
            dma((2, 2, 3)),
            dma((2, n_chip)),
            dma((2, 3, n_chip)),
            dma((n_freq,)),
            dma((PARTS, n_chip)),
            dma((PARTS, n_chip)),
            dma((64,)),
            dma((11,)),
        ],
        compiler_params=pltpu.CompilerParams(
            collective_id=0, has_side_effects=True, vmem_limit_bytes=63 * 1024 * 1024
        ),
    )(
        vertex,
        jnp.swapaxes(deriv_s, 1, 2),
        jnp.swapaxes(deriv_u, 1, 2),
        freq_map_s.reshape(1, nf),
        freq_map_u.reshape(1, nf),
        propagator.reshape(1, nf),
        left_pairs,
        right_pairs,
        pair_sym,
        lengths,
    )


def solution(mesh):
    dims = (mesh.shape["freq"], mesh.shape["pair"])
    return jax.shard_map(
        functools.partial(per_device, dims),
        mesh=mesh,
        in_specs=(
            P("pair", "freq", None),
            P("pair", None, "freq"),
            P("pair", None, "freq"),
            P(),
            P(),
            P("pair"),
            P(),
            P("pair", None),
            P("pair", None),
            P("pair"),
        ),
        out_specs=P("pair", "freq", None),
        check_vma=False,
    )
```

```python
import functools

import jax
import jax.numpy as jnp
from jax import lax
from jax.experimental import pallas as pl
from jax.experimental.pallas import tpu as pltpu
from jax.sharding import PartitionSpec as P

MESH = pl.DeviceIdType.MESH
BF16 = jnp.bfloat16
F32 = jnp.float32

BEFORE, OWN, AFTER = 0, 1, 2
VERTEX, DERIV = 0, 1
PARTS = 6


def regroup(parts):
    count = len(parts)
    rows, lanes = parts[0].shape
    width = lanes // count
    lane = lax.broadcasted_iota(jnp.int32, (rows, lanes), 1)
    parts = list(parts)
    step = 1
    while step < count:
        high = (lane & (width * step)) != 0
        for q in range(count):
            if (q // step) % 2 == 0:
                a, b = parts[q], parts[q + step]
                parts[q] = jnp.where(high, pltpu.roll(b, width * step, 1), a)
                parts[q + step] = jnp.where(high, b, pltpu.roll(a, lanes - width * step, 1))
        step *= 2
    return parts


def kernel(
    dims,
    v_in,
    s_in,
    u_in,
    map_s_in,
    map_u_in,
    prop_in,
    left_in,
    right_in,
    sym_in,
    len_in,
    out,
    s_ref,
    u_ref,
    map_s_ref,
    map_u_ref,
    prop_ref,
    left_ref,
    right_ref,
    sym_ref,
    len_ref,
    out_ref,
    right,
    packed,
    spread,
    lefts,
    chunks,
    columns,
    table,
    sums,
    part_out,
    part_in,
    sel_vec,
    sel,
    recv_right,
    recv_spread,
    recv_beside,
    recv_cols,
    recv_part,
    send_part,
    send,
    local,
):
    n_freq, n_pair = dims
    n_chip = n_freq // 2
    pairs, rows, nf = v_in.shape
    slots = left_ref.shape[1]
    freq, block = lax.axis_index("freq"), lax.axis_index("pair")
    chip, core = freq // 2, freq % 2

    sibling = (freq + 1 - 2 * core, block)
    x_up = (freq, (block + 1) % n_pair)
    x_down = (freq, (block + n_pair - 1) % n_pair)

    def own(kind, slot=OWN, of=core):
        return right.at[kind, of, slot * pairs : (slot + 1) * pairs]

    barrier = pltpu.get_barrier_semaphore()
    peers = [((freq + o) % n_freq, block) for o in range(1, n_freq)] + [x_up, x_down]
    for peer in peers:
        pl.semaphore_signal(barrier, inc=1, device_id=peer, device_id_type=MESH)
    loads = [
        pltpu.make_async_copy(src, dst, local.at[i])
        for i, (src, dst) in enumerate(
            (
                (v_in, own(VERTEX)),
                (sym_in, sym_ref),
                (s_in, s_ref),
                (u_in, u_ref),
                (map_s_in, map_s_ref),
                (map_u_in, map_u_ref),
                (prop_in, prop_ref),
                (left_in, left_ref),
                (right_in, right_ref),
                (len_in, len_ref),
            )
        )
    ]
    for load in loads:
        load.start()

    sent = []

    def push(src, dst, recv_sem, peer):
        copy = pltpu.make_async_remote_copy(
            src_ref=src,
            dst_ref=dst,
            send_sem=send.at[len(sent)],
            recv_sem=recv_sem,
            device_id=peer,
            device_id_type=MESH,
        )
        copy.start()
        sent.append(copy)

    def arrive(ref, recv_sem):
        pltpu.make_async_remote_copy(
            src_ref=ref,
            dst_ref=ref,
            send_sem=send.at[0],
            recv_sem=recv_sem,
            device_id=sibling,
            device_id_type=MESH,
        ).wait_recv()

    def push_beside(kind):
        push(own(kind), own(kind, BEFORE), recv_right.at[kind, core, BEFORE], x_up)
        push(own(kind), own(kind, AFTER), recv_right.at[kind, core, AFTER], x_down)

    def push_sibling(kind, slot):
        push(own(kind, slot), own(kind, slot), recv_right.at[kind, core, slot], sibling)

    n_packed = packed.shape[2]
    zero_rows = jnp.zeros((rows, nf), BF16)

    def pack_left(kind):
        for g in range(n_packed):
            four = [
                right[kind, core, OWN * pairs + p] if p < pairs else zero_rows
                for p in range(n_chip * g, n_chip * (g + 1))
            ]
            for c, tile in enumerate(regroup(four)):
                packed[kind, c, g] = tile
        spread[OWN, kind, chip] = packed[kind, chip]

    def push_left(kind):
        for o in (2, 1, 3):
            c = (chip + o) % n_chip
            push(
                packed.at[kind, c],
                spread.at[OWN, kind, chip],
                recv_spread.at[kind, chip],
                (2 * c + core, block),
            )

    def pass_chunk_on(kind, c):
        at = spread.at[OWN, kind, c]
        push(at, spread.at[BEFORE, kind, c], recv_beside.at[kind, BEFORE, c], x_up)
        push(at, spread.at[AFTER, kind, c], recv_beside.at[kind, AFTER, c], x_down)

    def pass_left_on(kind):
        for o in (1, 3, 2):
            c = (chip + o) % n_chip
            arrive(spread.at[OWN, kind, c], recv_spread.at[kind, c])
            pass_chunk_on(kind, c)

    def left_arrives(kind, slot):
        for o in (0, 1, 3, 2):
            c = (chip + o) % n_chip
            arrive(spread.at[slot, kind, c], recv_beside.at[kind, slot, c])

    loads[0].wait()
    pack_left(VERTEX)
    for load in loads[1:4]:
        load.wait()
    group = nf // rows
    n_groups = columns.shape[2]
    for kind in (0, 1):
        for g in range(n_groups):
            eight = []
            for p in range(g * group, (g + 1) * group):
                if p >= pairs:
                    eight.append(zero_rows)
                elif kind == 0:
                    eight.append(s_ref[p])
                else:
                    eight.append(u_ref[lax.rem(sym_ref[p], pairs)])
            for f, tile in enumerate(regroup(eight)):
                chunks[f, kind, g] = tile
    columns[freq] = chunks[freq]

    pl.semaphore_wait(barrier, len(peers))
    push_left(VERTEX)
    push_beside(VERTEX)
    pass_chunk_on(VERTEX, chip)
    for o in (4, 3, 5, 2, 6, 1, 7):
        f = (freq + o) % n_freq
        push(chunks.at[f], columns.at[freq], recv_cols.at[freq], (f, block))
    push_sibling(VERTEX, OWN)

    for load in loads[4:]:
        load.wait()
    wide = lax.broadcasted_iota(jnp.int32, (nf, nf), 0)
    table[0:nf, :] = jnp.where(wide == map_s_ref[...], 1.0, 0.0).astype(BF16)
    table[nf : 2 * nf, :] = jnp.where(wide == map_u_ref[...], 1.0, 0.0).astype(BF16)
    window_first = (block - 1) * pairs
    row_id = lax.broadcasted_iota(jnp.int32, (pairs, slots), 0)
    slot_id = lax.broadcasted_iota(jnp.int32, (pairs, slots), 1)
    count = jnp.zeros((pairs, slots), jnp.int32)
    for r in range(pairs):
        count = jnp.where(row_id == r, len_ref[r], count)
    target = jnp.where(slot_id < count, right_ref[...] - window_first, -1)
    source = left_ref[...] - window_first
    stride = n_chip * n_packed
    gap = stride - pairs
    source = source + 1 + jnp.where(source >= pairs, gap, 0) + jnp.where(source >= 2 * pairs, gap, 0)
    lanes = lax.broadcasted_iota(jnp.int32, (pairs, nf), 1)
    chosen = jnp.zeros((pairs, nf), jnp.int32)
    for k in range(slots):
        chosen = jnp.where(target[:, k : k + 1] == lanes, source[:, k : k + 1], chosen)
    sel_vec[...] = chosen
    to_scalar = pltpu.make_async_copy(sel_vec, sel, local.at[10])
    to_scalar.start()

    width = nf // n_chip
    tile_lane = lax.broadcasted_iota(jnp.int32, (rows, nf), 1)
    wide_prop = jnp.broadcast_to(prop_ref[...], (rows, nf))
    tiles = regroup([wide_prop] * n_chip)
    prop = tiles[0]
    for c in range(1, n_chip):
        prop = jnp.where(chip == c, tiles[c], prop)

    for half in (0, 1):
        lefts[half, 0] = jnp.zeros(lefts.shape[2:], BF16)
    zones = [
        (tile_lane >= width * z) & (tile_lane < width * (z + 1)) for z in range(n_chip)
    ]

    def fill_lefts(kind, slot):
        for g in range(n_packed):
            for c in range(n_chip):
                tile = (spread[slot, kind, c, g].astype(F32) * prop).astype(BF16)
                turned = [tile] + [pltpu.roll(tile, width * k, 1) for k in range(1, n_chip)]
                for q in range(n_chip):
                    at = 1 + slot * stride + g * n_chip + q
                    for half in (0, 1):
                        zone = 2 * half + kind
                        rest = zero_rows if kind == VERTEX else lefts[half, at, c]
                        lefts[half, at, c] = jnp.where(zones[zone], turned[(zone - q) % n_chip], rest)

    pass_left_on(VERTEX)

    for o in range(1, n_freq):
        f = (freq + o) % n_freq
        arrive(columns.at[f], recv_cols.at[f])
    for g in range(n_groups):
        cols = jnp.concatenate([columns[:, kind, g].reshape(nf, nf) for kind in (0, 1)], axis=0)
        rows_t = lax.dot_general(
            cols, table[...], (((0,), (0,)), ((), ())), preferred_element_type=F32
        ).astype(BF16)
        n = min(group, pairs - g * group)
        start = OWN * pairs + g * group
        right[DERIV, core, start : start + n] = rows_t.reshape(group, rows, nf)[:n]
    pack_left(DERIV)
    push_left(DERIV)
    pass_chunk_on(DERIV, chip)
    push_beside(DERIV)
    push_sibling(DERIV, OWN)

    for slot in (BEFORE, AFTER):
        arrive(own(VERTEX, slot), recv_right.at[VERTEX, core, slot])
        push_sibling(VERTEX, slot)
    fill_lefts(VERTEX, OWN)
    for slot in (BEFORE, AFTER):
        left_arrives(VERTEX, slot)
        fill_lefts(VERTEX, slot)

    pass_left_on(DERIV)
    fill_lefts(DERIV, OWN)
    for slot in (BEFORE, AFTER):
        arrive(own(DERIV, slot), recv_right.at[DERIV, core, slot])
        push_sibling(DERIV, slot)
    for slot in (BEFORE, AFTER):
        left_arrives(DERIV, slot)
        fill_lefts(DERIV, slot)
    other = 1 - core
    for slot in (OWN, BEFORE, AFTER):
        for kind in (VERTEX, DERIV):
            arrive(own(kind, slot, other), recv_right.at[kind, other, slot])

    to_scalar.wait()
    size = pairs // PARTS
    tall = n_chip * rows

    def part_copy(part, o):
        c = (chip + o) % n_chip
        return pltpu.make_async_remote_copy(
            src_ref=part_out.at[part, o],
            dst_ref=part_in.at[part, chip],
            send_sem=send_part.at[part, o],
            recv_sem=recv_part.at[part, chip],
            device_id=(2 * c + core, block),
            device_id_type=MESH,
        )

    def one_part(part, carry):
        first_row = part * size
        lhs, rhs = [], []
        for q in range(0, 3 * pairs, 2):
            lhs.append(
                jnp.concatenate(
                    [
                        (
                            lefts[0, sel[first_row + r, q]] + lefts[1, sel[first_row + r, q + 1]]
                        ).reshape(tall, nf)
                        for r in range(size)
                    ],
                    axis=0,
                )
            )
            for p in (q, q + 1):
                rhs += [right[kind, :, p].reshape(2 * rows, nf) for kind in (DERIV, VERTEX)]
        terms = jnp.dot(
            jnp.concatenate(lhs, axis=1),
            jnp.concatenate(rhs, axis=0),
            preferred_element_type=F32,
        )
        sums[...] = terms.reshape(size, n_chip, rows, nf)
        out_ref[pl.ds(first_row, size)] = sums[:, chip]
        for o in (2, 1, 3):
            part_out[part, o] = sums[:, (chip + o) % n_chip].astype(BF16)
            part_copy(part, o).start()
        return carry

    lax.fori_loop(0, PARTS, one_part, 0)
    stores = []
    for part in range(PARTS):
        at = slice(part * size, (part + 1) * size)
        total = out_ref[at]
        for o in (1, 3, 2):
            c = (chip + o) % n_chip
            arrive(part_in.at[part, c], recv_part.at[part, c])
            total = total + part_in[part, c].astype(F32)
        out_ref[at] = total
        stores.append(pltpu.make_async_copy(out_ref.at[at], out.at[at], local.at[part]))
        stores[-1].start()
    for part in range(PARTS):
        for o in (2, 1, 3):
            part_copy(part, o).wait_send()
    for store in stores:
        store.wait()
    for copy in sent:
        copy.wait_send()


def per_device(
    dims,
    vertex,
    deriv_s,
    deriv_u,
    freq_map_s,
    freq_map_u,
    pair_sym,
    propagator,
    left_pairs,
    right_pairs,
    lengths,
):
    n_freq, _ = dims
    n_chip = n_freq // 2
    pairs, rows, nf = vertex.shape
    n_groups = -(-pairs * rows // nf)
    n_packed = -(-pairs // n_chip)
    size = pairs // PARTS
    hbm = pl.BlockSpec(memory_space=pltpu.HBM)
    dma = pltpu.SemaphoreType.DMA
    return pl.pallas_call(
        functools.partial(kernel, dims),
        out_shape=jax.ShapeDtypeStruct((pairs, rows, nf), F32),
        in_specs=[hbm] * 10,
        out_specs=hbm,
        scratch_shapes=[
            pltpu.VMEM((pairs, rows, nf), BF16),
            pltpu.VMEM((pairs, rows, nf), BF16),
            pltpu.VMEM((1, nf), jnp.int32),
            pltpu.VMEM((1, nf), jnp.int32),
            pltpu.VMEM((1, nf), F32),
            pltpu.VMEM(left_pairs.shape, jnp.int32),
            pltpu.VMEM(right_pairs.shape, jnp.int32),
            pltpu.SMEM(pair_sym.shape, jnp.int32),
            pltpu.SMEM(lengths.shape, jnp.int32),
            pltpu.VMEM((pairs, rows, nf), F32),
            pltpu.VMEM((2, 2, 3 * pairs, rows, nf), BF16),
            pltpu.VMEM((2, n_chip, n_packed, rows, nf), BF16),
            pltpu.VMEM((3, 2, n_chip, n_packed, rows, nf), BF16),
            pltpu.VMEM((2, 1 + 3 * n_packed * n_chip, n_chip, rows, nf), BF16),
            pltpu.VMEM((n_freq, 2, n_groups, rows, nf), BF16),
            pltpu.VMEM((n_freq, 2, n_groups, rows, nf), BF16),
            pltpu.VMEM((2 * nf, nf), BF16),
            pltpu.VMEM((size, n_chip, rows, nf), F32),
            pltpu.VMEM((PARTS, n_chip, size, rows, nf), BF16),
            pltpu.VMEM((PARTS, n_chip, size, rows, nf), BF16),
            pltpu.VMEM((pairs, nf), jnp.int32),
            pltpu.SMEM((pairs, nf), jnp.int32),
            dma((2, 2, 3)),
            dma((2, n_chip)),
            dma((2, 3, n_chip)),
            dma((n_freq,)),
            dma((PARTS, n_chip)),
            dma((PARTS, n_chip)),
            dma((64,)),
            dma((11,)),
        ],
        compiler_params=pltpu.CompilerParams(
            collective_id=0, has_side_effects=True, vmem_limit_bytes=63 * 1024 * 1024
        ),
    )(
        vertex,
        jnp.swapaxes(deriv_s, 1, 2),
        jnp.swapaxes(deriv_u, 1, 2),
        freq_map_s.reshape(1, nf),
        freq_map_u.reshape(1, nf),
        propagator.reshape(1, nf),
        left_pairs,
        right_pairs,
        pair_sym,
        lengths,
    )


def solution(mesh):
    dims = (mesh.shape["freq"], mesh.shape["pair"])
    return jax.shard_map(
        functools.partial(per_device, dims),
        mesh=mesh,
        in_specs=(
            P("pair", "freq", None),
            P("pair", None, "freq"),
            P("pair", None, "freq"),
            P(),
            P(),
            P("pair"),
            P(),
            P("pair", None),
            P("pair", None),
            P("pair"),
        ),
        out_specs=P("pair", "freq", None),
        check_vma=False,
    )
```

```python
import functools

import jax
import jax.numpy as jnp
from jax import lax
from jax.experimental import pallas as pl
from jax.experimental.pallas import tpu as pltpu
from jax.sharding import PartitionSpec as P

MESH = pl.DeviceIdType.MESH
BF16 = jnp.bfloat16
F32 = jnp.float32

BEFORE, OWN, AFTER = 0, 1, 2
VERTEX, DERIV = 0, 1
PARTS = 6


def regroup(parts):
    count = len(parts)
    rows, lanes = parts[0].shape
    width = lanes // count
    lane = lax.broadcasted_iota(jnp.int32, (rows, lanes), 1)
    parts = list(parts)
    step = 1
    while step < count:
        high = (lane & (width * step)) != 0
        for q in range(count):
            if (q // step) % 2 == 0:
                a, b = parts[q], parts[q + step]
                parts[q] = jnp.where(high, pltpu.roll(b, width * step, 1), a)
                parts[q + step] = jnp.where(high, b, pltpu.roll(a, lanes - width * step, 1))
        step *= 2
    return parts


def kernel(
    dims,
    v_in,
    s_in,
    u_in,
    map_s_in,
    map_u_in,
    prop_in,
    left_in,
    right_in,
    sym_in,
    len_in,
    out,
    s_ref,
    u_ref,
    map_s_ref,
    map_u_ref,
    prop_ref,
    left_ref,
    right_ref,
    sym_ref,
    len_ref,
    out_ref,
    right,
    packed,
    spread,
    lefts,
    chunks,
    columns,
    table,
    sums,
    part_out,
    part_in,
    sel_vec,
    sel,
    recv_right,
    recv_spread,
    recv_beside,
    recv_cols,
    recv_part,
    send_part,
    send,
    local,
):
    n_freq, n_pair = dims
    n_chip = n_freq // 2
    pairs, rows, nf = v_in.shape
    slots = left_ref.shape[1]
    freq, block = lax.axis_index("freq"), lax.axis_index("pair")
    chip, core = freq // 2, freq % 2

    sibling = (freq + 1 - 2 * core, block)
    x_up = (freq, (block + 1) % n_pair)
    x_down = (freq, (block + n_pair - 1) % n_pair)

    def own(kind, slot=OWN, of=core):
        return right.at[kind, of, slot * pairs : (slot + 1) * pairs]

    barrier = pltpu.get_barrier_semaphore()
    peers = [((freq + o) % n_freq, block) for o in range(1, n_freq)] + [x_up, x_down]
    for peer in peers:
        pl.semaphore_signal(barrier, inc=1, device_id=peer, device_id_type=MESH)
    loads = [
        pltpu.make_async_copy(src, dst, local.at[i])
        for i, (src, dst) in enumerate(
            (
                (v_in, own(VERTEX)),
                (sym_in, sym_ref),
                (s_in, s_ref),
                (u_in, u_ref),
                (map_s_in, map_s_ref),
                (map_u_in, map_u_ref),
                (prop_in, prop_ref),
                (left_in, left_ref),
                (right_in, right_ref),
                (len_in, len_ref),
            )
        )
    ]
    for load in loads:
        load.start()

    sent = []

    def push(src, dst, recv_sem, peer):
        copy = pltpu.make_async_remote_copy(
            src_ref=src,
            dst_ref=dst,
            send_sem=send.at[len(sent)],
            recv_sem=recv_sem,
            device_id=peer,
            device_id_type=MESH,
        )
        copy.start()
        sent.append(copy)

    def arrive(ref, recv_sem):
        pltpu.make_async_remote_copy(
            src_ref=ref,
            dst_ref=ref,
            send_sem=send.at[0],
            recv_sem=recv_sem,
            device_id=sibling,
            device_id_type=MESH,
        ).wait_recv()

    def push_beside(kind):
        push(own(kind), own(kind, BEFORE), recv_right.at[kind, core, BEFORE], x_up)
        push(own(kind), own(kind, AFTER), recv_right.at[kind, core, AFTER], x_down)

    def push_sibling(kind, slot):
        push(own(kind, slot), own(kind, slot), recv_right.at[kind, core, slot], sibling)

    n_packed = packed.shape[2]
    zero_rows = jnp.zeros((rows, nf), BF16)

    def pack_left(kind):
        for g in range(n_packed):
            four = [
                right[kind, core, OWN * pairs + p] if p < pairs else zero_rows
                for p in range(n_chip * g, n_chip * (g + 1))
            ]
            for c, tile in enumerate(regroup(four)):
                packed[kind, c, g] = tile
        spread[OWN, kind, chip] = packed[kind, chip]

    def push_left(kind):
        for o in (2, 1, 3):
            c = (chip + o) % n_chip
            push(
                packed.at[kind, c],
                spread.at[OWN, kind, chip],
                recv_spread.at[kind, chip],
                (2 * c + core, block),
            )

    def pass_chunk_on(kind, c):
        at = spread.at[OWN, kind, c]
        push(at, spread.at[BEFORE, kind, c], recv_beside.at[kind, BEFORE, c], x_up)
        push(at, spread.at[AFTER, kind, c], recv_beside.at[kind, AFTER, c], x_down)

    def pass_left_on(kind):
        for o in (1, 3, 2):
            c = (chip + o) % n_chip
            arrive(spread.at[OWN, kind, c], recv_spread.at[kind, c])
            pass_chunk_on(kind, c)

    def left_arrives(kind, slot):
        for o in (0, 1, 3, 2):
            c = (chip + o) % n_chip
            arrive(spread.at[slot, kind, c], recv_beside.at[kind, slot, c])

    loads[0].wait()
    pack_left(VERTEX)
    for load in loads[1:4]:
        load.wait()
    group = nf // rows
    n_groups = columns.shape[2]
    for kind in (0, 1):
        for g in range(n_groups):
            eight = []
            for p in range(g * group, (g + 1) * group):
                if p >= pairs:
                    eight.append(zero_rows)
                elif kind == 0:
                    eight.append(s_ref[p])
                else:
                    eight.append(u_ref[lax.rem(sym_ref[p], pairs)])
            for f, tile in enumerate(regroup(eight)):
                chunks[f, kind, g] = tile
    columns[freq] = chunks[freq]

    pl.semaphore_wait(barrier, len(peers))
    push_left(VERTEX)
    push_beside(VERTEX)
    pass_chunk_on(VERTEX, chip)
    for o in (4, 3, 5, 2, 6, 1, 7):
        f = (freq + o) % n_freq
        push(chunks.at[f], columns.at[freq], recv_cols.at[freq], (f, block))
    push_sibling(VERTEX, OWN)

    for load in loads[4:]:
        load.wait()
    wide = lax.broadcasted_iota(jnp.int32, (nf, nf), 0)
    table[0:nf, :] = jnp.where(wide == map_s_ref[...], 1.0, 0.0).astype(BF16)
    table[nf : 2 * nf, :] = jnp.where(wide == map_u_ref[...], 1.0, 0.0).astype(BF16)
    window_first = (block - 1) * pairs
    row_id = lax.broadcasted_iota(jnp.int32, (pairs, slots), 0)
    slot_id = lax.broadcasted_iota(jnp.int32, (pairs, slots), 1)
    count = jnp.zeros((pairs, slots), jnp.int32)
    for r in range(pairs):
        count = jnp.where(row_id == r, len_ref[r], count)
    target = jnp.where(slot_id < count, right_ref[...] - window_first, -1)
    source = left_ref[...] - window_first
    stride = n_chip * n_packed
    gap = stride - pairs
    source = source + 1 + jnp.where(source >= pairs, gap, 0) + jnp.where(source >= 2 * pairs, gap, 0)
    lanes = lax.broadcasted_iota(jnp.int32, (pairs, nf), 1)
    chosen = jnp.zeros((pairs, nf), jnp.int32)
    for k in range(slots):
        chosen = jnp.where(target[:, k : k + 1] == lanes, source[:, k : k + 1], chosen)
    sel_vec[...] = chosen
    to_scalar = pltpu.make_async_copy(sel_vec, sel, local.at[10])
    to_scalar.start()

    width = nf // n_chip
    tile_lane = lax.broadcasted_iota(jnp.int32, (rows, nf), 1)
    wide_prop = jnp.broadcast_to(prop_ref[...], (rows, nf))
    tiles = regroup([wide_prop] * n_chip)
    prop = tiles[0]
    for c in range(1, n_chip):
        prop = jnp.where(chip == c, tiles[c], prop)

    for half in (0, 1):
        lefts[half, 0] = jnp.zeros(lefts.shape[2:], BF16)
    zones = [
        (tile_lane >= width * z) & (tile_lane < width * (z + 1)) for z in range(n_chip)
    ]

    def fill_lefts(kind, slot, chips=range(n_chip)):
        for g in range(n_packed):
            for c in chips:
                tile = (spread[slot, kind, c, g].astype(F32) * prop).astype(BF16)
                turned = [tile] + [pltpu.roll(tile, width * k, 1) for k in range(1, n_chip)]
                for q in range(n_chip):
                    at = 1 + slot * stride + g * n_chip + q
                    for half in (0, 1):
                        zone = 2 * half + kind
                        rest = zero_rows if kind == VERTEX else lefts[half, at, c]
                        lefts[half, at, c] = jnp.where(zones[zone], turned[(zone - q) % n_chip], rest)

    pass_left_on(VERTEX)

    for o in range(1, n_freq):
        f = (freq + o) % n_freq
        arrive(columns.at[f], recv_cols.at[f])
    for g in range(n_groups):
        cols = jnp.concatenate([columns[:, kind, g].reshape(nf, nf) for kind in (0, 1)], axis=0)
        rows_t = lax.dot_general(
            cols, table[...], (((0,), (0,)), ((), ())), preferred_element_type=F32
        ).astype(BF16)
        n = min(group, pairs - g * group)
        start = OWN * pairs + g * group
        right[DERIV, core, start : start + n] = rows_t.reshape(group, rows, nf)[:n]
    pack_left(DERIV)
    push_left(DERIV)
    pass_chunk_on(DERIV, chip)
    push_beside(DERIV)
    push_sibling(DERIV, OWN)

    for slot in (BEFORE, AFTER):
        arrive(own(VERTEX, slot), recv_right.at[VERTEX, core, slot])
        push_sibling(VERTEX, slot)
    fill_lefts(VERTEX, OWN)
    for slot in (BEFORE, AFTER):
        left_arrives(VERTEX, slot)
        fill_lefts(VERTEX, slot)

    pass_left_on(DERIV)
    fill_lefts(DERIV, OWN)
    for slot in (BEFORE, AFTER):
        arrive(own(DERIV, slot), recv_right.at[DERIV, core, slot])
        push_sibling(DERIV, slot)
    for o in (0, 1, 3, 2):
        c = (chip + o) % n_chip
        for slot in (BEFORE, AFTER):
            arrive(spread.at[slot, DERIV, c], recv_beside.at[DERIV, slot, c])
            fill_lefts(DERIV, slot, (c,))
    other = 1 - core
    for slot in (OWN, BEFORE, AFTER):
        for kind in (VERTEX, DERIV):
            arrive(own(kind, slot, other), recv_right.at[kind, other, slot])

    to_scalar.wait()
    size = pairs // PARTS
    tall = n_chip * rows

    def part_copy(part, o):
        c = (chip + o) % n_chip
        return pltpu.make_async_remote_copy(
            src_ref=part_out.at[part, o],
            dst_ref=part_in.at[part, chip],
            send_sem=send_part.at[part, o],
            recv_sem=recv_part.at[part, chip],
            device_id=(2 * c + core, block),
            device_id_type=MESH,
        )

    def one_part(part, carry):
        first_row = part * size
        lhs, rhs = [], []
        for q in range(0, 3 * pairs, 2):
            lhs.append(
                jnp.concatenate(
                    [
                        (
                            lefts[0, sel[first_row + r, q]] + lefts[1, sel[first_row + r, q + 1]]
                        ).reshape(tall, nf)
                        for r in range(size)
                    ],
                    axis=0,
                )
            )
            for p in (q, q + 1):
                rhs += [right[kind, :, p].reshape(2 * rows, nf) for kind in (DERIV, VERTEX)]
        terms = jnp.dot(
            jnp.concatenate(lhs, axis=1),
            jnp.concatenate(rhs, axis=0),
            preferred_element_type=F32,
        )
        sums[...] = terms.reshape(size, n_chip, rows, nf)
        out_ref[pl.ds(first_row, size)] = sums[:, chip]
        for o in (2, 1, 3):
            part_out[part, o] = sums[:, (chip + o) % n_chip].astype(BF16)
            part_copy(part, o).start()
        return carry

    lax.fori_loop(0, PARTS, one_part, 0)
    stores = []
    for part in range(PARTS):
        at = slice(part * size, (part + 1) * size)
        total = out_ref[at]
        for o in (1, 3, 2):
            c = (chip + o) % n_chip
            arrive(part_in.at[part, c], recv_part.at[part, c])
            total = total + part_in[part, c].astype(F32)
        out_ref[at] = total
        stores.append(pltpu.make_async_copy(out_ref.at[at], out.at[at], local.at[part]))
        stores[-1].start()
    for part in range(PARTS):
        for o in (2, 1, 3):
            part_copy(part, o).wait_send()
    for store in stores:
        store.wait()
    for copy in sent:
        copy.wait_send()


def per_device(
    dims,
    vertex,
    deriv_s,
    deriv_u,
    freq_map_s,
    freq_map_u,
    pair_sym,
    propagator,
    left_pairs,
    right_pairs,
    lengths,
):
    n_freq, _ = dims
    n_chip = n_freq // 2
    pairs, rows, nf = vertex.shape
    n_groups = -(-pairs * rows // nf)
    n_packed = -(-pairs // n_chip)
    size = pairs // PARTS
    hbm = pl.BlockSpec(memory_space=pltpu.HBM)
    dma = pltpu.SemaphoreType.DMA
    return pl.pallas_call(
        functools.partial(kernel, dims),
        out_shape=jax.ShapeDtypeStruct((pairs, rows, nf), F32),
        in_specs=[hbm] * 10,
        out_specs=hbm,
        scratch_shapes=[
            pltpu.VMEM((pairs, rows, nf), BF16),
            pltpu.VMEM((pairs, rows, nf), BF16),
            pltpu.VMEM((1, nf), jnp.int32),
            pltpu.VMEM((1, nf), jnp.int32),
            pltpu.VMEM((1, nf), F32),
            pltpu.VMEM(left_pairs.shape, jnp.int32),
            pltpu.VMEM(right_pairs.shape, jnp.int32),
            pltpu.SMEM(pair_sym.shape, jnp.int32),
            pltpu.SMEM(lengths.shape, jnp.int32),
            pltpu.VMEM((pairs, rows, nf), F32),
            pltpu.VMEM((2, 2, 3 * pairs, rows, nf), BF16),
            pltpu.VMEM((2, n_chip, n_packed, rows, nf), BF16),
            pltpu.VMEM((3, 2, n_chip, n_packed, rows, nf), BF16),
            pltpu.VMEM((2, 1 + 3 * n_packed * n_chip, n_chip, rows, nf), BF16),
            pltpu.VMEM((n_freq, 2, n_groups, rows, nf), BF16),
            pltpu.VMEM((n_freq, 2, n_groups, rows, nf), BF16),
            pltpu.VMEM((2 * nf, nf), BF16),
            pltpu.VMEM((size, n_chip, rows, nf), F32),
            pltpu.VMEM((PARTS, n_chip, size, rows, nf), BF16),
            pltpu.VMEM((PARTS, n_chip, size, rows, nf), BF16),
            pltpu.VMEM((pairs, nf), jnp.int32),
            pltpu.SMEM((pairs, nf), jnp.int32),
            dma((2, 2, 3)),
            dma((2, n_chip)),
            dma((2, 3, n_chip)),
            dma((n_freq,)),
            dma((PARTS, n_chip)),
            dma((PARTS, n_chip)),
            dma((64,)),
            dma((11,)),
        ],
        compiler_params=pltpu.CompilerParams(
            collective_id=0, has_side_effects=True, vmem_limit_bytes=63 * 1024 * 1024
        ),
    )(
        vertex,
        jnp.swapaxes(deriv_s, 1, 2),
        jnp.swapaxes(deriv_u, 1, 2),
        freq_map_s.reshape(1, nf),
        freq_map_u.reshape(1, nf),
        propagator.reshape(1, nf),
        left_pairs,
        right_pairs,
        pair_sym,
        lengths,
    )


def solution(mesh):
    dims = (mesh.shape["freq"], mesh.shape["pair"])
    return jax.shard_map(
        functools.partial(per_device, dims),
        mesh=mesh,
        in_specs=(
            P("pair", "freq", None),
            P("pair", None, "freq"),
            P("pair", None, "freq"),
            P(),
            P(),
            P("pair"),
            P(),
            P("pair", None),
            P("pair", None),
            P("pair"),
        ),
        out_specs=P("pair", "freq", None),
        check_vma=False,
    )
```

```python
import functools

import jax
import jax.numpy as jnp
from jax import lax
from jax.experimental import pallas as pl
from jax.experimental.pallas import tpu as pltpu
from jax.sharding import PartitionSpec as P

MESH = pl.DeviceIdType.MESH
BF16 = jnp.bfloat16
F32 = jnp.float32

BEFORE, OWN, AFTER = 0, 1, 2
VERTEX, DERIV = 0, 1
PARTS = 5


def regroup(parts):
    count = len(parts)
    rows, lanes = parts[0].shape
    width = lanes // count
    lane = lax.broadcasted_iota(jnp.int32, (rows, lanes), 1)
    parts = list(parts)
    step = 1
    while step < count:
        high = (lane & (width * step)) != 0
        for q in range(count):
            if (q // step) % 2 == 0:
                a, b = parts[q], parts[q + step]
                parts[q] = jnp.where(high, pltpu.roll(b, width * step, 1), a)
                parts[q + step] = jnp.where(high, b, pltpu.roll(a, lanes - width * step, 1))
        step *= 2
    return parts


def kernel(
    dims,
    v_in,
    s_in,
    u_in,
    map_s_in,
    map_u_in,
    prop_in,
    left_in,
    right_in,
    sym_in,
    len_in,
    out,
    s_ref,
    u_ref,
    map_s_ref,
    map_u_ref,
    prop_ref,
    left_ref,
    right_ref,
    sym_ref,
    len_ref,
    out_ref,
    right,
    packed,
    spread,
    lefts,
    chunks,
    columns,
    table,
    sums,
    part_out,
    part_in,
    sel_vec,
    sel,
    recv_right,
    recv_spread,
    recv_beside,
    recv_cols,
    recv_part,
    send_part,
    send,
    local,
):
    n_freq, n_pair = dims
    n_chip = n_freq // 2
    pairs, rows, nf = v_in.shape
    slots = left_ref.shape[1]
    freq, block = lax.axis_index("freq"), lax.axis_index("pair")
    chip, core = freq // 2, freq % 2

    sibling = (freq + 1 - 2 * core, block)
    x_up = (freq, (block + 1) % n_pair)
    x_down = (freq, (block + n_pair - 1) % n_pair)

    def own(kind, slot=OWN, of=core):
        return right.at[kind, of, slot * pairs : (slot + 1) * pairs]

    barrier = pltpu.get_barrier_semaphore()
    peers = [((freq + o) % n_freq, block) for o in range(1, n_freq)] + [x_up, x_down]
    for peer in peers:
        pl.semaphore_signal(barrier, inc=1, device_id=peer, device_id_type=MESH)
    loads = [
        pltpu.make_async_copy(src, dst, local.at[i])
        for i, (src, dst) in enumerate(
            (
                (v_in, own(VERTEX)),
                (sym_in, sym_ref),
                (s_in, s_ref),
                (u_in, u_ref),
                (map_s_in, map_s_ref),
                (map_u_in, map_u_ref),
                (prop_in, prop_ref),
                (left_in, left_ref),
                (right_in, right_ref),
                (len_in, len_ref),
            )
        )
    ]
    for load in loads:
        load.start()

    sent = []

    def push(src, dst, recv_sem, peer):
        copy = pltpu.make_async_remote_copy(
            src_ref=src,
            dst_ref=dst,
            send_sem=send.at[len(sent)],
            recv_sem=recv_sem,
            device_id=peer,
            device_id_type=MESH,
        )
        copy.start()
        sent.append(copy)

    def arrive(ref, recv_sem):
        pltpu.make_async_remote_copy(
            src_ref=ref,
            dst_ref=ref,
            send_sem=send.at[0],
            recv_sem=recv_sem,
            device_id=sibling,
            device_id_type=MESH,
        ).wait_recv()

    def push_beside(kind):
        push(own(kind), own(kind, BEFORE), recv_right.at[kind, core, BEFORE], x_up)
        push(own(kind), own(kind, AFTER), recv_right.at[kind, core, AFTER], x_down)

    def push_sibling(kind, slot):
        push(own(kind, slot), own(kind, slot), recv_right.at[kind, core, slot], sibling)

    n_packed = packed.shape[2]
    zero_rows = jnp.zeros((rows, nf), BF16)

    def pack_left(kind):
        for g in range(n_packed):
            four = [
                right[kind, core, OWN * pairs + p] if p < pairs else zero_rows
                for p in range(n_chip * g, n_chip * (g + 1))
            ]
            for c, tile in enumerate(regroup(four)):
                packed[kind, c, g] = tile
        spread[OWN, kind, chip] = packed[kind, chip]

    def push_left(kind):
        for o in (2, 1, 3):
            c = (chip + o) % n_chip
            push(
                packed.at[kind, c],
                spread.at[OWN, kind, chip],
                recv_spread.at[kind, chip],
                (2 * c + core, block),
            )

    def pass_chunk_on(kind, c):
        at = spread.at[OWN, kind, c]
        push(at, spread.at[BEFORE, kind, c], recv_beside.at[kind, BEFORE, c], x_up)
        push(at, spread.at[AFTER, kind, c], recv_beside.at[kind, AFTER, c], x_down)

    def pass_left_on(kind):
        for o in (1, 3, 2):
            c = (chip + o) % n_chip
            arrive(spread.at[OWN, kind, c], recv_spread.at[kind, c])
            pass_chunk_on(kind, c)

    def left_arrives(kind, slot):
        for o in (0, 1, 3, 2):
            c = (chip + o) % n_chip
            arrive(spread.at[slot, kind, c], recv_beside.at[kind, slot, c])

    loads[0].wait()
    pack_left(VERTEX)
    for load in loads[1:4]:
        load.wait()
    group = nf // rows
    n_groups = columns.shape[2]
    for kind in (0, 1):
        for g in range(n_groups):
            eight = []
            for p in range(g * group, (g + 1) * group):
                if p >= pairs:
                    eight.append(zero_rows)
                elif kind == 0:
                    eight.append(s_ref[p])
                else:
                    eight.append(u_ref[lax.rem(sym_ref[p], pairs)])
            for f, tile in enumerate(regroup(eight)):
                chunks[f, kind, g] = tile
    columns[freq] = chunks[freq]

    pl.semaphore_wait(barrier, len(peers))
    push_left(VERTEX)
    push_beside(VERTEX)
    pass_chunk_on(VERTEX, chip)
    for o in (4, 3, 5, 2, 6, 1, 7):
        f = (freq + o) % n_freq
        push(chunks.at[f], columns.at[freq], recv_cols.at[freq], (f, block))
    push_sibling(VERTEX, OWN)

    for load in loads[4:]:
        load.wait()
    wide = lax.broadcasted_iota(jnp.int32, (nf, nf), 0)
    table[0:nf, :] = jnp.where(wide == map_s_ref[...], 1.0, 0.0).astype(BF16)
    table[nf : 2 * nf, :] = jnp.where(wide == map_u_ref[...], 1.0, 0.0).astype(BF16)
    window_first = (block - 1) * pairs
    row_id = lax.broadcasted_iota(jnp.int32, (pairs, slots), 0)
    slot_id = lax.broadcasted_iota(jnp.int32, (pairs, slots), 1)
    count = jnp.zeros((pairs, slots), jnp.int32)
    for r in range(pairs):
        count = jnp.where(row_id == r, len_ref[r], count)
    target = jnp.where(slot_id < count, right_ref[...] - window_first, -1)
    source = left_ref[...] - window_first
    stride = n_chip * n_packed
    gap = stride - pairs
    source = source + 1 + jnp.where(source >= pairs, gap, 0) + jnp.where(source >= 2 * pairs, gap, 0)
    lanes = lax.broadcasted_iota(jnp.int32, (pairs, nf), 1)
    chosen = jnp.zeros((pairs, nf), jnp.int32)
    for k in range(slots):
        chosen = jnp.where(target[:, k : k + 1] == lanes, source[:, k : k + 1], chosen)
    sel_vec[...] = chosen
    to_scalar = pltpu.make_async_copy(sel_vec, sel, local.at[10])
    to_scalar.start()

    width = nf // n_chip
    tile_lane = lax.broadcasted_iota(jnp.int32, (rows, nf), 1)
    wide_prop = jnp.broadcast_to(prop_ref[...], (rows, nf))
    tiles = regroup([wide_prop] * n_chip)
    prop = tiles[0]
    for c in range(1, n_chip):
        prop = jnp.where(chip == c, tiles[c], prop)

    for half in (0, 1):
        lefts[half, 0] = jnp.zeros(lefts.shape[2:], BF16)
    zones = [
        (tile_lane >= width * z) & (tile_lane < width * (z + 1)) for z in range(n_chip)
    ]

    def fill_lefts(kind, slot):
        for g in range(n_packed):
            for c in range(n_chip):
                tile = (spread[slot, kind, c, g].astype(F32) * prop).astype(BF16)
                turned = [tile] + [pltpu.roll(tile, width * k, 1) for k in range(1, n_chip)]
                for q in range(n_chip):
                    at = 1 + slot * stride + g * n_chip + q
                    for half in (0, 1):
                        zone = 2 * half + kind
                        rest = zero_rows if kind == VERTEX else lefts[half, at, c]
                        lefts[half, at, c] = jnp.where(zones[zone], turned[(zone - q) % n_chip], rest)

    pass_left_on(VERTEX)

    for o in range(1, n_freq):
        f = (freq + o) % n_freq
        arrive(columns.at[f], recv_cols.at[f])
    for g in range(n_groups):
        cols = jnp.concatenate([columns[:, kind, g].reshape(nf, nf) for kind in (0, 1)], axis=0)
        rows_t = lax.dot_general(
            cols, table[...], (((0,), (0,)), ((), ())), preferred_element_type=F32
        ).astype(BF16)
        n = min(group, pairs - g * group)
        start = OWN * pairs + g * group
        right[DERIV, core, start : start + n] = rows_t.reshape(group, rows, nf)[:n]
    pack_left(DERIV)
    push_left(DERIV)
    pass_chunk_on(DERIV, chip)
    push_beside(DERIV)
    push_sibling(DERIV, OWN)

    for slot in (BEFORE, AFTER):
        arrive(own(VERTEX, slot), recv_right.at[VERTEX, core, slot])
        push_sibling(VERTEX, slot)
    fill_lefts(VERTEX, OWN)
    for slot in (BEFORE, AFTER):
        left_arrives(VERTEX, slot)
        fill_lefts(VERTEX, slot)

    pass_left_on(DERIV)
    fill_lefts(DERIV, OWN)
    for slot in (BEFORE, AFTER):
        arrive(own(DERIV, slot), recv_right.at[DERIV, core, slot])
        push_sibling(DERIV, slot)
    for slot in (BEFORE, AFTER):
        left_arrives(DERIV, slot)
        fill_lefts(DERIV, slot)
    other = 1 - core
    for slot in (OWN, BEFORE, AFTER):
        for kind in (VERTEX, DERIV):
            arrive(own(kind, slot, other), recv_right.at[kind, other, slot])

    to_scalar.wait()
    size = pairs // PARTS
    tall = n_chip * rows

    def part_copy(part, o):
        c = (chip + o) % n_chip
        return pltpu.make_async_remote_copy(
            src_ref=part_out.at[part, o],
            dst_ref=part_in.at[part, chip],
            send_sem=send_part.at[part, o],
            recv_sem=recv_part.at[part, chip],
            device_id=(2 * c + core, block),
            device_id_type=MESH,
        )

    def one_part(part, carry):
        first_row = part * size
        lhs, rhs = [], []
        for q in range(0, 3 * pairs, 2):
            lhs.append(
                jnp.concatenate(
                    [
                        (
                            lefts[0, sel[first_row + r, q]] + lefts[1, sel[first_row + r, q + 1]]
                        ).reshape(tall, nf)
                        for r in range(size)
                    ],
                    axis=0,
                )
            )
            for p in (q, q + 1):
                rhs += [right[kind, :, p].reshape(2 * rows, nf) for kind in (DERIV, VERTEX)]
        terms = jnp.dot(
            jnp.concatenate(lhs, axis=1),
            jnp.concatenate(rhs, axis=0),
            preferred_element_type=F32,
        )
        sums[...] = terms.reshape(size, n_chip, rows, nf)
        out_ref[pl.ds(first_row, size)] = sums[:, chip]
        for o in (2, 1, 3):
            part_out[part, o] = sums[:, (chip + o) % n_chip].astype(BF16)
            part_copy(part, o).start()
        return carry

    lax.fori_loop(0, PARTS, one_part, 0)
    stores = []
    for part in range(PARTS):
        at = slice(part * size, (part + 1) * size)
        total = out_ref[at]
        for o in (1, 3, 2):
            c = (chip + o) % n_chip
            arrive(part_in.at[part, c], recv_part.at[part, c])
            total = total + part_in[part, c].astype(F32)
        out_ref[at] = total
        stores.append(pltpu.make_async_copy(out_ref.at[at], out.at[at], local.at[part]))
        stores[-1].start()
    for part in range(PARTS):
        for o in (2, 1, 3):
            part_copy(part, o).wait_send()
    for store in stores:
        store.wait()
    for copy in sent:
        copy.wait_send()


def per_device(
    dims,
    vertex,
    deriv_s,
    deriv_u,
    freq_map_s,
    freq_map_u,
    pair_sym,
    propagator,
    left_pairs,
    right_pairs,
    lengths,
):
    n_freq, _ = dims
    n_chip = n_freq // 2
    pairs, rows, nf = vertex.shape
    n_groups = -(-pairs * rows // nf)
    n_packed = -(-pairs // n_chip)
    size = pairs // PARTS
    hbm = pl.BlockSpec(memory_space=pltpu.HBM)
    dma = pltpu.SemaphoreType.DMA
    return pl.pallas_call(
        functools.partial(kernel, dims),
        out_shape=jax.ShapeDtypeStruct((pairs, rows, nf), F32),
        in_specs=[hbm] * 10,
        out_specs=hbm,
        scratch_shapes=[
            pltpu.VMEM((pairs, rows, nf), BF16),
            pltpu.VMEM((pairs, rows, nf), BF16),
            pltpu.VMEM((1, nf), jnp.int32),
            pltpu.VMEM((1, nf), jnp.int32),
            pltpu.VMEM((1, nf), F32),
            pltpu.VMEM(left_pairs.shape, jnp.int32),
            pltpu.VMEM(right_pairs.shape, jnp.int32),
            pltpu.SMEM(pair_sym.shape, jnp.int32),
            pltpu.SMEM(lengths.shape, jnp.int32),
            pltpu.VMEM((pairs, rows, nf), F32),
            pltpu.VMEM((2, 2, 3 * pairs, rows, nf), BF16),
            pltpu.VMEM((2, n_chip, n_packed, rows, nf), BF16),
            pltpu.VMEM((3, 2, n_chip, n_packed, rows, nf), BF16),
            pltpu.VMEM((2, 1 + 3 * n_packed * n_chip, n_chip, rows, nf), BF16),
            pltpu.VMEM((n_freq, 2, n_groups, rows, nf), BF16),
            pltpu.VMEM((n_freq, 2, n_groups, rows, nf), BF16),
            pltpu.VMEM((2 * nf, nf), BF16),
            pltpu.VMEM((size, n_chip, rows, nf), F32),
            pltpu.VMEM((PARTS, n_chip, size, rows, nf), BF16),
            pltpu.VMEM((PARTS, n_chip, size, rows, nf), BF16),
            pltpu.VMEM((pairs, nf), jnp.int32),
            pltpu.SMEM((pairs, nf), jnp.int32),
            dma((2, 2, 3)),
            dma((2, n_chip)),
            dma((2, 3, n_chip)),
            dma((n_freq,)),
            dma((PARTS, n_chip)),
            dma((PARTS, n_chip)),
            dma((64,)),
            dma((11,)),
        ],
        compiler_params=pltpu.CompilerParams(
            collective_id=0, has_side_effects=True, vmem_limit_bytes=63 * 1024 * 1024
        ),
    )(
        vertex,
        jnp.swapaxes(deriv_s, 1, 2),
        jnp.swapaxes(deriv_u, 1, 2),
        freq_map_s.reshape(1, nf),
        freq_map_u.reshape(1, nf),
        propagator.reshape(1, nf),
        left_pairs,
        right_pairs,
        pair_sym,
        lengths,
    )


def solution(mesh):
    dims = (mesh.shape["freq"], mesh.shape["pair"])
    return jax.shard_map(
        functools.partial(per_device, dims),
        mesh=mesh,
        in_specs=(
            P("pair", "freq", None),
            P("pair", None, "freq"),
            P("pair", None, "freq"),
            P(),
            P(),
            P("pair"),
            P(),
            P("pair", None),
            P("pair", None),
            P("pair"),
        ),
        out_specs=P("pair", "freq", None),
        check_vma=False,
    )
```
